32 devices in a mesh: gx: 2 (over x), gy: 4 (over y, core), gz: 4 (over z).
Axes of the slice: x: 2, y: 2, z: 4, core: 2. Of those that a mesh axis runs over, the one named last changes fastest.
Arguments:
- left_core: float32 [256, 512, 256], P(None, ('gx', 'gy', 'gz')), may hold values from -4000 to 4000
- right_core: float32 [256, 512, 256], P(None, ('gx', 'gy', 'gz')), may hold values from -0.00036621094 to 0.00036621094
Outputs:
- left_out: float32 [256, 512, 128], P(None, ('gx', 'gy', 'gz'))
- right_out: float32 [128, 512, 256], P(None, ('gx', 'gy', 'gz'))
- next_factor: float32 [256, 256], replicated
The draws below stay inside these ranges and needn't reach their ends.
All inputs are finite; a program needn't handle non-finite values.
Results may differ from the reference program's by a relative error of at most 0.000075.
Values sent between devices are 32-bit elements; how exact they have to be, the bound alone decides.
No kernel may reach another device: no remote copies, remote signals or barrier semaphores. Data moves between devices by JAX's collectives and lax.ppermute only.
A program may use at most 192 MiB of HBM per device.

```python
import math
import jax
import jax.numpy as jnp
from jax import lax

RL = 256
R = 256
RK = 128
RR = 256
NPTS = 512


def draw_left_core(key, part):
    k_noise, k_cols, k_pts = jax.random.split(key, 3)
    base_noise = jnp.clip(jax.random.normal(k_noise, (RL, NPTS, R), jnp.float32), -6.0, 6.0)
    blended = base_noise + 0.5 * jnp.roll(base_noise, 1, axis=2)
    column_scale = jnp.exp(jax.random.uniform(k_cols, (R,), jnp.float32, 0.0, math.log(10.0)))
    rising = jnp.exp(math.log(3.0) * jnp.arange(NPTS, dtype=jnp.float32) / NPTS)
    point_scale = jnp.exp(jax.random.uniform(k_pts, (NPTS,), jnp.float32, 0.0, math.log(10.0))) * rising
    return blended * column_scale[None, None, :] * point_scale[None, :, None]


def levels(key, dims, shards, low, largest):
    level = 1.0
    for axis_at, parts in shards:
        draws = jax.random.uniform(jax.random.fold_in(jax.random.fold_in(key, 6), axis_at), (parts,), jnp.float32, low / len(shards), largest / len(shards))
        level = level * jnp.repeat(jnp.exp(draws), dims[axis_at] // parts).reshape((-1,) + (1,) * (len(dims) - 1 - axis_at))
    return level


def normal_values(own_key, dims, width, limit, cuts=(), kind=jnp.bfloat16):
    drawn = jax.random.normal(own_key, dims, jnp.float32) * width
    if len(cuts) > 0:
        drawn = levels(own_key, dims, cuts, -0.22, 0.18) * drawn
    return jnp.clip(drawn, min=-limit, max=limit).astype(kind)


def setup_inputs(seed: int = 0) -> dict:
    splits = jax.random.split(jax.random.key(seed), 3)
    return {
        "left_core": draw_left_core(jax.random.fold_in(splits[2], 71), 0),
        "right_core": normal_values(splits[1], (R, NPTS, RR), (RL * NPTS * 2048) ** -0.5, 0.00036621094, ((1, 32),), jnp.float32),
    }


def gram_of(matrix_rows):
    return lax.dot_general(matrix_rows.astype(jnp.float32), matrix_rows.astype(jnp.float32), (((0,), (0,)), ((), ())), precision=lax.Precision.HIGHEST, preferred_element_type=jnp.float32)

def reference(left_core, right_core):
    unfold = left_core.reshape(RL * NPTS, R)
    lower_full = jnp.linalg.cholesky(gram_of(unfold))
    upper = lower_full.T
    ortho_cols = lax.linalg.triangular_solve(lower_full[:RK, :RK], unfold[:, :RK], left_side=False, lower=True, transpose_a=True)
    left_out = (ortho_cols * math.sqrt(RL * NPTS)).reshape(RL, NPTS, RK)
    absorbed = jnp.dot(upper[:RK, :].astype(jnp.float32), right_core.reshape(R, NPTS * RR).astype(jnp.float32), precision=lax.Precision.HIGHEST, preferred_element_type=jnp.float32)
    right_out = absorbed.reshape(RK, NPTS, RR)
    next_gram = gram_of(absorbed.reshape(RK * NPTS, RR)) / (RK * NPTS)
    next_factor = jnp.linalg.cholesky(next_gram).T
    return (left_out, right_out, next_factor)
```

```python
import math

import jax
import jax.numpy as jnp
from jax import lax
from jax.sharding import PartitionSpec as P

RK = 128
AXES = ("gx", "gy", "gz")


def gram_of(lhs_rows, matrix_rows):
    return lax.dot_general(
        lhs_rows,
        matrix_rows,
        (((0,), (0,)), ((), ())),
        precision=lax.Precision.HIGHEST,
        preferred_element_type=jnp.float32,
    )


def sum_by_scatter(part, devices):
    rows, columns = part.shape
    tall = jnp.concatenate([part[:, : columns // 2], part[:, columns // 2 :]], axis=0)
    blocks = tall.reshape(devices, 2 * rows // devices, columns // 2)
    mine = jnp.sum(lax.all_to_all(blocks, AXES, 0, 0), axis=0)
    spread = jnp.broadcast_to(mine[None], blocks.shape)
    tall = lax.all_to_all(spread, AXES, 0, 0).reshape(2 * rows, columns // 2)
    return jnp.concatenate([tall[:rows], tall[rows:]], axis=1)


def exchange(value, axis, bit):
    size = lax.axis_size(axis)
    return lax.ppermute(value, axis, [(i, i ^ bit) for i in range(size)])


def sum_by_butterfly(part):
    rows, columns = part.shape
    odd = lax.axis_index("gy") % 2 == 1
    top, bottom = part[: rows // 2], part[rows // 2 :]
    keep = jnp.where(odd, bottom, top)
    total = keep + exchange(jnp.where(odd, top, bottom), "gy", 1)
    for axis in AXES:
        bit = 2 if axis == "gy" else 1
        while bit < lax.axis_size(axis):
            total = total + exchange(total, axis, bit)
            bit *= 2
    other = exchange(total, "gy", 1)
    return jnp.concatenate(
        [jnp.where(odd, other, total), jnp.where(odd, total, other)], axis=0
    )


def per_device(left_core, right_core):
    rank_left, points_local, rank_mid = left_core.shape
    rank_right = right_core.shape[2]
    devices = lax.axis_size("gx") * lax.axis_size("gy") * lax.axis_size("gz")
    total_points = points_local * devices
    unfold = left_core.reshape(rank_left * points_local, rank_mid)
    gram_top = sum_by_scatter(gram_of(unfold[:, :RK], unfold), devices)
    lower_one = jnp.linalg.cholesky(gram_top[:, :RK])
    upper_rest = lax.linalg.triangular_solve(
        lower_one, gram_top[:, RK:], left_side=True, lower=True
    )
    upper_top = jnp.concatenate([lower_one.T, upper_rest], axis=1)
    absorbed = jnp.dot(
        upper_top,
        right_core.reshape(rank_mid, points_local * rank_right),
        precision=lax.Precision.HIGHEST,
        preferred_element_type=jnp.float32,
    )
    rows = absorbed.reshape(RK * points_local, rank_right)
    summed = sum_by_butterfly(gram_of(rows, rows))
    ortho_cols = lax.linalg.triangular_solve(
        lower_one, unfold[:, :RK], left_side=False, lower=True, transpose_a=True
    )
    left_out = (ortho_cols * math.sqrt(rank_left * total_points)).reshape(
        rank_left, points_local, RK
    )
    factor = jnp.linalg.cholesky(summed / (RK * total_points)).T
    right_out = absorbed.reshape(RK, points_local, rank_right)
    return (left_out, right_out, factor)


def solution(mesh):
    in_specs = (P(None, AXES, None), P(None, AXES, None))
    out_specs = (P(None, AXES, None), P(None, AXES, None), P())
    return jax.shard_map(
        per_device, mesh=mesh, in_specs=in_specs, out_specs=out_specs, check_vma=False
    )
```

```python
import functools
import math

import jax
import jax.numpy as jnp
from jax import lax
from jax.experimental import pallas as pl
from jax.experimental.pallas import tpu as pltpu
from jax.sharding import PartitionSpec as P

RK = 128
AXES = ("gx", "gy", "gz")
LANES = 128
PANEL = 16
SPREAD_ONE = 4
SPREAD_TWO = 2
F32 = jnp.float32
BF16 = jnp.bfloat16
VMEM_LIMIT = 48 * 1024 * 1024


def split(x):
    hi = x.astype(BF16)
    return hi, (x - hi.astype(F32)).astype(BF16)


def dot_tn(a, b):
    return lax.dot_general(a, b, (((0,), (0,)), ((), ())), preferred_element_type=F32)


def dot_nt(a, b):
    return lax.dot_general(a, b, (((1,), (1,)), ((), ())), preferred_element_type=F32)


def dot_nn(a, b):
    return lax.dot_general(a, b, (((1,), (0,)), ((), ())), preferred_element_type=F32)


def stacked_pieces(x):
    one = x.astype(BF16).astype(F32)
    rest = x - one
    two = rest.astype(BF16).astype(F32)
    three = rest - two
    left = jnp.concatenate([one, one, two, two, one, three], axis=0).astype(BF16)
    right = jnp.concatenate([one, two, one, two, three, one], axis=0).astype(BF16)
    return left, right


def factor_rows(w_ref, blocks):
    row_id = lax.broadcasted_iota(jnp.int32, (PANEL, LANES), 0)
    for start in range(0, LANES, PANEL):
        rows = [w_ref[start : start + PANEL, b * LANES : (b + 1) * LANES] for b in range(blocks)]
        columns = [
            jnp.broadcast_to(rows[0][:, start + k : start + k + 1], (PANEL, LANES))
            for k in range(PANEL)
        ]
        scale = jnp.zeros((PANEL, LANES), F32)
        for k in range(PANEL):
            pivot = jnp.broadcast_to(columns[k][k : k + 1, :], (PANEL, LANES))
            inverse = lax.rsqrt(pivot)
            inverse = inverse * (1.5 - 0.5 * pivot * inverse * inverse)
            multiples = columns[k] * inverse
            for m in range(k + 1, PANEL):
                columns[m] = columns[m] - multiples * multiples[m : m + 1, :]
            below = jnp.where(row_id > k, multiples * inverse, 0.0)
            rows = [r - below * r[k : k + 1, :] for r in rows]
            scale = jnp.where(row_id == k, inverse, scale)
        rows = [r * scale for r in rows]
        for b in range(blocks):
            w_ref[start : start + PANEL, b * LANES : (b + 1) * LANES] = rows[b]
        if start + PANEL < LANES:
            both = [stacked_pieces(r) for r in rows]
            left = both[0][0]
            right = jnp.concatenate([b[1] for b in both], axis=1)
            update = dot_tn(left, right)
            w_ref[start + PANEL :, :] = w_ref[start + PANEL :, :] - update[start + PANEL :, :]


def triangle_ids():
    return (
        lax.broadcasted_iota(jnp.int32, (LANES, LANES), 0),
        lax.broadcasted_iota(jnp.int32, (LANES, LANES), 1),
    )


def store_blocks(tall_ref, outs):
    me = lax.rem(lax.axis_index("gy"), len(outs))
    size = outs[0].shape[0]
    for d, out in enumerate(outs):
        out[...] = tall_ref[pl.ds(pl.multiple_of((me ^ d) * size, 8), size), :]


def load_blocks(blocks, tall_ref):
    me = lax.rem(lax.axis_index("gy"), len(blocks))
    size = blocks[0].shape[0]
    for d, block in enumerate(blocks):
        tall_ref[pl.ds(pl.multiple_of((me ^ d) * size, 8), size), :] = block[...]


def gram_kernel(a_ref, *refs):
    outs, tall_ref = refs[:-1], refs[-1]
    step = pl.program_id(0)

    @pl.when(step == 0)
    def _():
        tall_ref[...] = jnp.zeros_like(tall_ref)

    hi, lo = split(a_ref[...])
    both = dot_tn(hi[:, :RK], jnp.concatenate([hi, lo], axis=1))
    top = both[:, :256] + both[:, 256:] + dot_tn(lo[:, :RK], hi)
    tall_ref[:RK, :] += top[:, :RK]
    tall_ref[RK:, :] += top[:, RK:]

    @pl.when(step == pl.num_programs(0) - 1)
    def _():
        store_blocks(tall_ref, outs)


def relay_kernel(points, left_ref, right_ref, hi_ref, lo_ref):
    count = left_ref.shape[0] // points
    for p in range(points):
        for c, half in enumerate((left_ref, right_ref)):
            hi, lo = split(half[pl.ds(p, count, stride=points), :])
            hi_ref[p, :, c * LANES : (c + 1) * LANES] = hi
            lo_ref[p, :, c * LANES : (c + 1) * LANES] = lo


def absorb_kernel(scale, n_in, n_out, *refs):
    blocks = refs[:n_in]
    hi_hbm, lo_hbm = refs[n_in : n_in + 2]
    absorbed_ref, linv_ref = refs[n_in + 2 : n_in + 4]
    outs = refs[n_in + 4 : n_in + 4 + n_out]
    tall_ref, w_ref, hi_ref, lo_ref, pack_ref, sems = refs[n_in + 4 + n_out :]
    copy_hi = pltpu.make_async_copy(hi_hbm, hi_ref, sems.at[0])
    copy_lo = pltpu.make_async_copy(lo_hbm, lo_ref, sems.at[1])
    copy_hi.start()
    copy_lo.start()
    load_blocks(blocks, tall_ref)
    row, col = triangle_ids()
    w_ref[:, :LANES] = tall_ref[:RK, :]
    w_ref[:, LANES : 2 * LANES] = tall_ref[RK:, :]
    w_ref[:, 2 * LANES :] = jnp.where(row == col, 1.0, 0.0).astype(F32)
    factor_rows(w_ref, 3)
    linv_ref[...] = w_ref[:, 2 * LANES :] * scale
    upper = jnp.concatenate(
        [jnp.where(col >= row, w_ref[:, :LANES], 0.0), w_ref[:, LANES : 2 * LANES]], axis=1
    )
    upper_hi, upper_lo = split(upper)
    upper_both = jnp.concatenate([upper_hi, upper_lo], axis=0)
    copy_hi.wait()
    copy_lo.wait()
    points = hi_ref.shape[0]

    def body(p, total):
        high = hi_ref[p]
        first = dot_nn(upper_both, high)
        b = first[:RK, :] + first[RK:, :] + dot_nn(upper_hi, lo_ref[p])
        absorbed_ref[p] = b
        b_hi, b_lo = split(b)
        return total + dot_tn(b_hi, jnp.concatenate([b_hi, b_lo], axis=1))

    total = lax.fori_loop(0, points, body, jnp.zeros((256, 512), F32), unroll=2)
    cross = total[:, 256:]
    gram = total[:, :256] + cross + cross.T
    lower_right = gram[LANES:, LANES:]
    pack_ref[:LANES, :] = jnp.where(col >= row, gram[:LANES, :LANES], lower_right)
    pack_ref[LANES : 2 * LANES, :] = gram[:LANES, LANES:]
    diagonal = jnp.sum(jnp.where(row == col, lower_right, 0.0), axis=0, keepdims=True)
    tail = pack_ref.shape[0] - 2 * LANES
    pack_ref[2 * LANES :, :] = jnp.broadcast_to(diagonal, (tail, LANES))
    store_blocks(pack_ref, outs)


def outputs_kernel(points, a_ref, linv_ref, absorbed_ref, left_ref, right_ref):
    l_hi, l_lo = split(linv_ref[...])
    hi, lo = split(a_ref[...])
    left_ref[...] = dot_nt(hi, l_hi) + dot_nt(hi, l_lo) + dot_nt(lo, l_hi)
    count = absorbed_ref.shape[1]
    for p in range(points):
        right_ref[pl.ds(p, count, stride=points), :] = absorbed_ref[p]


def factor_kernel(scale, n_in, *refs):
    blocks, out_ref = refs[:n_in], refs[n_in]
    pack_ref, w_ref, rest_ref = refs[n_in + 1 :]
    load_blocks(blocks, pack_ref)
    row, col = triangle_ids()
    packed = pack_ref[:LANES, :] * scale
    turned = packed.T
    diagonal = jnp.broadcast_to(pack_ref[2 * LANES : 2 * LANES + 1, :], (LANES, LANES)) * scale
    w_ref[:, :LANES] = jnp.where(col >= row, packed, turned)
    w_ref[:, LANES:] = pack_ref[LANES : 2 * LANES, :] * scale
    rest_ref[...] = jnp.where(row > col, packed, jnp.where(row == col, diagonal, turned))
    factor_rows(w_ref, 2)
    out_ref[:LANES, :LANES] = jnp.where(col >= row, w_ref[:, :LANES], 0.0)
    out_ref[:LANES, LANES:] = w_ref[:, LANES:]
    left, right = stacked_pieces(w_ref[:, LANES:])
    rest_ref[...] = rest_ref[...] - dot_tn(left, right)
    factor_rows(rest_ref, 1)
    out_ref[LANES:, :LANES] = jnp.zeros((LANES, LANES), F32)
    out_ref[LANES:, LANES:] = jnp.where(col >= row, rest_ref[...], 0.0)


def exchange(value, axis, bit):
    size = lax.axis_size(axis)
    return lax.ppermute(value, axis, [(i, i ^ bit) for i in range(size)])


def sum_over_devices(blocks):
    n = len(blocks)
    total = blocks[0]
    for d in range(1, n):
        total = total + exchange(blocks[d], "gy", d)
    for axis in AXES:
        bit = n if axis == "gy" else 1
        while bit < lax.axis_size(axis):
            total = total + exchange(total, axis, bit)
            bit *= 2
    return [total] + [exchange(total, "gy", d) for d in range(1, n)]


def shape(*dims, dtype=F32):
    return jax.ShapeDtypeStruct(dims, dtype)


def params(semantics=None):
    return pltpu.CompilerParams(dimension_semantics=semantics, vmem_limit_bytes=VMEM_LIMIT)


def per_device(left_core, right_core):
    rank_left, points, rank_mid = left_core.shape
    rank_right = right_core.shape[2]
    devices = lax.axis_size("gx") * lax.axis_size("gy") * lax.axis_size("gz")
    total_points = points * devices
    unfold = left_core.reshape(rank_left * points, rank_mid)
    rows_right = right_core.reshape(rank_mid * points, rank_right)
    vmem = pl.BlockSpec(memory_space=pltpu.VMEM)
    anywhere = pl.BlockSpec(memory_space=pl.ANY)

    steps = 8
    chunk = unfold.shape[0] // steps
    size_one = 2 * RK // SPREAD_ONE
    blocks = pl.pallas_call(
        gram_kernel,
        grid=(steps,),
        in_specs=[pl.BlockSpec((chunk, rank_mid), lambda i: (i, 0))],
        out_specs=[pl.BlockSpec((size_one, LANES), lambda i: (0, 0))] * SPREAD_ONE,
        out_shape=[shape(size_one, LANES)] * SPREAD_ONE,
        scratch_shapes=[pltpu.VMEM((2 * RK, LANES), F32)],
        compiler_params=params(("arbitrary",)),
        name="gram_top",
    )(unfold)
    summed = sum_over_devices(blocks)

    ranks = rank_mid // steps
    right_hi, right_lo = pl.pallas_call(
        functools.partial(relay_kernel, points),
        grid=(steps,),
        in_specs=[
            pl.BlockSpec((ranks * points, LANES), lambda i: (i, 0)),
            pl.BlockSpec((ranks * points, LANES), lambda i: (i, 1)),
        ],
        out_specs=[pl.BlockSpec((points, ranks, rank_right), lambda i: (0, i, 0))] * 2,
        out_shape=[shape(points, rank_mid, rank_right, dtype=BF16)] * 2,
        compiler_params=params(("arbitrary",)),
        cost_estimate=pl.CostEstimate(flops=0, bytes_accessed=24 * 2**20, transcendentals=0),
        name="relay_right",
    )(rows_right, rows_right)

    packed_rows = 2 * LANES + 8 * SPREAD_TWO
    size_two = packed_rows // SPREAD_TWO
    absorbed, linv, *blocks = pl.pallas_call(
        functools.partial(
            absorb_kernel, math.sqrt(rank_left * total_points), SPREAD_ONE, SPREAD_TWO
        ),
        in_specs=[vmem] * SPREAD_ONE + [anywhere] * 2,
        out_specs=[vmem] * (2 + SPREAD_TWO),
        out_shape=[shape(points, RK, rank_right), shape(RK, RK)]
        + [shape(size_two, LANES)] * SPREAD_TWO,
        scratch_shapes=[
            pltpu.VMEM((2 * RK, LANES), F32),
            pltpu.VMEM((LANES, 3 * LANES), F32),
            pltpu.VMEM((points, rank_mid, rank_right), BF16),
            pltpu.VMEM((points, rank_mid, rank_right), BF16),
            pltpu.VMEM((packed_rows, LANES), F32),
            pltpu.SemaphoreType.DMA((2,)),
        ],
        compiler_params=params(),
        name="factor_absorb",
    )(*summed, right_hi, right_lo)
    summed = sum_over_devices(blocks)

    ranks = 2 * RK // steps
    left_out, right_out = pl.pallas_call(
        functools.partial(outputs_kernel, points),
        grid=(steps // 2, 2),
        in_specs=[
            pl.BlockSpec((chunk, RK), lambda i, c: (2 * i + c, 0)),
            pl.BlockSpec((RK, RK), lambda i, c: (0, 0)),
            pl.BlockSpec((points, ranks, LANES), lambda i, c: (0, i, c)),
        ],
        out_specs=[
            pl.BlockSpec((chunk, RK), lambda i, c: (2 * i + c, 0)),
            pl.BlockSpec((ranks * points, LANES), lambda i, c: (i, c)),
        ],
        out_shape=[shape(rank_left * points, RK), shape(RK * points, rank_right)],
        compiler_params=params(("arbitrary", "arbitrary")),
        cost_estimate=pl.CostEstimate(flops=0, bytes_accessed=24 * 2**20, transcendentals=0),
        name="outputs",
    )(unfold, linv, absorbed)

    factor = pl.pallas_call(
        functools.partial(factor_kernel, 1.0 / (RK * total_points), SPREAD_TWO),
        in_specs=[vmem] * SPREAD_TWO,
        out_specs=vmem,
        out_shape=shape(rank_right, rank_right),
        scratch_shapes=[
            pltpu.VMEM((packed_rows, LANES), F32),
            pltpu.VMEM((LANES, 2 * LANES), F32),
            pltpu.VMEM((LANES, LANES), F32),
        ],
        compiler_params=params(),
        name="factor_next",
    )(*summed)
    return (
        left_out.reshape(rank_left, points, RK),
        right_out.reshape(RK, points, rank_right),
        factor,
    )


def solution(mesh):
    in_specs = (P(None, AXES, None), P(None, AXES, None))
    out_specs = (P(None, AXES, None), P(None, AXES, None), P())
    return jax.shard_map(
        per_device, mesh=mesh, in_specs=in_specs, out_specs=out_specs, check_vma=False
    )
```

```python
import functools
import math

import jax
import jax.numpy as jnp
from jax import lax
from jax.experimental import pallas as pl
from jax.experimental.pallas import tpu as pltpu
from jax.sharding import PartitionSpec as P

RK = 128
AXES = ("gx", "gy", "gz")
LANES = 128
PANEL = 16
SCATTER = ("gx", "gy")
RELAYS = 2
F32 = jnp.float32
BF16 = jnp.bfloat16
VMEM_LIMIT = 48 * 1024 * 1024


def split(x):
    hi = x.astype(BF16)
    return hi, (x - hi.astype(F32)).astype(BF16)


def dot_tn(a, b):
    return lax.dot_general(a, b, (((0,), (0,)), ((), ())), preferred_element_type=F32)


def dot_nt(a, b):
    return lax.dot_general(a, b, (((1,), (1,)), ((), ())), preferred_element_type=F32)


def dot_nn(a, b):
    return lax.dot_general(a, b, (((1,), (0,)), ((), ())), preferred_element_type=F32)


def stacked_pieces(x):
    one = x.astype(BF16).astype(F32)
    rest = x - one
    two = rest.astype(BF16).astype(F32)
    three = rest - two
    left = jnp.concatenate([one, one, two, two, one, three], axis=0).astype(BF16)
    right = jnp.concatenate([one, two, one, two, three, one], axis=0).astype(BF16)
    return left, right


def factor_rows(w_ref, blocks):
    row_id = lax.broadcasted_iota(jnp.int32, (PANEL, LANES), 0)
    for start in range(0, LANES, PANEL):
        rows = [w_ref[start : start + PANEL, b * LANES : (b + 1) * LANES] for b in range(blocks)]
        columns = [
            jnp.broadcast_to(rows[0][:, start + k : start + k + 1], (PANEL, LANES))
            for k in range(PANEL)
        ]
        scale = jnp.zeros((PANEL, LANES), F32)
        for k in range(PANEL):
            pivot = jnp.broadcast_to(columns[k][k : k + 1, :], (PANEL, LANES))
            inverse = lax.rsqrt(pivot)
            inverse = inverse * (1.5 - 0.5 * pivot * inverse * inverse)
            multiples = columns[k] * inverse
            for m in range(k + 1, PANEL):
                columns[m] = columns[m] - multiples * multiples[m : m + 1, :]
            below = jnp.where(row_id > k, multiples * inverse, 0.0)
            rows = [r - below * r[k : k + 1, :] for r in rows]
            scale = jnp.where(row_id == k, inverse, scale)
        rows = [r * scale for r in rows]
        for b in range(blocks):
            w_ref[start : start + PANEL, b * LANES : (b + 1) * LANES] = rows[b]
        if start + PANEL < LANES:
            both = [stacked_pieces(r) for r in rows]
            left = both[0][0]
            right = jnp.concatenate([b[1] for b in both], axis=1)
            update = dot_tn(left, right)
            w_ref[start + PANEL :, :] = w_ref[start + PANEL :, :] - update[start + PANEL :, :]


def triangle_ids():
    return (
        lax.broadcasted_iota(jnp.int32, (LANES, LANES), 0),
        lax.broadcasted_iota(jnp.int32, (LANES, LANES), 1),
    )


def gram_kernel(a_ref, tall_ref, token_ref):
    @pl.when(pl.program_id(0) == 0)
    def _():
        tall_ref[...] = jnp.zeros_like(tall_ref)
        token_ref[...] = jnp.zeros_like(token_ref)

    hi, lo = split(a_ref[...])
    both = dot_tn(hi[:, :RK], jnp.concatenate([hi, lo], axis=1))
    top = both[:, :256] + both[:, 256:] + dot_tn(lo[:, :RK], hi)
    tall_ref[:RK, :] += top[:, :RK]
    tall_ref[RK:, :] += top[:, RK:]


def add_kernel(copies, terms_ref, _, out_ref, token_ref):
    total = terms_ref[0]
    for i in range(1, terms_ref.shape[0]):
        total = total + terms_ref[i]
    for i in range(copies):
        out_ref[i] = total
    token_ref[...] = jnp.zeros_like(token_ref)


def relay_kernel(points, left_ref, right_ref, _, hi_ref, lo_ref, token_ref):
    token_ref[...] = jnp.zeros_like(token_ref)
    count = left_ref.shape[0] // points
    for p in range(points):
        for c, half in enumerate((left_ref, right_ref)):
            hi, lo = split(half[pl.ds(p, count, stride=points), :])
            hi_ref[p, :, c * LANES : (c + 1) * LANES] = hi
            lo_ref[p, :, c * LANES : (c + 1) * LANES] = lo


def absorb_kernel(scale, tall_ref, *refs):
    highs, lows = refs[:RELAYS], refs[RELAYS : 2 * RELAYS]
    absorbed_ref, linv_ref, pack_ref, w_ref, total_ref = refs[2 * RELAYS :]
    row, col = triangle_ids()
    w_ref[:, :LANES] = tall_ref[:RK, :]
    w_ref[:, LANES : 2 * LANES] = tall_ref[RK:, :]
    w_ref[:, 2 * LANES :] = jnp.where(row == col, 1.0, 0.0).astype(F32)
    factor_rows(w_ref, 3)
    linv_ref[...] = w_ref[:, 2 * LANES :] * scale
    upper = jnp.concatenate(
        [jnp.where(col >= row, w_ref[:, :LANES], 0.0), w_ref[:, LANES : 2 * LANES]], axis=1
    )
    upper_hi, upper_lo = split(upper)
    upper_both = jnp.concatenate([upper_hi, upper_lo], axis=0)
    points = absorbed_ref.shape[0]
    group = 4
    total_ref[...] = jnp.zeros_like(total_ref)

    def body(step, carry):
        pieces = []
        for i in range(group):
            p = step * group + i
            high = jnp.concatenate([ref[p] for ref in highs], axis=0)
            low = jnp.concatenate([ref[p] for ref in lows], axis=0)
            first = dot_nn(upper_both, high)
            b = first[:RK, :] + first[RK:, :] + dot_nn(upper_hi, low)
            absorbed_ref[p] = b
            pieces.append(split(b))
        b_hi = jnp.concatenate([x[0] for x in pieces], axis=0)
        b_lo = jnp.concatenate([x[1] for x in pieces], axis=0)
        total_ref[...] += dot_tn(b_hi, jnp.concatenate([b_hi, b_lo], axis=1))
        return carry

    lax.fori_loop(0, points // group, body, 0)
    cross = total_ref[:, 256:]
    gram = total_ref[:, :256] + cross + cross.T
    lower_right = gram[LANES:, LANES:]
    pack_ref[:LANES, :] = jnp.where(col >= row, gram[:LANES, :LANES], lower_right)
    pack_ref[LANES : 2 * LANES, :] = gram[:LANES, LANES:]
    diagonal = jnp.sum(jnp.where(row == col, lower_right, 0.0), axis=0, keepdims=True)
    tail = pack_ref.shape[0] - 2 * LANES
    pack_ref[2 * LANES :, :] = jnp.broadcast_to(diagonal, (tail, LANES))


def left_kernel(a_ref, linv_ref, left_ref, token_ref):
    l_hi, l_lo = split(linv_ref[...])
    hi, lo = split(a_ref[...])
    left_ref[...] = dot_nt(hi, l_hi) + dot_nt(hi, l_lo) + dot_nt(lo, l_hi)
    token_ref[...] = jnp.zeros_like(token_ref)


def right_kernel(points, absorbed_ref, _, right_ref, token_ref):
    count = absorbed_ref.shape[1]
    for p in range(points):
        right_ref[pl.ds(p, count, stride=points), :] = absorbed_ref[p]
    token_ref[...] = jnp.zeros_like(token_ref)


def factor_kernel(scale, pack_ref, out_ref, w_ref, rest_ref):
    row, col = triangle_ids()
    packed = pack_ref[:LANES, :] * scale
    turned = packed.T
    diagonal = jnp.broadcast_to(pack_ref[2 * LANES : 2 * LANES + 1, :], (LANES, LANES)) * scale
    w_ref[:, :LANES] = jnp.where(col >= row, packed, turned)
    w_ref[:, LANES:] = pack_ref[LANES : 2 * LANES, :] * scale
    rest_ref[...] = jnp.where(row > col, packed, jnp.where(row == col, diagonal, turned))
    factor_rows(w_ref, 2)
    out_ref[:LANES, :LANES] = jnp.where(col >= row, w_ref[:, :LANES], 0.0)
    out_ref[:LANES, LANES:] = w_ref[:, LANES:]
    left, right = stacked_pieces(w_ref[:, LANES:])
    rest_ref[...] = rest_ref[...] - dot_tn(left, right)
    factor_rows(rest_ref, 1)
    out_ref[LANES:, :LANES] = jnp.zeros((LANES, LANES), F32)
    out_ref[LANES:, LANES:] = jnp.where(col >= row, rest_ref[...], 0.0)


def shape(*dims, dtype=F32):
    return jax.ShapeDtypeStruct(dims, dtype)


TOKEN = shape(8, LANES)


def params(steps=0, limit=VMEM_LIMIT):
    return pltpu.CompilerParams(
        dimension_semantics=("arbitrary",) * steps or None, vmem_limit_bytes=limit
    )


def cost(mebibytes):
    return pl.CostEstimate(flops=0, bytes_accessed=mebibytes * 2**20, transcendentals=0)


def add_terms(terms, token, copies):
    vmem = pl.BlockSpec(memory_space=pltpu.VMEM)
    return pl.pallas_call(
        functools.partial(add_kernel, copies),
        in_specs=[vmem] * 2,
        out_specs=[vmem] * 2,
        out_shape=[shape(copies, *terms.shape[1:]), TOKEN],
        compiler_params=params(limit=8 * 1024 * 1024),
        cost_estimate=cost(1),
        name="add_terms",
    )(terms, token)


def sum_over_devices(tall, token, first_work, second_work):
    spread = lax.axis_size("gx") * lax.axis_size("gy")
    layers = lax.axis_size("gz")
    blocks = tall.reshape(spread, tall.shape[0] // spread, LANES)
    received = lax.all_to_all(blocks, SCATTER, 0, 0)
    first, token = first_work(token)
    copies, token = add_terms(received, token, layers)
    received = lax.all_to_all(copies, "gz", 0, 0)
    second, token = second_work(token)
    copies, _ = add_terms(received, token, spread)
    gathered = lax.all_to_all(copies, SCATTER, 0, 0)
    return gathered.reshape(tall.shape), first, second


def relay_part(rows_right, points, part, token):
    steps = 4
    chunk = rows_right.shape[0] // (RELAYS * steps)
    ranks = chunk // points
    width = rows_right.shape[1]
    high, low, token = pl.pallas_call(
        functools.partial(relay_kernel, points),
        grid=(steps,),
        in_specs=[
            pl.BlockSpec((chunk, LANES), lambda i: (part * steps + i, 0)),
            pl.BlockSpec((chunk, LANES), lambda i: (part * steps + i, 1)),
            pl.BlockSpec((8, LANES), lambda i: (0, 0)),
        ],
        out_specs=[pl.BlockSpec((points, ranks, width), lambda i: (0, i, 0))] * 2
        + [pl.BlockSpec((8, LANES), lambda i: (0, 0))],
        out_shape=[shape(points, steps * ranks, width, dtype=BF16)] * 2 + [TOKEN],
        compiler_params=params(1, 16 * 1024 * 1024),
        cost_estimate=cost(8),
        name="relay_right",
    )(rows_right, rows_right, token)
    return (high, low), token


def left_part(unfold, linv, _):
    steps = 4
    chunk = unfold.shape[0] // steps
    return pl.pallas_call(
        left_kernel,
        grid=(steps,),
        in_specs=[
            pl.BlockSpec((chunk, RK), lambda i: (i, 0)),
            pl.BlockSpec((RK, RK), lambda i: (0, 0)),
        ],
        out_specs=[
            pl.BlockSpec((chunk, RK), lambda i: (i, 0)),
            pl.BlockSpec((8, LANES), lambda i: (0, 0)),
        ],
        out_shape=[shape(unfold.shape[0], RK), TOKEN],
        compiler_params=params(1, 16 * 1024 * 1024),
        cost_estimate=cost(8),
        name="left_out",
    )(unfold, linv)


def right_part(absorbed, token):
    points, ranks, width = absorbed.shape
    steps = 2
    return pl.pallas_call(
        functools.partial(right_kernel, points),
        grid=(steps, 2),
        in_specs=[
            pl.BlockSpec((points, ranks // steps, LANES), lambda i, c: (0, i, c)),
            pl.BlockSpec((8, LANES), lambda i, c: (0, 0)),
        ],
        out_specs=[
            pl.BlockSpec((ranks // steps * points, LANES), lambda i, c: (i, c)),
            pl.BlockSpec((8, LANES), lambda i, c: (0, 0)),
        ],
        out_shape=[shape(ranks * points, width), TOKEN],
        compiler_params=params(2, 16 * 1024 * 1024),
        cost_estimate=cost(8),
        name="right_out",
    )(absorbed, token)


def per_device(left_core, right_core):
    rank_left, points, rank_mid = left_core.shape
    rank_right = right_core.shape[2]
    spread = lax.axis_size("gx") * lax.axis_size("gy")
    total_points = points * spread * lax.axis_size("gz")
    unfold = left_core.reshape(rank_left * points, rank_mid)
    rows_right = right_core.reshape(rank_mid * points, rank_right)
    vmem = pl.BlockSpec(memory_space=pltpu.VMEM)

    steps = 8
    tall, token = pl.pallas_call(
        gram_kernel,
        grid=(steps,),
        in_specs=[pl.BlockSpec((unfold.shape[0] // steps, rank_mid), lambda i: (i, 0))],
        out_specs=[
            pl.BlockSpec((2 * RK, LANES), lambda i: (0, 0)),
            pl.BlockSpec((8, LANES), lambda i: (0, 0)),
        ],
        out_shape=[shape(2 * RK, LANES), TOKEN],
        compiler_params=params(1, 56 * 1024 * 1024),
        name="gram_top",
    )(unfold)
    tall, *relayed = sum_over_devices(
        tall,
        token,
        functools.partial(relay_part, rows_right, points, 0),
        functools.partial(relay_part, rows_right, points, 1),
    )

    block_rows = -(-(2 * LANES + 8) // (8 * spread)) * 8
    absorbed, linv, packed = pl.pallas_call(
        functools.partial(absorb_kernel, math.sqrt(rank_left * total_points)),
        in_specs=[vmem] * (1 + 2 * RELAYS),
        out_specs=[vmem] * 3,
        out_shape=[
            shape(points, RK, rank_right),
            shape(RK, RK),
            shape(block_rows * spread, LANES),
        ],
        scratch_shapes=[
            pltpu.VMEM((LANES, 3 * LANES), F32),
            pltpu.VMEM((rank_right, 2 * rank_right), F32),
        ],
        compiler_params=params(limit=24 * 1024 * 1024),
        name="factor_absorb",
    )(tall, *[r[0] for r in relayed], *[r[1] for r in relayed])
    packed, left_out, right_out = sum_over_devices(
        packed,
        linv,
        functools.partial(left_part, unfold, linv),
        functools.partial(right_part, absorbed),
    )

    factor = pl.pallas_call(
        functools.partial(factor_kernel, 1.0 / (RK * total_points)),
        in_specs=[vmem],
        out_specs=vmem,
        out_shape=shape(rank_right, rank_right),
        scratch_shapes=[
            pltpu.VMEM((LANES, 2 * LANES), F32),
            pltpu.VMEM((LANES, LANES), F32),
        ],
        compiler_params=params(limit=16 * 1024 * 1024),
        name="factor_next",
    )(packed)
    return (
        left_out.reshape(rank_left, points, RK),
        right_out.reshape(RK, points, rank_right),
        factor,
    )


def solution(mesh):
    in_specs = (P(None, AXES, None), P(None, AXES, None))
    out_specs = (P(None, AXES, None), P(None, AXES, None), P())
    return jax.shard_map(
        per_device, mesh=mesh, in_specs=in_specs, out_specs=out_specs, check_vma=False
    )
```

```python
import functools
import math

import jax
import jax.numpy as jnp
from jax import lax
from jax.experimental import pallas as pl
from jax.experimental.pallas import tpu as pltpu
from jax.sharding import PartitionSpec as P

RK = 128
AXES = ("gx", "gy", "gz")
LANES = 128
RELAYS = 2
F32 = jnp.float32
BF16 = jnp.bfloat16
VMEM_LIMIT = 48 * 1024 * 1024


def split(x):
    hi = x.astype(BF16)
    return hi, (x - hi.astype(F32)).astype(BF16)


def dot_tn(a, b):
    return lax.dot_general(a, b, (((0,), (0,)), ((), ())), preferred_element_type=F32)


def dot_nt(a, b):
    return lax.dot_general(a, b, (((1,), (1,)), ((), ())), preferred_element_type=F32)


def dot_nn(a, b):
    return lax.dot_general(a, b, (((1,), (0,)), ((), ())), preferred_element_type=F32)


def stacked_pieces(x):
    one = x.astype(BF16).astype(F32)
    rest = x - one
    two = rest.astype(BF16).astype(F32)
    three = rest - two
    left = jnp.concatenate([one, one, two, two, one, three], axis=0).astype(BF16)
    right = jnp.concatenate([one, two, one, two, three, one], axis=0).astype(BF16)
    return left, right


def spread_row(x, k):
    return jnp.broadcast_to(x[k : k + 1, :], x.shape)


def factor_rows(w_ref, blocks, panel):
    row_id = lax.broadcasted_iota(jnp.int32, (8, LANES), 0)
    groups = panel // 8
    for start in range(0, LANES, panel):
        rows = [
            [
                w_ref[start + 8 * v : start + 8 * v + 8, b * LANES : (b + 1) * LANES]
                for b in range(blocks)
            ]
            for v in range(groups)
        ]
        columns = [
            [
                jnp.broadcast_to(rows[v][0][:, start + k : start + k + 1], (8, LANES))
                for v in range(groups)
            ]
            for k in range(panel)
        ]
        scales = [jnp.zeros((8, LANES), F32)] * groups
        pivot = spread_row(columns[0][0], 0)
        for k in range(panel):
            home, at = k // 8, k % 8
            inverse = pl.reciprocal(pivot, approx=True)
            scales[home] = jnp.where(row_id == at, lax.rsqrt(pivot), scales[home])
            multiples = [columns[k][v] * inverse for v in range(groups)]
            for m in range(k + 1, panel):
                entry = spread_row(columns[k][m // 8], m % 8)
                if m == k + 1:
                    pivot = spread_row(columns[m][m // 8], m % 8) - (entry * inverse) * entry
                for v in range(m // 8, groups):
                    columns[m][v] = columns[m][v] - multiples[v] * entry
            for b in range(blocks):
                source = spread_row(rows[home][b], at)
                for v in range(home, groups):
                    below = multiples[v]
                    if v == home:
                        below = jnp.where(row_id > at, below, 0.0)
                    rows[v][b] = rows[v][b] - below * source
        done = [
            jnp.concatenate([rows[v][b] * scales[v] for v in range(groups)], axis=0)
            for b in range(blocks)
        ]
        for b in range(blocks):
            w_ref[start : start + panel, b * LANES : (b + 1) * LANES] = done[b]
        if start + panel < LANES:
            both = [stacked_pieces(x) for x in done]
            left = both[0][0]
            right = jnp.concatenate([x[1] for x in both], axis=1)
            update = dot_tn(left, right)
            w_ref[start + panel :, :] = w_ref[start + panel :, :] - update[start + panel :, :]


def triangle_ids():
    return (
        lax.broadcasted_iota(jnp.int32, (LANES, LANES), 0),
        lax.broadcasted_iota(jnp.int32, (LANES, LANES), 1),
    )


def store_blocks(tall_ref, outs):
    me = lax.rem(lax.axis_index("gy"), len(outs))
    size = outs[0].shape[0]
    for d, out in enumerate(outs):
        out[...] = tall_ref[pl.ds(pl.multiple_of((me ^ d) * size, 8), size), :]


def load_blocks(blocks, tall_ref):
    me = lax.rem(lax.axis_index("gy"), len(blocks))
    size = blocks[0].shape[0]
    for d, block in enumerate(blocks):
        tall_ref[pl.ds(pl.multiple_of((me ^ d) * size, 8), size), :] = block[...]


def gram_kernel(a_hbm, first_ref, second_ref, a_ref, tall_ref, sems):
    steps = a_ref.shape[0]
    chunk = a_ref.shape[1]

    def copy(i):
        return pltpu.make_async_copy(
            a_hbm.at[pl.ds(i * chunk, chunk), :], a_ref.at[i], sems.at[i]
        )

    for i in range(steps):
        copy(i).start()
    tall_ref[...] = jnp.zeros_like(tall_ref)

    def body(i, carry):
        copy(i).wait()
        hi, lo = split(a_ref[i])
        both = dot_tn(hi[:, :RK], jnp.concatenate([hi, lo], axis=1))
        top = both[:, :256] + both[:, 256:] + dot_tn(lo[:, :RK], hi)
        tall_ref[:RK, :] += top[:, :RK]
        tall_ref[RK:, :] += top[:, RK:]
        return carry

    lax.fori_loop(0, steps, body, 0)
    store_blocks(tall_ref, (first_ref, second_ref))


def relay_kernel(points, left_ref, right_ref, _, hi_ref, lo_ref, token_ref):
    token_ref[...] = jnp.zeros_like(token_ref)
    count = left_ref.shape[0] // points
    for p in range(points):
        for c, half in enumerate((left_ref, right_ref)):
            hi, lo = split(half[pl.ds(p, count, stride=points), :])
            hi_ref[p, :, c * LANES : (c + 1) * LANES] = hi
            lo_ref[p, :, c * LANES : (c + 1) * LANES] = lo


def absorb_kernel(scale, own_ref, other_ref, *refs):
    highs, lows = refs[:RELAYS], refs[RELAYS : 2 * RELAYS]
    absorbed_ref, linv_ref, first_ref, second_ref = refs[2 * RELAYS : 2 * RELAYS + 4]
    tall_ref, pack_ref, w_ref, total_ref = refs[2 * RELAYS + 4 :]
    row, col = triangle_ids()
    load_blocks((own_ref, other_ref), tall_ref)
    w_ref[:, :LANES] = tall_ref[:RK, :]
    w_ref[:, LANES : 2 * LANES] = tall_ref[RK:, :]
    w_ref[:, 2 * LANES :] = jnp.where(row == col, 1.0, 0.0).astype(F32)
    factor_rows(w_ref, 3, 16)
    linv_ref[...] = w_ref[:, 2 * LANES :] * scale
    upper = jnp.concatenate(
        [jnp.where(col >= row, w_ref[:, :LANES], 0.0), w_ref[:, LANES : 2 * LANES]], axis=1
    )
    upper_hi, upper_lo = split(upper)
    upper_both = jnp.concatenate([upper_hi, upper_lo], axis=0)
    points = absorbed_ref.shape[0]
    group = 4
    total_ref[...] = jnp.zeros_like(total_ref)

    def body(step, carry):
        pieces = []
        for i in range(group):
            p = step * group + i
            high = jnp.concatenate([ref[p] for ref in highs], axis=0)
            low = jnp.concatenate([ref[p] for ref in lows], axis=0)
            first = dot_nn(upper_both, high)
            b = first[:RK, :] + first[RK:, :] + dot_nn(upper_hi, low)
            absorbed_ref[p] = b
            pieces.append(split(b))
        b_hi = jnp.concatenate([x[0] for x in pieces], axis=0)
        b_lo = jnp.concatenate([x[1] for x in pieces], axis=0)
        total_ref[...] += dot_tn(b_hi, jnp.concatenate([b_hi, b_lo], axis=1))
        return carry

    lax.fori_loop(0, points // group, body, 0)
    cross = total_ref[:, 256:]
    gram = total_ref[:, :256] + cross + cross.T
    lower_right = gram[LANES:, LANES:]
    pack_ref[:LANES, :] = jnp.where(col >= row, gram[:LANES, :LANES], lower_right)
    pack_ref[LANES : 2 * LANES, :] = gram[:LANES, LANES:]
    diagonal = jnp.sum(jnp.where(row == col, lower_right, 0.0), axis=0, keepdims=True)
    tail = pack_ref.shape[0] - 2 * LANES
    pack_ref[2 * LANES :, :] = jnp.broadcast_to(diagonal, (tail, LANES))
    store_blocks(pack_ref, (first_ref, second_ref))


def left_kernel(a_ref, linv_ref, _, left_ref, token_ref):
    l_hi, l_lo = split(linv_ref[...])
    hi, lo = split(a_ref[...])
    left_ref[...] = dot_nt(hi, l_hi) + dot_nt(hi, l_lo) + dot_nt(lo, l_hi)
    token_ref[...] = jnp.zeros_like(token_ref)


def right_kernel(points, absorbed_ref, _, right_ref, token_ref):
    count = absorbed_ref.shape[1]
    for p in range(points):
        right_ref[pl.ds(p, count, stride=points), :] = absorbed_ref[p]
    token_ref[...] = jnp.zeros_like(token_ref)


def factor_kernel(scale, own_ref, other_ref, out_ref, pack_ref, w_ref, rest_ref):
    load_blocks((own_ref, other_ref), pack_ref)
    row, col = triangle_ids()
    packed = pack_ref[:LANES, :] * scale
    turned = packed.T
    diagonal = jnp.broadcast_to(pack_ref[2 * LANES : 2 * LANES + 1, :], (LANES, LANES)) * scale
    w_ref[:, :LANES] = jnp.where(col >= row, packed, turned)
    w_ref[:, LANES:] = pack_ref[LANES : 2 * LANES, :] * scale
    rest_ref[...] = jnp.where(row > col, packed, jnp.where(row == col, diagonal, turned))
    factor_rows(w_ref, 2, 32)
    out_ref[:LANES, :LANES] = jnp.where(col >= row, w_ref[:, :LANES], 0.0)
    out_ref[:LANES, LANES:] = w_ref[:, LANES:]
    left, right = stacked_pieces(w_ref[:, LANES:])
    rest_ref[...] = rest_ref[...] - dot_tn(left, right)
    factor_rows(rest_ref, 1, 32)
    out_ref[LANES:, :LANES] = jnp.zeros((LANES, LANES), F32)
    out_ref[LANES:, LANES:] = jnp.where(col >= row, rest_ref[...], 0.0)


def shape(*dims, dtype=F32):
    return jax.ShapeDtypeStruct(dims, dtype)


TOKEN = shape(8, LANES)


def params(steps=0, limit=VMEM_LIMIT):
    return pltpu.CompilerParams(
        dimension_semantics=("arbitrary",) * steps or None, vmem_limit_bytes=limit
    )


def cost(mebibytes):
    return pl.CostEstimate(flops=0, bytes_accessed=mebibytes * 2**20, transcendentals=0)


def exchange(value, axis, bit):
    size = lax.axis_size(axis)
    return lax.ppermute(value, axis, [(i, i ^ bit) for i in range(size)])


def sum_over_devices(blocks, works):
    total = blocks[0] + exchange(blocks[1], "gy", 1)
    stages = [
        (axis, 1 << bit)
        for axis in ("gy", "gx", "gz")
        for bit in range(lax.axis_size(axis).bit_length() - 1)
        if (axis, bit) != ("gy", 0)
    ]
    results = []
    for i, (axis, bit) in enumerate(stages):
        received = exchange(total, axis, bit)
        if i in works:
            result, token = works[i](total)
            results.append(result)
            received = received + token[:1, :]
        total = total + received
    return [total, exchange(total, "gy", 1)], results


def relay_part(rows_right, points, part, token):
    steps = 4
    chunk = rows_right.shape[0] // (RELAYS * steps)
    ranks = chunk // points
    width = rows_right.shape[1]
    high, low, token = pl.pallas_call(
        functools.partial(relay_kernel, points),
        grid=(steps,),
        in_specs=[
            pl.BlockSpec((chunk, LANES), lambda i: (part * steps + i, 0)),
            pl.BlockSpec((chunk, LANES), lambda i: (part * steps + i, 1)),
            pl.BlockSpec((8, LANES), lambda i: (0, 0)),
        ],
        out_specs=[pl.BlockSpec((points, ranks, width), lambda i: (0, i, 0))] * 2
        + [pl.BlockSpec((8, LANES), lambda i: (0, 0))],
        out_shape=[shape(points, steps * ranks, width, dtype=BF16)] * 2 + [TOKEN],
        compiler_params=params(1, 16 * 1024 * 1024),
        cost_estimate=cost(8),
        name="relay_right",
    )(rows_right, rows_right, token)
    return (high, low), token


def left_part(unfold, linv, token):
    steps = 4
    chunk = unfold.shape[0] // steps
    return pl.pallas_call(
        left_kernel,
        grid=(steps,),
        in_specs=[
            pl.BlockSpec((chunk, RK), lambda i: (i, 0)),
            pl.BlockSpec((RK, RK), lambda i: (0, 0)),
            pl.BlockSpec((8, LANES), lambda i: (0, 0)),
        ],
        out_specs=[
            pl.BlockSpec((chunk, RK), lambda i: (i, 0)),
            pl.BlockSpec((8, LANES), lambda i: (0, 0)),
        ],
        out_shape=[shape(unfold.shape[0], RK), TOKEN],
        compiler_params=params(1, 16 * 1024 * 1024),
        cost_estimate=cost(8),
        name="left_out",
    )(unfold, linv, token)


def right_part(absorbed, token):
    points, ranks, width = absorbed.shape
    steps = 2
    return pl.pallas_call(
        functools.partial(right_kernel, points),
        grid=(steps, 2),
        in_specs=[
            pl.BlockSpec((points, ranks // steps, LANES), lambda i, c: (0, i, c)),
            pl.BlockSpec((8, LANES), lambda i, c: (0, 0)),
        ],
        out_specs=[
            pl.BlockSpec((ranks // steps * points, LANES), lambda i, c: (i, c)),
            pl.BlockSpec((8, LANES), lambda i, c: (0, 0)),
        ],
        out_shape=[shape(ranks * points, width), TOKEN],
        compiler_params=params(2, 16 * 1024 * 1024),
        cost_estimate=cost(8),
        name="right_out",
    )(absorbed, token)


def per_device(left_core, right_core):
    rank_left, points, rank_mid = left_core.shape
    rank_right = right_core.shape[2]
    total_points = points * lax.axis_size("gx") * lax.axis_size("gy") * lax.axis_size("gz")
    unfold = left_core.reshape(rank_left * points, rank_mid)
    rows_right = right_core.reshape(rank_mid * points, rank_right)
    vmem = pl.BlockSpec(memory_space=pltpu.VMEM)

    steps = 8
    half = RK
    blocks = pl.pallas_call(
        gram_kernel,
        in_specs=[pl.BlockSpec(memory_space=pl.ANY)],
        out_specs=[vmem] * 2,
        out_shape=[shape(half, LANES)] * 2,
        scratch_shapes=[
            pltpu.VMEM((steps, unfold.shape[0] // steps, rank_mid), F32),
            pltpu.VMEM((2 * half, LANES), F32),
            pltpu.SemaphoreType.DMA((steps,)),
        ],
        compiler_params=params(limit=62 * 1024 * 1024),
        name="gram_top",
    )(unfold)
    summed, relayed = sum_over_devices(
        blocks,
        {2 + i: functools.partial(relay_part, rows_right, points, i) for i in range(RELAYS)},
    )

    half = LANES + 8
    absorbed, linv, *blocks = pl.pallas_call(
        functools.partial(absorb_kernel, math.sqrt(rank_left * total_points)),
        in_specs=[vmem] * (2 + 2 * RELAYS),
        out_specs=[vmem] * 4,
        out_shape=[shape(points, RK, rank_right), shape(RK, RK)] + [shape(half, LANES)] * 2,
        scratch_shapes=[
            pltpu.VMEM((2 * RK, LANES), F32),
            pltpu.VMEM((2 * half, LANES), F32),
            pltpu.VMEM((LANES, 3 * LANES), F32),
            pltpu.VMEM((rank_right, 2 * rank_right), F32),
        ],
        compiler_params=params(limit=24 * 1024 * 1024),
        name="factor_absorb",
    )(*summed, *[r[0] for r in relayed], *[r[1] for r in relayed])
    summed, (right_out, left_out) = sum_over_devices(
        blocks,
        {
            2: functools.partial(right_part, absorbed),
            3: functools.partial(left_part, unfold, linv),
        },
    )

    factor = pl.pallas_call(
        functools.partial(factor_kernel, 1.0 / (RK * total_points)),
        in_specs=[vmem] * 2,
        out_specs=vmem,
        out_shape=shape(rank_right, rank_right),
        scratch_shapes=[
            pltpu.VMEM((2 * half, LANES), F32),
            pltpu.VMEM((LANES, 2 * LANES), F32),
            pltpu.VMEM((LANES, LANES), F32),
        ],
        compiler_params=params(limit=16 * 1024 * 1024),
        name="factor_next",
    )(*summed)
    return (
        left_out.reshape(rank_left, points, RK),
        right_out.reshape(RK, points, rank_right),
        factor,
    )


def solution(mesh):
    in_specs = (P(None, AXES, None), P(None, AXES, None))
    out_specs = (P(None, AXES, None), P(None, AXES, None), P())
    return jax.shard_map(
        per_device, mesh=mesh, in_specs=in_specs, out_specs=out_specs, check_vma=False
    )
```

```python
import functools
import math

import jax
import jax.numpy as jnp
from jax import lax
from jax.experimental import pallas as pl
from jax.experimental.pallas import tpu as pltpu
from jax.sharding import PartitionSpec as P

RK = 128
AXES = ("gx", "gy", "gz")
LANES = 128
PANEL = 16
F32 = jnp.float32
BF16 = jnp.bfloat16
VMEM_LIMIT = 48 * 1024 * 1024


def split(x):
    hi = x.astype(BF16)
    return hi, (x - hi.astype(F32)).astype(BF16)


def dot_tn(a, b):
    return lax.dot_general(a, b, (((0,), (0,)), ((), ())), preferred_element_type=F32)


def dot_nt(a, b):
    return lax.dot_general(a, b, (((1,), (1,)), ((), ())), preferred_element_type=F32)


def dot_nn(a, b):
    return lax.dot_general(a, b, (((1,), (0,)), ((), ())), preferred_element_type=F32)


def stacked_pieces(x):
    one = x.astype(BF16).astype(F32)
    rest = x - one
    two = rest.astype(BF16).astype(F32)
    three = rest - two
    left = jnp.concatenate([one, one, two, two, one, three], axis=0).astype(BF16)
    right = jnp.concatenate([one, two, one, two, three, one], axis=0).astype(BF16)
    return left, right


def spread_row(x, k):
    return jnp.broadcast_to(x[k : k + 1, :], x.shape)


def factor_rows(w_ref, blocks):
    row_id = lax.broadcasted_iota(jnp.int32, (8, LANES), 0)
    groups = PANEL // 8
    rows = [
        [w_ref[g : g + 8, b * LANES : (b + 1) * LANES] for b in range(blocks)]
        for g in range(0, LANES, 8)
    ]
    for start in range(0, LANES, PANEL):
        base = start // 8
        last = start + PANEL == LANES
        columns = [
            [
                jnp.broadcast_to(rows[base + v][0][:, start + k : start + k + 1], (8, LANES))
                for v in range(groups)
            ]
            for k in range(PANEL)
        ]
        ahead_groups = 0 if last else groups
        if not last:
            turned = jnp.concatenate([rows[base + v][0] for v in range(groups)], axis=0).T
            below_rows = [
                turned[start + PANEL + 8 * v : start + PANEL + 8 * v + 8, :] for v in range(groups)
            ]
            ahead = [
                [jnp.broadcast_to(below_rows[v][:, k : k + 1], (8, LANES)) for v in range(groups)]
                for k in range(PANEL)
            ]
        scales = [jnp.zeros((8, LANES), F32)] * groups
        pivot = spread_row(columns[0][0], 0)
        for k in range(PANEL):
            home, at = k // 8, k % 8
            inverse = pl.reciprocal(pivot, approx=True)
            scales[home] = jnp.where(row_id == at, lax.rsqrt(pivot), scales[home])
            multiples = [columns[k][v] * inverse for v in range(groups)]
            ahead_multiples = [ahead[k][v] * inverse for v in range(ahead_groups)]
            for m in range(k + 1, PANEL):
                entry = spread_row(columns[k][m // 8], m % 8)
                if m == k + 1:
                    pivot = spread_row(columns[m][m // 8], m % 8) - (entry * inverse) * entry
                for v in range(m // 8, groups):
                    columns[m][v] = columns[m][v] - multiples[v] * entry
                for v in range(ahead_groups):
                    ahead[m][v] = ahead[m][v] - ahead_multiples[v] * entry
            for b in range(blocks):
                source = spread_row(rows[base + home][b], at)
                for v in range(home, groups):
                    below = multiples[v]
                    if v == home:
                        below = jnp.where(row_id > at, below, 0.0)
                    rows[base + v][b] = rows[base + v][b] - below * source
                for v in range(ahead_groups):
                    g = base + groups + v
                    rows[g][b] = rows[g][b] - ahead_multiples[v] * source
        done = [
            jnp.concatenate([rows[base + v][b] * scales[v] for v in range(groups)], axis=0)
            for b in range(blocks)
        ]
        for b in range(blocks):
            w_ref[start : start + PANEL, b * LANES : (b + 1) * LANES] = done[b]
        if start + 2 * PANEL < LANES:
            both = [stacked_pieces(x) for x in done]
            left = both[0][0]
            right = jnp.concatenate([x[1] for x in both], axis=1)
            update = dot_tn(left, right)
            for g in range(base + 2 * groups, LANES // 8):
                for b in range(blocks):
                    rows[g][b] = (
                        rows[g][b] - update[8 * g : 8 * g + 8, b * LANES : (b + 1) * LANES]
                    )


def triangle_ids():
    return (
        lax.broadcasted_iota(jnp.int32, (LANES, LANES), 0),
        lax.broadcasted_iota(jnp.int32, (LANES, LANES), 1),
    )


def store_blocks(tall_ref, outs):
    me = lax.rem(lax.axis_index("gy"), len(outs))
    size = outs[0].shape[0]
    for d, out in enumerate(outs):
        out[...] = tall_ref[pl.ds(pl.multiple_of((me ^ d) * size, 8), size), :]


def load_blocks(blocks, tall_ref):
    me = lax.rem(lax.axis_index("gy"), len(blocks))
    size = blocks[0].shape[0]
    for d, block in enumerate(blocks):
        tall_ref[pl.ds(pl.multiple_of((me ^ d) * size, 8), size), :] = block[...]


def chunk_copies(source, held, sems):
    steps, chunk = held.shape[:2]

    def copy(i):
        return pltpu.make_async_copy(
            source.at[pl.ds(i * chunk, chunk), :], held.at[i], sems.at[i]
        )

    for i in range(steps):
        copy(i).start()
    return copy


def gram_kernel(a_hbm, first_ref, second_ref, a_ref, total_ref, tall_ref, sems):
    copy = chunk_copies(a_hbm, a_ref, sems)
    total_ref[...] = jnp.zeros_like(total_ref)

    def body(i, carry):
        copy(i).wait()
        hi, lo = split(a_ref[i])
        total_ref[...] += dot_tn(hi, jnp.concatenate([hi, lo], axis=1))
        return carry

    lax.fori_loop(0, a_ref.shape[0], body, 0)
    width = a_ref.shape[2]
    cross = total_ref[:, width : width + RK]
    tall_ref[:RK, :] = total_ref[:RK, :RK] + total_ref[:RK, width : width + RK] + cross[:RK, :].T
    tall_ref[RK:, :] = total_ref[:RK, RK:width] + total_ref[:RK, width + RK :] + cross[RK:, :].T
    store_blocks(tall_ref, (first_ref, second_ref))


def relay_kernel(points, r_hbm, _, hi_ref, lo_ref, token_ref, r_ref, sems):
    token_ref[...] = jnp.zeros_like(token_ref)
    halves, steps, chunk, _ = r_ref.shape
    ranks = chunk // points

    def copy(c, i):
        return pltpu.make_async_copy(
            r_hbm.at[pl.ds(i * chunk, chunk), pl.ds(c * LANES, LANES)],
            r_ref.at[c, i],
            sems.at[c, i],
        )

    for i in range(steps):
        for c in range(halves):
            copy(c, i).start()

    def body(i, carry):
        for c in range(halves):
            copy(c, i).wait()
            for p in range(points):
                hi, lo = split(r_ref[c, i, pl.ds(p, ranks, stride=points), :])
                place = pl.ds(pl.multiple_of(i * ranks, ranks), ranks)
                hi_ref[p, place, c * LANES : (c + 1) * LANES] = hi
                lo_ref[p, place, c * LANES : (c + 1) * LANES] = lo
        return carry

    lax.fori_loop(0, steps, body, 0)


def absorb_kernel(
    scale,
    own_ref,
    other_ref,
    hi_ref,
    lo_ref,
    absorbed_ref,
    linv_ref,
    first_ref,
    second_ref,
    tall_ref,
    pack_ref,
    w_ref,
    total_ref,
):
    row, col = triangle_ids()
    load_blocks((own_ref, other_ref), tall_ref)
    w_ref[:, :LANES] = tall_ref[:RK, :]
    w_ref[:, LANES : 2 * LANES] = tall_ref[RK:, :]
    w_ref[:, 2 * LANES :] = jnp.where(row == col, 1.0, 0.0).astype(F32)
    factor_rows(w_ref, 3)
    linv_ref[...] = w_ref[:, 2 * LANES :] * scale
    upper = jnp.concatenate(
        [jnp.where(col >= row, w_ref[:, :LANES], 0.0), w_ref[:, LANES : 2 * LANES]], axis=1
    )
    upper_hi, upper_lo = split(upper)
    upper_both = jnp.concatenate([upper_hi, upper_lo], axis=0)
    points = absorbed_ref.shape[0]
    group = 4
    total_ref[...] = jnp.zeros_like(total_ref)

    def body(step, carry):
        pieces = []
        for i in range(group):
            p = step * group + i
            first = dot_nn(upper_both, hi_ref[p])
            b = first[:RK, :] + first[RK:, :] + dot_nn(upper_hi, lo_ref[p])
            absorbed_ref[p] = b
            pieces.append(split(b))
        b_hi = jnp.concatenate([x[0] for x in pieces], axis=0)
        b_lo = jnp.concatenate([x[1] for x in pieces], axis=0)
        total_ref[...] += dot_tn(b_hi, jnp.concatenate([b_hi, b_lo], axis=1))
        return carry

    lax.fori_loop(0, points // group, body, 0)
    cross = total_ref[:, 256:]
    gram = total_ref[:, :256] + cross + cross.T
    lower_right = gram[LANES:, LANES:]
    pack_ref[:LANES, :] = jnp.where(col >= row, gram[:LANES, :LANES], lower_right)
    pack_ref[LANES : 2 * LANES, :] = gram[:LANES, LANES:]
    diagonal = jnp.sum(jnp.where(row == col, lower_right, 0.0), axis=0, keepdims=True)
    tail = pack_ref.shape[0] - 2 * LANES
    pack_ref[2 * LANES :, :] = jnp.broadcast_to(diagonal, (tail, LANES))
    store_blocks(pack_ref, (first_ref, second_ref))


def left_kernel(a_ref, linv_ref, _, left_ref, token_ref):
    l_hi, l_lo = split(linv_ref[...])
    hi, lo = split(a_ref[...])
    left_ref[...] = dot_nt(hi, l_hi) + dot_nt(hi, l_lo) + dot_nt(lo, l_hi)
    token_ref[...] = jnp.zeros_like(token_ref)


def right_kernel(points, absorbed_ref, _, right_ref, token_ref):
    count = absorbed_ref.shape[1]
    for p in range(points):
        right_ref[pl.ds(p, count, stride=points), :] = absorbed_ref[p]
    token_ref[...] = jnp.zeros_like(token_ref)


def factor_kernel(scale, own_ref, other_ref, out_ref, pack_ref, w_ref, rest_ref):
    load_blocks((own_ref, other_ref), pack_ref)
    row, col = triangle_ids()
    packed = pack_ref[:LANES, :] * scale
    turned = packed.T
    diagonal = jnp.broadcast_to(pack_ref[2 * LANES : 2 * LANES + 1, :], (LANES, LANES)) * scale
    w_ref[:, :LANES] = jnp.where(col >= row, packed, turned)
    w_ref[:, LANES:] = pack_ref[LANES : 2 * LANES, :] * scale
    rest_ref[...] = jnp.where(row > col, packed, jnp.where(row == col, diagonal, turned))
    factor_rows(w_ref, 2)
    out_ref[:LANES, :LANES] = jnp.where(col >= row, w_ref[:, :LANES], 0.0)
    out_ref[:LANES, LANES:] = w_ref[:, LANES:]
    left, right = stacked_pieces(w_ref[:, LANES:])
    rest_ref[...] = rest_ref[...] - dot_tn(left, right)
    factor_rows(rest_ref, 1)
    out_ref[LANES:, :LANES] = jnp.zeros((LANES, LANES), F32)
    out_ref[LANES:, LANES:] = jnp.where(col >= row, rest_ref[...], 0.0)


def shape(*dims, dtype=F32):
    return jax.ShapeDtypeStruct(dims, dtype)


TOKEN = shape(8, LANES)


def params(steps=0, limit=VMEM_LIMIT):
    return pltpu.CompilerParams(
        dimension_semantics=("arbitrary",) * steps or None, vmem_limit_bytes=limit
    )


def cost(mebibytes):
    return pl.CostEstimate(flops=0, bytes_accessed=mebibytes * 2**20, transcendentals=0)


def exchange(value, axis, bit):
    size = lax.axis_size(axis)
    return lax.ppermute(value, axis, [(i, i ^ bit) for i in range(size)])


def sum_over_devices(blocks, works):
    total = blocks[0] + exchange(blocks[1], "gy", 1)
    stages = [
        (axis, 1 << bit)
        for axis in ("gy", "gx", "gz")
        for bit in range(lax.axis_size(axis).bit_length() - 1)
        if (axis, bit) != ("gy", 0)
    ]
    results = []
    for i, (axis, bit) in enumerate(stages):
        received = exchange(total, axis, bit)
        if i in works:
            result, token = works[i](total)
            results.append(result)
            received = received + token[:1, :]
        total = total + received
    return [total, exchange(total, "gy", 1)], results


def relay_part(rows_right, points, token):
    steps = 4
    rows, width = rows_right.shape
    chunk = rows // steps
    vmem = pl.BlockSpec(memory_space=pltpu.VMEM)
    high, low, token = pl.pallas_call(
        functools.partial(relay_kernel, points),
        in_specs=[pl.BlockSpec(memory_space=pl.ANY), vmem],
        out_specs=[vmem] * 3,
        out_shape=[shape(points, rows // points, width, dtype=BF16)] * 2 + [TOKEN],
        scratch_shapes=[
            pltpu.VMEM((width // LANES, steps, chunk, LANES), F32),
            pltpu.SemaphoreType.DMA((width // LANES, steps)),
        ],
        compiler_params=params(limit=47 * 1024 * 1024),
        cost_estimate=cost(8),
        name="relay_right",
    )(rows_right, token)
    return (high, low), token


def left_part(unfold, linv, token):
    steps = 4
    chunk = unfold.shape[0] // steps
    return pl.pallas_call(
        left_kernel,
        grid=(steps,),
        in_specs=[
            pl.BlockSpec((chunk, RK), lambda i: (i, 0)),
            pl.BlockSpec((RK, RK), lambda i: (0, 0)),
            pl.BlockSpec((8, LANES), lambda i: (0, 0)),
        ],
        out_specs=[
            pl.BlockSpec((chunk, RK), lambda i: (i, 0)),
            pl.BlockSpec((8, LANES), lambda i: (0, 0)),
        ],
        out_shape=[shape(unfold.shape[0], RK), TOKEN],
        compiler_params=params(1, 16 * 1024 * 1024),
        cost_estimate=cost(8),
        name="left_out",
    )(unfold, linv, token)


def right_part(absorbed, token):
    points, ranks, width = absorbed.shape
    steps = 2
    return pl.pallas_call(
        functools.partial(right_kernel, points),
        grid=(steps, 2),
        in_specs=[
            pl.BlockSpec((points, ranks // steps, LANES), lambda i, c: (0, i, c)),
            pl.BlockSpec((8, LANES), lambda i, c: (0, 0)),
        ],
        out_specs=[
            pl.BlockSpec((ranks // steps * points, LANES), lambda i, c: (i, c)),
            pl.BlockSpec((8, LANES), lambda i, c: (0, 0)),
        ],
        out_shape=[shape(ranks * points, width), TOKEN],
        compiler_params=params(2, 16 * 1024 * 1024),
        cost_estimate=cost(8),
        name="right_out",
    )(absorbed, token)


def per_device(left_core, right_core):
    rank_left, points, rank_mid = left_core.shape
    rank_right = right_core.shape[2]
    total_points = points * lax.axis_size("gx") * lax.axis_size("gy") * lax.axis_size("gz")
    unfold = left_core.reshape(rank_left * points, rank_mid)
    rows_right = right_core.reshape(rank_mid * points, rank_right)
    vmem = pl.BlockSpec(memory_space=pltpu.VMEM)

    steps = 8
    half = RK
    blocks = pl.pallas_call(
        gram_kernel,
        in_specs=[pl.BlockSpec(memory_space=pl.ANY)],
        out_specs=[vmem] * 2,
        out_shape=[shape(half, LANES)] * 2,
        scratch_shapes=[
            pltpu.VMEM((steps, unfold.shape[0] // steps, rank_mid), F32),
            pltpu.VMEM((rank_mid, 2 * rank_mid), F32),
            pltpu.VMEM((2 * half, LANES), F32),
            pltpu.SemaphoreType.DMA((steps,)),
        ],
        compiler_params=params(limit=53 * 1024 * 1024),
        name="gram_top",
    )(unfold)
    summed, (relayed,) = sum_over_devices(
        blocks,
        {3: functools.partial(relay_part, rows_right, points)},
    )

    half = LANES + 8
    absorbed, linv, *blocks = pl.pallas_call(
        functools.partial(absorb_kernel, math.sqrt(rank_left * total_points)),
        in_specs=[vmem] * 4,
        out_specs=[vmem] * 4,
        out_shape=[shape(points, RK, rank_right), shape(RK, RK)] + [shape(half, LANES)] * 2,
        scratch_shapes=[
            pltpu.VMEM((2 * RK, LANES), F32),
            pltpu.VMEM((2 * half, LANES), F32),
            pltpu.VMEM((LANES, 3 * LANES), F32),
            pltpu.VMEM((rank_right, 2 * rank_right), F32),
        ],
        compiler_params=params(limit=24 * 1024 * 1024),
        name="factor_absorb",
    )(*summed, *relayed)
    summed, (right_out, left_out) = sum_over_devices(
        blocks,
        {
            2: functools.partial(right_part, absorbed),
            3: functools.partial(left_part, unfold, linv),
        },
    )

    factor = pl.pallas_call(
        functools.partial(factor_kernel, 1.0 / (RK * total_points)),
        in_specs=[vmem] * 2,
        out_specs=vmem,
        out_shape=shape(rank_right, rank_right),
        scratch_shapes=[
            pltpu.VMEM((2 * half, LANES), F32),
            pltpu.VMEM((LANES, 2 * LANES), F32),
            pltpu.VMEM((LANES, LANES), F32),
        ],
        compiler_params=params(limit=16 * 1024 * 1024),
        name="factor_next",
    )(*summed)
    return (
        left_out.reshape(rank_left, points, RK),
        right_out.reshape(RK, points, rank_right),
        factor,
    )


def solution(mesh):
    in_specs = (P(None, AXES, None), P(None, AXES, None))
    out_specs = (P(None, AXES, None), P(None, AXES, None), P())
    return jax.shard_map(
        per_device, mesh=mesh, in_specs=in_specs, out_specs=out_specs, check_vma=False
    )
```

```python
import functools
import math

import jax
import jax.numpy as jnp
from jax import lax
from jax.experimental import pallas as pl
from jax.experimental.pallas import tpu as pltpu
from jax.sharding import PartitionSpec as P

RK = 128
AXES = ("gx", "gy", "gz")
LANES = 128
PANEL = 8
PLANE = ("gx", "gy")
SPREAD_ONE = 8
SPREAD_TWO = 2
F32 = jnp.float32
BF16 = jnp.bfloat16
VMEM_LIMIT = 48 * 1024 * 1024


def split(x):
    hi = x.astype(BF16)
    return hi, (x - hi.astype(F32)).astype(BF16)


def dot_tn(a, b):
    return lax.dot_general(a, b, (((0,), (0,)), ((), ())), preferred_element_type=F32)


def dot_nt(a, b):
    return lax.dot_general(a, b, (((1,), (1,)), ((), ())), preferred_element_type=F32)


def dot_nn(a, b):
    return lax.dot_general(a, b, (((1,), (0,)), ((), ())), preferred_element_type=F32)


def stacked_pieces(x):
    one = x.astype(BF16).astype(F32)
    rest = x - one
    two = rest.astype(BF16).astype(F32)
    three = rest - two
    left = jnp.concatenate([one, one, two, two, one, three], axis=0).astype(BF16)
    right = jnp.concatenate([one, two, one, two, three, one], axis=0).astype(BF16)
    return left, right


def spread_row(x, k):
    return jnp.broadcast_to(x[k : k + 1, :], x.shape)


def factor_rows(w_ref, blocks):
    size = w_ref.shape[0]
    row_id = lax.broadcasted_iota(jnp.int32, (PANEL, LANES), 0)
    rows = [
        [w_ref[g : g + PANEL, b * LANES : (b + 1) * LANES] for b in range(blocks)]
        for g in range(0, size, PANEL)
    ]
    for now in range(len(rows)):
        own, lane = divmod(now * PANEL, LANES)
        panel = rows[now]
        columns = [
            jnp.broadcast_to(panel[own][:, lane + k : lane + k + 1], (PANEL, LANES))
            for k in range(PANEL)
        ]
        follows = now + 1 < len(rows)
        if follows:
            block, down = divmod((now + 1) * PANEL, LANES)
            turned = panel[block].T[down : down + PANEL, :]
            ahead = [jnp.broadcast_to(turned[:, k : k + 1], (PANEL, LANES)) for k in range(PANEL)]
        scale = jnp.zeros((PANEL, LANES), F32)
        pivot = spread_row(columns[0], 0)
        for k in range(PANEL):
            inverse = pl.reciprocal(pivot, approx=True)
            scale = jnp.where(row_id == k, lax.rsqrt(pivot), scale)
            multiples = columns[k] * inverse
            if follows:
                ahead_multiples = ahead[k] * inverse
            for m in range(k + 1, PANEL):
                entry = spread_row(columns[k], m)
                if m == k + 1:
                    pivot = spread_row(columns[m], m) - (entry * inverse) * entry
                columns[m] = columns[m] - multiples * entry
                if follows:
                    ahead[m] = ahead[m] - ahead_multiples * entry
            below = jnp.where(row_id > k, multiples, 0.0)
            for b in range(own, blocks):
                source = spread_row(panel[b], k)
                panel[b] = panel[b] - below * source
                if follows:
                    rows[now + 1][b] = rows[now + 1][b] - ahead_multiples * source
        done = [panel[b] * scale for b in range(own, blocks)]
        for b in range(own, blocks):
            w_ref[now * PANEL : (now + 1) * PANEL, b * LANES : (b + 1) * LANES] = done[b - own]
        if now + 2 < len(rows):
            both = [stacked_pieces(x) for x in done]
            left = jnp.concatenate([x[0] for x in both[: size // LANES - own]], axis=1)
            right = jnp.concatenate([x[1] for x in both], axis=1)
            update = dot_tn(left, right)
            for g in range(now + 2, len(rows)):
                top = g * PANEL - own * LANES
                for b in range(g * PANEL // LANES, blocks):
                    across = (b - own) * LANES
                    rows[g][b] = (
                        rows[g][b] - update[top : top + PANEL, across : across + LANES]
                    )


def triangle_ids():
    return (
        lax.broadcasted_iota(jnp.int32, (LANES, LANES), 0),
        lax.broadcasted_iota(jnp.int32, (LANES, LANES), 1),
    )


def store_blocks(tall_ref, outs):
    me = lax.rem(lax.axis_index(PLANE), len(outs))
    size = outs[0].shape[0]
    for d, out in enumerate(outs):
        out[...] = tall_ref[pl.ds(pl.multiple_of((me ^ d) * size, 8), size), :]


def load_blocks(blocks, tall_ref):
    me = lax.rem(lax.axis_index(PLANE), len(blocks))
    size = blocks[0].shape[0]
    for d, block in enumerate(blocks):
        tall_ref[pl.ds(pl.multiple_of((me ^ d) * size, 8), size), :] = block[...]


def chunk_copies(source, held, sems):
    steps, chunk = held.shape[:2]

    def copy(i):
        return pltpu.make_async_copy(
            source.at[pl.ds(i * chunk, chunk), :], held.at[i], sems.at[i]
        )

    for i in range(steps):
        copy(i).start()
    return copy


def gram_kernel(a_hbm, *refs):
    outs = refs[:SPREAD_ONE]
    a_ref, total_ref, tall_ref, sems = refs[SPREAD_ONE:]
    copy = chunk_copies(a_hbm, a_ref, sems)
    total_ref[...] = jnp.zeros_like(total_ref)

    def body(i, carry):
        copy(i).wait()
        hi, lo = split(a_ref[i])
        total_ref[...] += dot_tn(hi, jnp.concatenate([hi, lo], axis=1))
        return carry

    lax.fori_loop(0, a_ref.shape[0], body, 0)
    width = a_ref.shape[2]
    cross = total_ref[:, width : width + RK]
    tall_ref[:RK, :] = total_ref[:RK, :RK] + total_ref[:RK, width : width + RK] + cross[:RK, :].T
    tall_ref[RK:, :] = total_ref[:RK, RK:width] + total_ref[:RK, width + RK :] + cross[RK:, :].T
    store_blocks(tall_ref, outs)


def relay_kernel(points, r_hbm, _, hi_ref, lo_ref, token_ref, r_ref, sems):
    token_ref[...] = jnp.zeros_like(token_ref)
    halves, steps, chunk, _ = r_ref.shape
    ranks = chunk // points

    def copy(c, i):
        return pltpu.make_async_copy(
            r_hbm.at[pl.ds(i * chunk, chunk), pl.ds(c * LANES, LANES)],
            r_ref.at[c, i],
            sems.at[c, i],
        )

    for i in range(steps):
        for c in range(halves):
            copy(c, i).start()

    def body(i, carry):
        for c in range(halves):
            copy(c, i).wait()
            for p in range(points):
                hi, lo = split(r_ref[c, i, pl.ds(p, ranks, stride=points), :])
                place = pl.ds(pl.multiple_of(i * ranks, ranks), ranks)
                hi_ref[p, place, c * LANES : (c + 1) * LANES] = hi
                lo_ref[p, place, c * LANES : (c + 1) * LANES] = lo
        return carry

    lax.fori_loop(0, steps, body, 0)


def absorb_kernel(scale, *refs):
    blocks, refs = refs[:SPREAD_ONE], refs[SPREAD_ONE:]
    hi_ref, lo_ref, absorbed_ref, linv_ref = refs[:4]
    outs = refs[4 : 4 + SPREAD_TWO]
    tall_ref, pack_ref, w_ref, total_ref = refs[4 + SPREAD_TWO :]
    row, col = triangle_ids()
    load_blocks(blocks, tall_ref)
    w_ref[:, :LANES] = tall_ref[:RK, :]
    w_ref[:, LANES : 2 * LANES] = tall_ref[RK:, :]
    w_ref[:, 2 * LANES :] = jnp.where(row == col, 1.0, 0.0).astype(F32)
    factor_rows(w_ref, 3)
    linv_ref[...] = w_ref[:, 2 * LANES :] * scale
    upper = jnp.concatenate(
        [jnp.where(col >= row, w_ref[:, :LANES], 0.0), w_ref[:, LANES : 2 * LANES]], axis=1
    )
    upper_hi, upper_lo = split(upper)
    upper_both = jnp.concatenate([upper_hi, upper_lo], axis=0)
    points = absorbed_ref.shape[0]
    group = 4
    total_ref[...] = jnp.zeros_like(total_ref)

    def body(step, carry):
        pieces = []
        for i in range(group):
            p = step * group + i
            first = dot_nn(upper_both, hi_ref[p])
            b = first[:RK, :] + first[RK:, :] + dot_nn(upper_hi, lo_ref[p])
            absorbed_ref[p] = b
            pieces.append(split(b))
        b_hi = jnp.concatenate([x[0] for x in pieces], axis=0)
        b_lo = jnp.concatenate([x[1] for x in pieces], axis=0)
        total_ref[...] += dot_tn(b_hi, jnp.concatenate([b_hi, b_lo], axis=1))
        return carry

    lax.fori_loop(0, points // group, body, 0)
    cross = total_ref[:, 256:]
    gram = total_ref[:, :256] + cross + cross.T
    lower_right = gram[LANES:, LANES:]
    pack_ref[:LANES, :] = jnp.where(col >= row, gram[:LANES, :LANES], lower_right)
    pack_ref[LANES : 2 * LANES, :] = gram[:LANES, LANES:]
    diagonal = jnp.sum(jnp.where(row == col, lower_right, 0.0), axis=0, keepdims=True)
    tail = pack_ref.shape[0] - 2 * LANES
    pack_ref[2 * LANES :, :] = jnp.broadcast_to(diagonal, (tail, LANES))
    store_blocks(pack_ref, outs)


def left_kernel(a_ref, linv_ref, _, left_ref, token_ref):
    l_hi, l_lo = split(linv_ref[...])
    hi, lo = split(a_ref[...])
    left_ref[...] = dot_nt(hi, l_hi) + dot_nt(hi, l_lo) + dot_nt(lo, l_hi)
    token_ref[...] = jnp.zeros_like(token_ref)


def right_kernel(points, absorbed_ref, _, right_ref, token_ref):
    count = absorbed_ref.shape[1]
    for p in range(points):
        right_ref[pl.ds(p, count, stride=points), :] = absorbed_ref[p]
    token_ref[...] = jnp.zeros_like(token_ref)


def factor_kernel(scale, *refs):
    blocks, (out_ref, pack_ref, w_ref) = refs[:SPREAD_TWO], refs[SPREAD_TWO:]
    load_blocks(blocks, pack_ref)
    row, col = triangle_ids()
    packed = pack_ref[:LANES, :] * scale
    turned = packed.T
    diagonal = jnp.broadcast_to(pack_ref[2 * LANES : 2 * LANES + 1, :], (LANES, LANES)) * scale
    w_ref[:LANES, :LANES] = jnp.where(col >= row, packed, turned)
    w_ref[:LANES, LANES:] = pack_ref[LANES : 2 * LANES, :] * scale
    w_ref[LANES:, :LANES] = jnp.zeros((LANES, LANES), F32)
    w_ref[LANES:, LANES:] = jnp.where(row > col, packed, jnp.where(row == col, diagonal, turned))
    factor_rows(w_ref, 2)
    out_ref[:LANES, :LANES] = jnp.where(col >= row, w_ref[:LANES, :LANES], 0.0)
    out_ref[:LANES, LANES:] = w_ref[:LANES, LANES:]
    out_ref[LANES:, :LANES] = jnp.zeros((LANES, LANES), F32)
    out_ref[LANES:, LANES:] = jnp.where(col >= row, w_ref[LANES:, LANES:], 0.0)


def shape(*dims, dtype=F32):
    return jax.ShapeDtypeStruct(dims, dtype)


TOKEN = shape(8, LANES)


def params(steps=0, limit=VMEM_LIMIT):
    return pltpu.CompilerParams(
        dimension_semantics=("arbitrary",) * steps or None, vmem_limit_bytes=limit
    )


def cost(mebibytes):
    return pl.CostEstimate(flops=0, bytes_accessed=mebibytes * 2**20, transcendentals=0)


def swap(value, axes, mask):
    axes = axes if isinstance(axes, tuple) else (axes,)
    size = math.prod(lax.axis_size(a) for a in axes)
    return lax.ppermute(value, axes, [(i, i ^ mask) for i in range(size)])


def beside(received, work, start):
    result, token = work(start)
    return received + token[:1, :], result


def four_sum(total, axes, one, two, work):
    first = swap(total, axes, one)
    second = swap(total, axes, two)
    third = swap(total, axes, one ^ two)
    third, result = beside(third, work, total)
    return (total + first) + (second + third), result


def rest_sum(total, pairs):
    for axes, mask in pairs:
        total = total + swap(total, axes, mask)
    return total


def bits(axis, first):
    return [1 << i for i in range(first, lax.axis_size(axis).bit_length() - 1)]


def sum_over_devices(blocks, works):
    n = len(blocks)
    total = blocks[0]
    for d in range(1, n):
        total = total + swap(blocks[d], PLANE, d)
    far = [("gx", m) for m in bits("gx", 1)]
    if n == 8:
        total, *results = four_sum(total, "gz", 1, 2, works[0])
    else:
        total, first = four_sum(total, PLANE, 2, 4, works[0])
        total = rest_sum(total, [("gz", 1)])
        received, second = beside(swap(total, "gz", 2), works[1], total)
        total = total + received
        results = [first, second]
    total = rest_sum(total, far + [("gz", m) for m in bits("gz", 2)])
    return [total] + [swap(total, PLANE, d) for d in range(1, n)], results


def relay_part(rows_right, points, token):
    steps = 4
    rows, width = rows_right.shape
    chunk = rows // steps
    vmem = pl.BlockSpec(memory_space=pltpu.VMEM)
    high, low, token = pl.pallas_call(
        functools.partial(relay_kernel, points),
        in_specs=[pl.BlockSpec(memory_space=pl.ANY), vmem],
        out_specs=[vmem] * 3,
        out_shape=[shape(points, rows // points, width, dtype=BF16)] * 2 + [TOKEN],
        scratch_shapes=[
            pltpu.VMEM((width // LANES, steps, chunk, LANES), F32),
            pltpu.SemaphoreType.DMA((width // LANES, steps)),
        ],
        compiler_params=params(limit=47 * 1024 * 1024),
        cost_estimate=cost(8),
        name="relay_right",
    )(rows_right, token)
    return (high, low), token


def left_part(unfold, linv, token):
    steps = 4
    chunk = unfold.shape[0] // steps
    return pl.pallas_call(
        left_kernel,
        grid=(steps,),
        in_specs=[
            pl.BlockSpec((chunk, RK), lambda i: (i, 0)),
            pl.BlockSpec((RK, RK), lambda i: (0, 0)),
            pl.BlockSpec((8, LANES), lambda i: (0, 0)),
        ],
        out_specs=[
            pl.BlockSpec((chunk, RK), lambda i: (i, 0)),
            pl.BlockSpec((8, LANES), lambda i: (0, 0)),
        ],
        out_shape=[shape(unfold.shape[0], RK), TOKEN],
        compiler_params=params(1, 16 * 1024 * 1024),
        cost_estimate=cost(8),
        name="left_out",
    )(unfold, linv, token)


def right_part(absorbed, token):
    points, ranks, width = absorbed.shape
    steps = 2
    return pl.pallas_call(
        functools.partial(right_kernel, points),
        grid=(steps, 2),
        in_specs=[
            pl.BlockSpec((points, ranks // steps, LANES), lambda i, c: (0, i, c)),
            pl.BlockSpec((8, LANES), lambda i, c: (0, 0)),
        ],
        out_specs=[
            pl.BlockSpec((ranks // steps * points, LANES), lambda i, c: (i, c)),
            pl.BlockSpec((8, LANES), lambda i, c: (0, 0)),
        ],
        out_shape=[shape(ranks * points, width), TOKEN],
        compiler_params=params(2, 16 * 1024 * 1024),
        cost_estimate=cost(8),
        name="right_out",
    )(absorbed, token)


def per_device(left_core, right_core):
    rank_left, points, rank_mid = left_core.shape
    rank_right = right_core.shape[2]
    total_points = points * lax.axis_size("gx") * lax.axis_size("gy") * lax.axis_size("gz")
    unfold = left_core.reshape(rank_left * points, rank_mid)
    rows_right = right_core.reshape(rank_mid * points, rank_right)
    vmem = pl.BlockSpec(memory_space=pltpu.VMEM)

    steps = 8
    block_rows = 2 * RK // SPREAD_ONE
    blocks = pl.pallas_call(
        gram_kernel,
        in_specs=[pl.BlockSpec(memory_space=pl.ANY)],
        out_specs=[vmem] * SPREAD_ONE,
        out_shape=[shape(block_rows, LANES)] * SPREAD_ONE,
        scratch_shapes=[
            pltpu.VMEM((steps, unfold.shape[0] // steps, rank_mid), F32),
            pltpu.VMEM((rank_mid, 2 * rank_mid), F32),
            pltpu.VMEM((2 * RK, LANES), F32),
            pltpu.SemaphoreType.DMA((steps,)),
        ],
        compiler_params=params(limit=53 * 1024 * 1024),
        name="gram_top",
    )(unfold)
    summed, (relayed,) = sum_over_devices(
        blocks,
        [functools.partial(relay_part, rows_right, points)],
    )

    block_rows = LANES + 8
    packed_rows = SPREAD_TWO * block_rows
    absorbed, linv, *blocks = pl.pallas_call(
        functools.partial(absorb_kernel, math.sqrt(rank_left * total_points)),
        in_specs=[vmem] * (SPREAD_ONE + 2),
        out_specs=[vmem] * (2 + SPREAD_TWO),
        out_shape=[shape(points, RK, rank_right), shape(RK, RK)] + [shape(block_rows, LANES)] * SPREAD_TWO,
        scratch_shapes=[
            pltpu.VMEM((2 * RK, LANES), F32),
            pltpu.VMEM((packed_rows, LANES), F32),
            pltpu.VMEM((LANES, 3 * LANES), F32),
            pltpu.VMEM((rank_right, 2 * rank_right), F32),
        ],
        compiler_params=params(limit=24 * 1024 * 1024),
        name="factor_absorb",
    )(*summed, *relayed)
    summed, (right_out, left_out) = sum_over_devices(
        blocks,
        [
            functools.partial(right_part, absorbed),
            functools.partial(left_part, unfold, linv),
        ],
    )

    factor = pl.pallas_call(
        functools.partial(factor_kernel, 1.0 / (RK * total_points)),
        in_specs=[vmem] * SPREAD_TWO,
        out_specs=vmem,
        out_shape=shape(rank_right, rank_right),
        scratch_shapes=[
            pltpu.VMEM((packed_rows, LANES), F32),
            pltpu.VMEM((2 * LANES, 2 * LANES), F32),
        ],
        compiler_params=params(limit=16 * 1024 * 1024),
        name="factor_next",
    )(*summed)
    return (
        left_out.reshape(rank_left, points, RK),
        right_out.reshape(RK, points, rank_right),
        factor,
    )


def solution(mesh):
    in_specs = (P(None, AXES, None), P(None, AXES, None))
    out_specs = (P(None, AXES, None), P(None, AXES, None), P())
    return jax.shard_map(
        per_device, mesh=mesh, in_specs=in_specs, out_specs=out_specs, check_vma=False
    )
```

```python
import functools
import math

import jax
import jax.numpy as jnp
from jax import lax
from jax.experimental import pallas as pl
from jax.experimental.pallas import tpu as pltpu
from jax.sharding import PartitionSpec as P

RK = 128
AXES = ("gx", "gy", "gz")
LANES = 128
PANEL = 16
PLANE = ("gx", "gy")
SPREAD_ONE = 2
SPREAD_TWO = 2
F32 = jnp.float32
BF16 = jnp.bfloat16
VMEM_LIMIT = 48 * 1024 * 1024


def split(x):
    hi = x.astype(BF16)
    return hi, (x - hi.astype(F32)).astype(BF16)


def dot_tn(a, b):
    return lax.dot_general(a, b, (((0,), (0,)), ((), ())), preferred_element_type=F32)


def dot_nt(a, b):
    return lax.dot_general(a, b, (((1,), (1,)), ((), ())), preferred_element_type=F32)


def dot_nn(a, b):
    return lax.dot_general(a, b, (((1,), (0,)), ((), ())), preferred_element_type=F32)


def stacked_pieces(x):
    one = x.astype(BF16).astype(F32)
    rest = x - one
    two = rest.astype(BF16).astype(F32)
    three = rest - two
    left = jnp.concatenate([one, one, two, two, one, three], axis=0).astype(BF16)
    right = jnp.concatenate([one, two, one, two, three, one], axis=0).astype(BF16)
    return left, right


def spread_row(x, k):
    return jnp.broadcast_to(x[k : k + 1, :], x.shape)


def factor_rows(w_ref, blocks):
    size = w_ref.shape[0]
    row_id = lax.broadcasted_iota(jnp.int32, (PANEL, LANES), 0)
    rows = [
        [w_ref[g : g + PANEL, b * LANES : (b + 1) * LANES] for b in range(blocks)]
        for g in range(0, size, PANEL)
    ]
    for now in range(len(rows)):
        own, lane = divmod(now * PANEL, LANES)
        panel = rows[now]
        columns = [
            jnp.broadcast_to(panel[own][:, lane + k : lane + k + 1], (PANEL, LANES))
            for k in range(PANEL)
        ]
        follows = now + 1 < len(rows)
        if follows:
            block, down = divmod((now + 1) * PANEL, LANES)
            turned = panel[block].T[down : down + PANEL, :]
            ahead = [jnp.broadcast_to(turned[:, k : k + 1], (PANEL, LANES)) for k in range(PANEL)]
        scale = jnp.zeros((PANEL, LANES), F32)
        pivot = spread_row(columns[0], 0)
        for k in range(PANEL):
            inverse = pl.reciprocal(pivot, approx=True)
            scale = jnp.where(row_id == k, lax.rsqrt(pivot), scale)
            multiples = columns[k] * inverse
            if follows:
                ahead_multiples = ahead[k] * inverse
            for m in range(k + 1, PANEL):
                entry = spread_row(columns[k], m)
                if m == k + 1:
                    pivot = spread_row(columns[m], m) - (entry * inverse) * entry
                columns[m] = columns[m] - multiples * entry
                if follows:
                    ahead[m] = ahead[m] - ahead_multiples * entry
            below = jnp.where(row_id > k, multiples, 0.0)
            for b in range(own, blocks):
                source = spread_row(panel[b], k)
                panel[b] = panel[b] - below * source
                if follows:
                    rows[now + 1][b] = rows[now + 1][b] - ahead_multiples * source
        done = [panel[b] * scale for b in range(own, blocks)]
        for b in range(own, blocks):
            w_ref[now * PANEL : (now + 1) * PANEL, b * LANES : (b + 1) * LANES] = done[b - own]
        if now + 2 < len(rows):
            both = [stacked_pieces(x) for x in done]
            left = jnp.concatenate([x[0] for x in both[: size // LANES - own]], axis=1)
            right = jnp.concatenate([x[1] for x in both], axis=1)
            update = dot_tn(left, right)
            for g in range(now + 2, len(rows)):
                top = g * PANEL - own * LANES
                for b in range(g * PANEL // LANES, blocks):
                    across = (b - own) * LANES
                    rows[g][b] = (
                        rows[g][b] - update[top : top + PANEL, across : across + LANES]
                    )


def triangle_ids():
    return (
        lax.broadcasted_iota(jnp.int32, (LANES, LANES), 0),
        lax.broadcasted_iota(jnp.int32, (LANES, LANES), 1),
    )


def store_blocks(tall_ref, outs):
    me = lax.rem(lax.axis_index(PLANE), len(outs))
    size = outs[0].shape[0]
    for d, out in enumerate(outs):
        out[...] = tall_ref[pl.ds(pl.multiple_of((me ^ d) * size, 8), size), :]


def load_blocks(blocks, tall_ref):
    me = lax.rem(lax.axis_index(PLANE), len(blocks))
    size = blocks[0].shape[0]
    for d, block in enumerate(blocks):
        tall_ref[pl.ds(pl.multiple_of((me ^ d) * size, 8), size), :] = block[...]


def chunk_copies(source, held, sems):
    steps, chunk = held.shape[:2]

    def copy(i):
        return pltpu.make_async_copy(
            source.at[pl.ds(i * chunk, chunk), :], held.at[i], sems.at[i]
        )

    for i in range(steps):
        copy(i).start()
    return copy


def gram_kernel(a_hbm, *refs):
    outs = refs[:SPREAD_ONE]
    a_ref, total_ref, tall_ref, sems = refs[SPREAD_ONE:]
    copy = chunk_copies(a_hbm, a_ref, sems)
    total_ref[...] = jnp.zeros_like(total_ref)

    def body(i, carry):
        copy(i).wait()
        hi, lo = split(a_ref[i])
        total_ref[...] += dot_tn(hi, jnp.concatenate([hi, lo], axis=1))
        return carry

    lax.fori_loop(0, a_ref.shape[0], body, 0)
    width = a_ref.shape[2]
    cross = total_ref[:, width : width + RK]
    tall_ref[:RK, :] = total_ref[:RK, :RK] + total_ref[:RK, width : width + RK] + cross[:RK, :].T
    tall_ref[RK:, :] = total_ref[:RK, RK:width] + total_ref[:RK, width + RK :] + cross[RK:, :].T
    store_blocks(tall_ref, outs)


def relay_kernel(points, r_hbm, _, hi_ref, lo_ref, token_ref, r_ref, sems):
    token_ref[...] = jnp.zeros_like(token_ref)
    halves, steps, chunk, _ = r_ref.shape
    ranks = chunk // points

    def copy(c, i):
        return pltpu.make_async_copy(
            r_hbm.at[pl.ds(i * chunk, chunk), pl.ds(c * LANES, LANES)],
            r_ref.at[c, i],
            sems.at[c, i],
        )

    for i in range(steps):
        for c in range(halves):
            copy(c, i).start()

    def body(i, carry):
        for c in range(halves):
            copy(c, i).wait()
            for p in range(points):
                hi, lo = split(r_ref[c, i, pl.ds(p, ranks, stride=points), :])
                place = pl.ds(pl.multiple_of(i * ranks, ranks), ranks)
                hi_ref[p, place, c * LANES : (c + 1) * LANES] = hi
                lo_ref[p, place, c * LANES : (c + 1) * LANES] = lo
        return carry

    lax.fori_loop(0, steps, body, 0)


def absorb_kernel(scale, *refs):
    blocks, refs = refs[:SPREAD_ONE], refs[SPREAD_ONE:]
    hi_ref, lo_ref, absorbed_ref, linv_ref = refs[:4]
    outs = refs[4 : 4 + SPREAD_TWO]
    tall_ref, pack_ref, w_ref, total_ref = refs[4 + SPREAD_TWO :]
    row, col = triangle_ids()
    load_blocks(blocks, tall_ref)
    w_ref[:, :LANES] = tall_ref[:RK, :]
    w_ref[:, LANES : 2 * LANES] = tall_ref[RK:, :]
    w_ref[:, 2 * LANES :] = jnp.where(row == col, 1.0, 0.0).astype(F32)
    factor_rows(w_ref, 3)
    linv_ref[...] = w_ref[:, 2 * LANES :] * scale
    upper = jnp.concatenate(
        [jnp.where(col >= row, w_ref[:, :LANES], 0.0), w_ref[:, LANES : 2 * LANES]], axis=1
    )
    upper_hi, upper_lo = split(upper)
    upper_both = jnp.concatenate([upper_hi, upper_lo], axis=0)
    points = absorbed_ref.shape[0]
    group = 4
    total_ref[...] = jnp.zeros_like(total_ref)

    def body(step, carry):
        pieces = []
        for i in range(group):
            p = step * group + i
            first = dot_nn(upper_both, hi_ref[p])
            b = first[:RK, :] + first[RK:, :] + dot_nn(upper_hi, lo_ref[p])
            absorbed_ref[p] = b
            pieces.append(split(b))
        b_hi = jnp.concatenate([x[0] for x in pieces], axis=0)
        b_lo = jnp.concatenate([x[1] for x in pieces], axis=0)
        total_ref[...] += dot_tn(b_hi, jnp.concatenate([b_hi, b_lo], axis=1))
        return carry

    lax.fori_loop(0, points // group, body, 0)
    cross = total_ref[:, 256:]
    gram = total_ref[:, :256] + cross + cross.T
    lower_right = gram[LANES:, LANES:]
    pack_ref[:LANES, :] = jnp.where(col >= row, gram[:LANES, :LANES], lower_right)
    pack_ref[LANES : 2 * LANES, :] = gram[:LANES, LANES:]
    diagonal = jnp.sum(jnp.where(row == col, lower_right, 0.0), axis=0, keepdims=True)
    tail = pack_ref.shape[0] - 2 * LANES
    pack_ref[2 * LANES :, :] = jnp.broadcast_to(diagonal, (tail, LANES))
    store_blocks(pack_ref, outs)


def left_kernel(a_ref, linv_ref, _, left_ref, token_ref):
    l_hi, l_lo = split(linv_ref[...])
    hi, lo = split(a_ref[...])
    left_ref[...] = dot_nt(hi, l_hi) + dot_nt(hi, l_lo) + dot_nt(lo, l_hi)
    token_ref[...] = jnp.zeros_like(token_ref)


def right_kernel(points, absorbed_ref, _, right_ref, token_ref):
    count = absorbed_ref.shape[1]
    for p in range(points):
        right_ref[pl.ds(p, count, stride=points), :] = absorbed_ref[p]
    token_ref[...] = jnp.zeros_like(token_ref)


def factor_kernel(scale, *refs):
    blocks, (out_ref, pack_ref, w_ref) = refs[:SPREAD_TWO], refs[SPREAD_TWO:]
    load_blocks(blocks, pack_ref)
    row, col = triangle_ids()
    packed = pack_ref[:LANES, :] * scale
    turned = packed.T
    diagonal = jnp.broadcast_to(pack_ref[2 * LANES : 2 * LANES + 1, :], (LANES, LANES)) * scale
    w_ref[:LANES, :LANES] = jnp.where(col >= row, packed, turned)
    w_ref[:LANES, LANES:] = pack_ref[LANES : 2 * LANES, :] * scale
    w_ref[LANES:, :LANES] = jnp.zeros((LANES, LANES), F32)
    w_ref[LANES:, LANES:] = jnp.where(row > col, packed, jnp.where(row == col, diagonal, turned))
    factor_rows(w_ref, 2)
    out_ref[:LANES, :LANES] = jnp.where(col >= row, w_ref[:LANES, :LANES], 0.0)
    out_ref[:LANES, LANES:] = w_ref[:LANES, LANES:]
    out_ref[LANES:, :LANES] = jnp.zeros((LANES, LANES), F32)
    out_ref[LANES:, LANES:] = jnp.where(col >= row, w_ref[LANES:, LANES:], 0.0)


def shape(*dims, dtype=F32):
    return jax.ShapeDtypeStruct(dims, dtype)


TOKEN = shape(8, LANES)


def params(steps=0, limit=VMEM_LIMIT):
    return pltpu.CompilerParams(
        dimension_semantics=("arbitrary",) * steps or None, vmem_limit_bytes=limit
    )


def cost(mebibytes):
    return pl.CostEstimate(flops=0, bytes_accessed=mebibytes * 2**20, transcendentals=0)


def swap(value, axes, mask):
    axes = axes if isinstance(axes, tuple) else (axes,)
    size = math.prod(lax.axis_size(a) for a in axes)
    return lax.ppermute(value, axes, [(i, i ^ mask) for i in range(size)])


def four_sum(total, axes, one, two, work):
    first = swap(total, axes, one)
    second = swap(total, axes, two)
    third = swap(total, axes, one ^ two)
    result = None
    if work is not None:
        result, token = work(total)
        third = third + token[:1, :]
    return (total + first) + (second + third), result


def rest_sum(total, pairs):
    for axes, mask in pairs:
        total = total + swap(total, axes, mask)
    return total


def bits(axis, first):
    return [1 << i for i in range(first, lax.axis_size(axis).bit_length() - 1)]


def sum_over_devices(blocks, works):
    n = len(blocks)
    total = blocks[0]
    for d in range(1, n):
        total = total + swap(blocks[d], PLANE, d)
    far = [("gx", m) for m in bits("gx", 1)] + [("gz", m) for m in bits("gz", 2)]
    total, first = four_sum(total, PLANE, 2, 4, works[0])
    total, second = four_sum(total, "gz", 1, 2, works[1])
    total = rest_sum(total, far)
    return [total] + [swap(total, PLANE, d) for d in range(1, n)], (first, second)


def relay_part(rows_right, points, token):
    steps = 4
    rows, width = rows_right.shape
    chunk = rows // steps
    vmem = pl.BlockSpec(memory_space=pltpu.VMEM)
    high, low, token = pl.pallas_call(
        functools.partial(relay_kernel, points),
        in_specs=[pl.BlockSpec(memory_space=pl.ANY), vmem],
        out_specs=[vmem] * 3,
        out_shape=[shape(points, rows // points, width, dtype=BF16)] * 2 + [TOKEN],
        scratch_shapes=[
            pltpu.VMEM((width // LANES, steps, chunk, LANES), F32),
            pltpu.SemaphoreType.DMA((width // LANES, steps)),
        ],
        compiler_params=params(limit=47 * 1024 * 1024),
        cost_estimate=cost(8),
        name="relay_right",
    )(rows_right, token)
    return (high, low), token


def left_part(unfold, linv, token):
    steps = 4
    chunk = unfold.shape[0] // steps
    return pl.pallas_call(
        left_kernel,
        grid=(steps,),
        in_specs=[
            pl.BlockSpec((chunk, RK), lambda i: (i, 0)),
            pl.BlockSpec((RK, RK), lambda i: (0, 0)),
            pl.BlockSpec((8, LANES), lambda i: (0, 0)),
        ],
        out_specs=[
            pl.BlockSpec((chunk, RK), lambda i: (i, 0)),
            pl.BlockSpec((8, LANES), lambda i: (0, 0)),
        ],
        out_shape=[shape(unfold.shape[0], RK), TOKEN],
        compiler_params=params(1, 16 * 1024 * 1024),
        cost_estimate=cost(8),
        name="left_out",
    )(unfold, linv, token)


def right_part(absorbed, token):
    points, ranks, width = absorbed.shape
    steps = 2
    return pl.pallas_call(
        functools.partial(right_kernel, points),
        grid=(steps, 2),
        in_specs=[
            pl.BlockSpec((points, ranks // steps, LANES), lambda i, c: (0, i, c)),
            pl.BlockSpec((8, LANES), lambda i, c: (0, 0)),
        ],
        out_specs=[
            pl.BlockSpec((ranks // steps * points, LANES), lambda i, c: (i, c)),
            pl.BlockSpec((8, LANES), lambda i, c: (0, 0)),
        ],
        out_shape=[shape(ranks * points, width), TOKEN],
        compiler_params=params(2, 16 * 1024 * 1024),
        cost_estimate=cost(8),
        name="right_out",
    )(absorbed, token)


def per_device(left_core, right_core):
    rank_left, points, rank_mid = left_core.shape
    rank_right = right_core.shape[2]
    total_points = points * lax.axis_size("gx") * lax.axis_size("gy") * lax.axis_size("gz")
    unfold = left_core.reshape(rank_left * points, rank_mid)
    rows_right = right_core.reshape(rank_mid * points, rank_right)
    vmem = pl.BlockSpec(memory_space=pltpu.VMEM)

    steps = 8
    block_rows = 2 * RK // SPREAD_ONE
    blocks = pl.pallas_call(
        gram_kernel,
        in_specs=[pl.BlockSpec(memory_space=pl.ANY)],
        out_specs=[vmem] * SPREAD_ONE,
        out_shape=[shape(block_rows, LANES)] * SPREAD_ONE,
        scratch_shapes=[
            pltpu.VMEM((steps, unfold.shape[0] // steps, rank_mid), F32),
            pltpu.VMEM((rank_mid, 2 * rank_mid), F32),
            pltpu.VMEM((2 * RK, LANES), F32),
            pltpu.SemaphoreType.DMA((steps,)),
        ],
        compiler_params=params(limit=53 * 1024 * 1024),
        name="gram_top",
    )(unfold)
    summed, (_, relayed) = sum_over_devices(
        blocks,
        [None, functools.partial(relay_part, rows_right, points)],
    )

    block_rows = LANES + 8
    packed_rows = SPREAD_TWO * block_rows
    absorbed, linv, *blocks = pl.pallas_call(
        functools.partial(absorb_kernel, math.sqrt(rank_left * total_points)),
        in_specs=[vmem] * (SPREAD_ONE + 2),
        out_specs=[vmem] * (2 + SPREAD_TWO),
        out_shape=[shape(points, RK, rank_right), shape(RK, RK)] + [shape(block_rows, LANES)] * SPREAD_TWO,
        scratch_shapes=[
            pltpu.VMEM((2 * RK, LANES), F32),
            pltpu.VMEM((packed_rows, LANES), F32),
            pltpu.VMEM((LANES, 3 * LANES), F32),
            pltpu.VMEM((rank_right, 2 * rank_right), F32),
        ],
        compiler_params=params(limit=24 * 1024 * 1024),
        name="factor_absorb",
    )(*summed, *relayed)
    summed, (right_out, left_out) = sum_over_devices(
        blocks,
        [
            functools.partial(right_part, absorbed),
            functools.partial(left_part, unfold, linv),
        ],
    )

    factor = pl.pallas_call(
        functools.partial(factor_kernel, 1.0 / (RK * total_points)),
        in_specs=[vmem] * SPREAD_TWO,
        out_specs=vmem,
        out_shape=shape(rank_right, rank_right),
        scratch_shapes=[
            pltpu.VMEM((packed_rows, LANES), F32),
            pltpu.VMEM((2 * LANES, 2 * LANES), F32),
        ],
        compiler_params=params(limit=16 * 1024 * 1024),
        name="factor_next",
    )(*summed)
    return (
        left_out.reshape(rank_left, points, RK),
        right_out.reshape(RK, points, rank_right),
        factor,
    )


def solution(mesh):
    in_specs = (P(None, AXES, None), P(None, AXES, None))
    out_specs = (P(None, AXES, None), P(None, AXES, None), P())
    return jax.shard_map(
        per_device, mesh=mesh, in_specs=in_specs, out_specs=out_specs, check_vma=False
    )
```

```python
import functools
import math

import jax
import jax.numpy as jnp
from jax import lax
from jax.experimental import pallas as pl
from jax.experimental.pallas import tpu as pltpu
from jax.sharding import PartitionSpec as P

RK = 128
AXES = ("gx", "gy", "gz")
LANES = 128
PANEL = 16
PLANE = ("gx", "gy")
SPREAD_ONE = 2
SPREAD_TWO = 2
F32 = jnp.float32
BF16 = jnp.bfloat16
VMEM_LIMIT = 48 * 1024 * 1024


def split(x):
    hi = x.astype(BF16)
    return hi, (x - hi.astype(F32)).astype(BF16)


def dot_tn(a, b):
    return lax.dot_general(a, b, (((0,), (0,)), ((), ())), preferred_element_type=F32)


def dot_nt(a, b):
    return lax.dot_general(a, b, (((1,), (1,)), ((), ())), preferred_element_type=F32)


def dot_nn(a, b):
    return lax.dot_general(a, b, (((1,), (0,)), ((), ())), preferred_element_type=F32)


def stacked_pieces(x):
    one = x.astype(BF16).astype(F32)
    rest = x - one
    two = rest.astype(BF16).astype(F32)
    three = rest - two
    left = jnp.concatenate([one, one, two, two, one, three], axis=0).astype(BF16)
    right = jnp.concatenate([one, two, one, two, three, one], axis=0).astype(BF16)
    return left, right


def spread_row(x, k):
    return jnp.broadcast_to(x[k : k + 1, :], x.shape)


def factor_rows(w_ref, blocks):
    size = w_ref.shape[0]
    row_id = lax.broadcasted_iota(jnp.int32, (PANEL, LANES), 0)
    rows = [
        [w_ref[g : g + PANEL, b * LANES : (b + 1) * LANES] for b in range(blocks)]
        for g in range(0, size, PANEL)
    ]
    for now in range(len(rows)):
        own, lane = divmod(now * PANEL, LANES)
        panel = rows[now]
        columns = [
            jnp.broadcast_to(panel[own][:, lane + k : lane + k + 1], (PANEL, LANES))
            for k in range(PANEL)
        ]
        follows = now + 1 < len(rows)
        if follows:
            block, down = divmod((now + 1) * PANEL, LANES)
            turned = panel[block].T[down : down + PANEL, :]
            ahead = [jnp.broadcast_to(turned[:, k : k + 1], (PANEL, LANES)) for k in range(PANEL)]
        scale = jnp.zeros((PANEL, LANES), F32)
        pivot = spread_row(columns[0], 0)
        for k in range(PANEL):
            inverse = pl.reciprocal(pivot, approx=True)
            scale = jnp.where(row_id == k, lax.rsqrt(pivot), scale)
            multiples = columns[k] * inverse
            if follows:
                ahead_multiples = ahead[k] * inverse
            for m in range(k + 1, PANEL):
                entry = spread_row(columns[k], m)
                if m == k + 1:
                    pivot = spread_row(columns[m], m) - (entry * inverse) * entry
                columns[m] = columns[m] - multiples * entry
                if follows:
                    ahead[m] = ahead[m] - ahead_multiples * entry
            below = jnp.where(row_id > k, multiples, 0.0)
            for b in range(own, blocks):
                source = spread_row(panel[b], k)
                panel[b] = panel[b] - below * source
                if follows:
                    rows[now + 1][b] = rows[now + 1][b] - ahead_multiples * source
        done = [panel[b] * scale for b in range(own, blocks)]
        for b in range(own, blocks):
            w_ref[now * PANEL : (now + 1) * PANEL, b * LANES : (b + 1) * LANES] = done[b - own]
        if now + 2 < len(rows):
            both = [stacked_pieces(x) for x in done]
            left = jnp.concatenate([x[0] for x in both[: size // LANES - own]], axis=1)
            right = jnp.concatenate([x[1] for x in both], axis=1)
            update = dot_tn(left, right)
            for g in range(now + 2, len(rows)):
                top = g * PANEL - own * LANES
                for b in range(g * PANEL // LANES, blocks):
                    across = (b - own) * LANES
                    rows[g][b] = (
                        rows[g][b] - update[top : top + PANEL, across : across + LANES]
                    )


def triangle_ids():
    return (
        lax.broadcasted_iota(jnp.int32, (LANES, LANES), 0),
        lax.broadcasted_iota(jnp.int32, (LANES, LANES), 1),
    )


def store_blocks(tall_ref, outs):
    me = lax.rem(lax.axis_index(PLANE), len(outs))
    size = outs[0].shape[0]
    for d, out in enumerate(outs):
        out[...] = tall_ref[pl.ds(pl.multiple_of((me ^ d) * size, 8), size), :]


def load_blocks(blocks, tall_ref):
    me = lax.rem(lax.axis_index(PLANE), len(blocks))
    size = blocks[0].shape[0]
    for d, block in enumerate(blocks):
        tall_ref[pl.ds(pl.multiple_of((me ^ d) * size, 8), size), :] = block[...]


def chunk_copies(source, held, sems):
    steps, chunk = held.shape[:2]

    def copy(i):
        return pltpu.make_async_copy(
            source.at[pl.ds(i * chunk, chunk), :], held.at[i], sems.at[i]
        )

    for i in range(steps):
        copy(i).start()
    return copy


def gram_kernel(a_hbm, *refs):
    outs = refs[:SPREAD_ONE]
    a_ref, total_ref, tall_ref, sems = refs[SPREAD_ONE:]
    copy = chunk_copies(a_hbm, a_ref, sems)
    total_ref[...] = jnp.zeros_like(total_ref)

    def body(i, carry):
        copy(i).wait()
        hi, lo = split(a_ref[i])
        total_ref[...] += dot_tn(hi, jnp.concatenate([hi, lo], axis=1))
        return carry

    lax.fori_loop(0, a_ref.shape[0], body, 0)
    width = a_ref.shape[2]
    cross = total_ref[:, width : width + RK]
    first = total_ref[:RK, :RK] + total_ref[:RK, width : width + RK] + cross[:RK, :].T
    row, col = triangle_ids()
    half = RK // 2
    lower = jnp.concatenate([first[half:, half:], first[half:, :half]], axis=1)
    tall_ref[:half, :] = jnp.where((row >= col)[:half, :], lower, first[:half, :])
    tall_ref[half : half + RK, :] = (
        total_ref[:RK, RK:width] + total_ref[:RK, width + RK :] + cross[RK:, :].T
    )
    diagonal = jnp.sum(jnp.where(row == col, first, 0.0), axis=0, keepdims=True)
    tail = tall_ref.shape[0] - half - RK
    tall_ref[half + RK :, :] = jnp.broadcast_to(diagonal, (tail, LANES))
    store_blocks(tall_ref, outs)


def relay_kernel(points, r_hbm, _, hi_ref, lo_ref, token_ref, r_ref, sems):
    token_ref[...] = jnp.zeros_like(token_ref)
    halves, steps, chunk, _ = r_ref.shape
    ranks = chunk // points

    def copy(c, i):
        return pltpu.make_async_copy(
            r_hbm.at[pl.ds(i * chunk, chunk), pl.ds(c * LANES, LANES)],
            r_ref.at[c, i],
            sems.at[c, i],
        )

    for i in range(steps):
        for c in range(halves):
            copy(c, i).start()

    def body(i, carry):
        for c in range(halves):
            copy(c, i).wait()
            for p in range(points):
                hi, lo = split(r_ref[c, i, pl.ds(p, ranks, stride=points), :])
                place = pl.ds(pl.multiple_of(i * ranks, ranks), ranks)
                hi_ref[p, place, c * LANES : (c + 1) * LANES] = hi
                lo_ref[p, place, c * LANES : (c + 1) * LANES] = lo
        return carry

    lax.fori_loop(0, steps, body, 0)


def absorb_kernel(scale, *refs):
    blocks, refs = refs[:SPREAD_ONE], refs[SPREAD_ONE:]
    hi_ref, lo_ref, absorbed_ref, linv_ref = refs[:4]
    outs = refs[4 : 4 + SPREAD_TWO]
    tall_ref, pack_ref, w_ref, total_ref = refs[4 + SPREAD_TWO :]
    row, col = triangle_ids()
    load_blocks(blocks, tall_ref)
    half = RK // 2
    top = tall_ref[:half, :]
    mixed = jnp.concatenate(
        [top, jnp.concatenate([top[:, half:], top[:, :half]], axis=1)], axis=0
    )
    sent = ((row < half) & (col > row)) | ((col >= half) & (row > col))
    diagonal = jnp.broadcast_to(tall_ref[half + RK : half + RK + 1, :], (LANES, LANES))
    w_ref[:, :LANES] = jnp.where(sent, mixed, jnp.where(row == col, diagonal, mixed.T))
    w_ref[:, LANES : 2 * LANES] = tall_ref[half : half + RK, :]
    w_ref[:, 2 * LANES :] = jnp.where(row == col, 1.0, 0.0).astype(F32)
    factor_rows(w_ref, 3)
    linv_ref[...] = w_ref[:, 2 * LANES :] * scale
    upper = jnp.concatenate(
        [jnp.where(col >= row, w_ref[:, :LANES], 0.0), w_ref[:, LANES : 2 * LANES]], axis=1
    )
    upper_hi, upper_lo = split(upper)
    upper_both = jnp.concatenate([upper_hi, upper_lo], axis=0)
    points = absorbed_ref.shape[0]
    group = 4
    for step in range(points // group):
        pieces = []
        for i in range(group):
            p = step * group + i
            first = dot_nn(upper_both, hi_ref[p])
            b = first[:RK, :] + first[RK:, :] + dot_nn(upper_hi, lo_ref[p])
            absorbed_ref[p] = b
            pieces.append(split(b))
        b_hi = jnp.concatenate([x[0] for x in pieces], axis=0)
        b_lo = jnp.concatenate([x[1] for x in pieces], axis=0)
        part = dot_tn(b_hi, jnp.concatenate([b_hi, b_lo], axis=1))
        total_ref[...] = part if step == 0 else total_ref[...] + part
    cross = total_ref[:, 256:]
    gram = total_ref[:, :256] + cross + cross.T
    lower_right = gram[LANES:, LANES:]
    pack_ref[:LANES, :] = jnp.where(col >= row, gram[:LANES, :LANES], lower_right)
    pack_ref[LANES : 2 * LANES, :] = gram[:LANES, LANES:]
    diagonal = jnp.sum(jnp.where(row == col, lower_right, 0.0), axis=0, keepdims=True)
    tail = pack_ref.shape[0] - 2 * LANES
    pack_ref[2 * LANES :, :] = jnp.broadcast_to(diagonal, (tail, LANES))
    store_blocks(pack_ref, outs)


def left_kernel(a_ref, linv_ref, _, left_ref, token_ref):
    l_hi, l_lo = split(linv_ref[...])
    hi, lo = split(a_ref[...])
    left_ref[...] = dot_nt(hi, l_hi) + dot_nt(hi, l_lo) + dot_nt(lo, l_hi)
    token_ref[...] = jnp.zeros_like(token_ref)


def right_kernel(points, absorbed_ref, _, right_ref, token_ref):
    count = absorbed_ref.shape[1]
    for p in range(points):
        right_ref[pl.ds(p, count, stride=points), :] = absorbed_ref[p]
    token_ref[...] = jnp.zeros_like(token_ref)


def factor_kernel(scale, *refs):
    blocks, (out_ref, pack_ref, w_ref) = refs[:SPREAD_TWO], refs[SPREAD_TWO:]
    load_blocks(blocks, pack_ref)
    row, col = triangle_ids()
    packed = pack_ref[:LANES, :] * scale
    turned = packed.T
    diagonal = jnp.broadcast_to(pack_ref[2 * LANES : 2 * LANES + 1, :], (LANES, LANES)) * scale
    w_ref[:LANES, :LANES] = jnp.where(col >= row, packed, turned)
    w_ref[:LANES, LANES:] = pack_ref[LANES : 2 * LANES, :] * scale
    w_ref[LANES:, :LANES] = jnp.zeros((LANES, LANES), F32)
    w_ref[LANES:, LANES:] = jnp.where(row > col, packed, jnp.where(row == col, diagonal, turned))
    factor_rows(w_ref, 2)
    out_ref[:LANES, :LANES] = jnp.where(col >= row, w_ref[:LANES, :LANES], 0.0)
    out_ref[:LANES, LANES:] = w_ref[:LANES, LANES:]
    out_ref[LANES:, :LANES] = jnp.zeros((LANES, LANES), F32)
    out_ref[LANES:, LANES:] = jnp.where(col >= row, w_ref[LANES:, LANES:], 0.0)


def shape(*dims, dtype=F32):
    return jax.ShapeDtypeStruct(dims, dtype)


TOKEN = shape(8, LANES)


def params(steps=0, limit=VMEM_LIMIT):
    return pltpu.CompilerParams(
        dimension_semantics=("arbitrary",) * steps or None, vmem_limit_bytes=limit
    )


def cost(mebibytes):
    return pl.CostEstimate(flops=0, bytes_accessed=mebibytes * 2**20, transcendentals=0)


def swap(value, axes, mask):
    axes = axes if isinstance(axes, tuple) else (axes,)
    size = math.prod(lax.axis_size(a) for a in axes)
    return lax.ppermute(value, axes, [(i, i ^ mask) for i in range(size)])


def four_sum(total, axes, one, two, work):
    first = swap(total, axes, one)
    second = swap(total, axes, two)
    third = swap(total, axes, one ^ two)
    result = None
    if work is not None:
        result, token = work(total)
        third = third + token[:1, :]
    return (total + first) + (second + third), result


def rest_sum(total, pairs):
    for axes, mask in pairs:
        total = total + swap(total, axes, mask)
    return total


def bits(axis, first):
    return [1 << i for i in range(first, lax.axis_size(axis).bit_length() - 1)]


def sum_over_devices(blocks, works):
    n = len(blocks)
    total = blocks[0]
    for d in range(1, n):
        total = total + swap(blocks[d], PLANE, d)
    far = [("gx", m) for m in bits("gx", 1)] + [("gz", m) for m in bits("gz", 2)]
    total, first = four_sum(total, PLANE, 2, 4, works[0])
    total, second = four_sum(total, "gz", 1, 2, works[1])
    total = rest_sum(total, far)
    return [total] + [swap(total, PLANE, d) for d in range(1, n)], (first, second)


def relay_part(rows_right, points, token):
    steps = 4
    rows, width = rows_right.shape
    chunk = rows // steps
    vmem = pl.BlockSpec(memory_space=pltpu.VMEM)
    high, low, token = pl.pallas_call(
        functools.partial(relay_kernel, points),
        in_specs=[pl.BlockSpec(memory_space=pl.ANY), vmem],
        out_specs=[vmem] * 3,
        out_shape=[shape(points, rows // points, width, dtype=BF16)] * 2 + [TOKEN],
        scratch_shapes=[
            pltpu.VMEM((width // LANES, steps, chunk, LANES), F32),
            pltpu.SemaphoreType.DMA((width // LANES, steps)),
        ],
        compiler_params=params(limit=47 * 1024 * 1024),
        cost_estimate=cost(8),
        name="relay_right",
    )(rows_right, token)
    return (high, low), token


def left_part(unfold, linv, token):
    steps = 4
    chunk = unfold.shape[0] // steps
    return pl.pallas_call(
        left_kernel,
        grid=(steps,),
        in_specs=[
            pl.BlockSpec((chunk, RK), lambda i: (i, 0)),
            pl.BlockSpec((RK, RK), lambda i: (0, 0)),
            pl.BlockSpec((8, LANES), lambda i: (0, 0)),
        ],
        out_specs=[
            pl.BlockSpec((chunk, RK), lambda i: (i, 0)),
            pl.BlockSpec((8, LANES), lambda i: (0, 0)),
        ],
        out_shape=[shape(unfold.shape[0], RK), TOKEN],
        compiler_params=params(1, 16 * 1024 * 1024),
        cost_estimate=cost(8),
        name="left_out",
    )(unfold, linv, token)


def right_part(absorbed, token):
    points, ranks, width = absorbed.shape
    steps = 2
    return pl.pallas_call(
        functools.partial(right_kernel, points),
        grid=(steps, 2),
        in_specs=[
            pl.BlockSpec((points, ranks // steps, LANES), lambda i, c: (0, i, c)),
            pl.BlockSpec((8, LANES), lambda i, c: (0, 0)),
        ],
        out_specs=[
            pl.BlockSpec((ranks // steps * points, LANES), lambda i, c: (i, c)),
            pl.BlockSpec((8, LANES), lambda i, c: (0, 0)),
        ],
        out_shape=[shape(ranks * points, width), TOKEN],
        compiler_params=params(2, 16 * 1024 * 1024),
        cost_estimate=cost(8),
        name="right_out",
    )(absorbed, token)


def per_device(left_core, right_core):
    rank_left, points, rank_mid = left_core.shape
    rank_right = right_core.shape[2]
    total_points = points * lax.axis_size("gx") * lax.axis_size("gy") * lax.axis_size("gz")
    unfold = left_core.reshape(rank_left * points, rank_mid)
    rows_right = right_core.reshape(rank_mid * points, rank_right)
    vmem = pl.BlockSpec(memory_space=pltpu.VMEM)

    steps = 8
    block_rows = (RK // 2 + RK + 16) // SPREAD_ONE
    blocks = pl.pallas_call(
        gram_kernel,
        in_specs=[pl.BlockSpec(memory_space=pl.ANY)],
        out_specs=[vmem] * SPREAD_ONE,
        out_shape=[shape(block_rows, LANES)] * SPREAD_ONE,
        scratch_shapes=[
            pltpu.VMEM((steps, unfold.shape[0] // steps, rank_mid), F32),
            pltpu.VMEM((rank_mid, 2 * rank_mid), F32),
            pltpu.VMEM((SPREAD_ONE * block_rows, LANES), F32),
            pltpu.SemaphoreType.DMA((steps,)),
        ],
        compiler_params=params(limit=53 * 1024 * 1024),
        name="gram_top",
    )(unfold)
    summed, (_, relayed) = sum_over_devices(
        blocks,
        [None, functools.partial(relay_part, rows_right, points)],
    )

    tall_rows = SPREAD_ONE * block_rows
    block_rows = LANES + 8
    packed_rows = SPREAD_TWO * block_rows
    absorbed, linv, *blocks = pl.pallas_call(
        functools.partial(absorb_kernel, math.sqrt(rank_left * total_points)),
        in_specs=[vmem] * (SPREAD_ONE + 2),
        out_specs=[vmem] * (2 + SPREAD_TWO),
        out_shape=[shape(points, RK, rank_right), shape(RK, RK)] + [shape(block_rows, LANES)] * SPREAD_TWO,
        scratch_shapes=[
            pltpu.VMEM((tall_rows, LANES), F32),
            pltpu.VMEM((packed_rows, LANES), F32),
            pltpu.VMEM((LANES, 3 * LANES), F32),
            pltpu.VMEM((rank_right, 2 * rank_right), F32),
        ],
        compiler_params=params(limit=24 * 1024 * 1024),
        name="factor_absorb",
    )(*summed, *relayed)
    summed, (right_out, left_out) = sum_over_devices(
        blocks,
        [
            functools.partial(right_part, absorbed),
            functools.partial(left_part, unfold, linv),
        ],
    )

    factor = pl.pallas_call(
        functools.partial(factor_kernel, 1.0 / (RK * total_points)),
        in_specs=[vmem] * SPREAD_TWO,
        out_specs=vmem,
        out_shape=shape(rank_right, rank_right),
        scratch_shapes=[
            pltpu.VMEM((packed_rows, LANES), F32),
            pltpu.VMEM((2 * LANES, 2 * LANES), F32),
        ],
        compiler_params=params(limit=16 * 1024 * 1024),
        name="factor_next",
    )(*summed)
    return (
        left_out.reshape(rank_left, points, RK),
        right_out.reshape(RK, points, rank_right),
        factor,
    )


def solution(mesh):
    in_specs = (P(None, AXES, None), P(None, AXES, None))
    out_specs = (P(None, AXES, None), P(None, AXES, None), P())
    return jax.shard_map(
        per_device, mesh=mesh, in_specs=in_specs, out_specs=out_specs, check_vma=False
    )
```

```python
import functools
import math

import jax
import jax.numpy as jnp
from jax import lax
from jax.experimental import pallas as pl
from jax.experimental.pallas import tpu as pltpu
from jax.sharding import PartitionSpec as P

RK = 128
AXES = ("gx", "gy", "gz")
LANES = 128
PANEL = 16
PLANE = ("gx", "gy")
SPREAD_ONE = 2
SPREAD_TWO = 2
F32 = jnp.float32
BF16 = jnp.bfloat16
VMEM_LIMIT = 48 * 1024 * 1024


def split(x):
    hi = x.astype(BF16)
    return hi, (x - hi.astype(F32)).astype(BF16)


def dot_tn(a, b):
    return lax.dot_general(a, b, (((0,), (0,)), ((), ())), preferred_element_type=F32)


def dot_nt(a, b):
    return lax.dot_general(a, b, (((1,), (1,)), ((), ())), preferred_element_type=F32)


def dot_nn(a, b):
    return lax.dot_general(a, b, (((1,), (0,)), ((), ())), preferred_element_type=F32)


def stacked_pieces(x):
    one = x.astype(BF16).astype(F32)
    rest = x - one
    two = rest.astype(BF16).astype(F32)
    three = rest - two
    left = jnp.concatenate([one, one, two, two, one, three], axis=0).astype(BF16)
    right = jnp.concatenate([one, two, one, two, three, one], axis=0).astype(BF16)
    return left, right


def three_pieces(x):
    one = x.astype(BF16)
    rest = x - one.astype(F32)
    two = rest.astype(BF16)
    return one, two, (rest - two.astype(F32)).astype(BF16)


def turned_product(tall, wide):
    a, b, c = three_pieces(tall)
    x, y, z = three_pieces(wide)
    small = dot_nn(c, x) + dot_nn(a, z) + dot_nn(b, y)
    return small + (dot_nn(b, x) + dot_nn(a, y)) + dot_nn(a, x)


def spread_row(x, k):
    return jnp.broadcast_to(x[k : k + 1, :], x.shape)


def factor_rows(w_ref, blocks, stacked):
    size = w_ref.shape[0]
    row_id = lax.broadcasted_iota(jnp.int32, (PANEL, LANES), 0)
    rows = [
        [w_ref[g : g + PANEL, b * LANES : (b + 1) * LANES] for b in range(blocks)]
        for g in range(0, size, PANEL)
    ]
    for now in range(len(rows)):
        own, lane = divmod(now * PANEL, LANES)
        panel = rows[now]
        columns = [
            jnp.broadcast_to(panel[own][:, lane + k : lane + k + 1], (PANEL, LANES))
            for k in range(PANEL)
        ]
        follows = now + 1 < len(rows)
        if follows:
            block, down = divmod((now + 1) * PANEL, LANES)
            turned = panel[block].T[down : down + PANEL, :]
            ahead = [jnp.broadcast_to(turned[:, k : k + 1], (PANEL, LANES)) for k in range(PANEL)]
        scale = jnp.zeros((PANEL, LANES), F32)
        pivot = spread_row(columns[0], 0)
        for k in range(PANEL):
            inverse = pl.reciprocal(pivot, approx=True)
            scale = jnp.where(row_id == k, lax.rsqrt(pivot), scale)
            multiples = columns[k] * inverse
            if follows:
                ahead_multiples = ahead[k] * inverse
            for m in range(k + 1, PANEL):
                entry = spread_row(columns[k], m)
                if m == k + 1:
                    pivot = spread_row(columns[m], m) - (entry * inverse) * entry
                columns[m] = columns[m] - multiples * entry
                if follows:
                    ahead[m] = ahead[m] - ahead_multiples * entry
            below = jnp.where(row_id > k, multiples, 0.0)
            for b in range(own, blocks):
                source = spread_row(panel[b], k)
                panel[b] = panel[b] - below * source
                if follows:
                    rows[now + 1][b] = rows[now + 1][b] - ahead_multiples * source
        done = [panel[b] * scale for b in range(own, blocks)]
        for b in range(own, blocks):
            w_ref[now * PANEL : (now + 1) * PANEL, b * LANES : (b + 1) * LANES] = done[b - own]
        if now + 2 < len(rows):
            if stacked:
                both = [stacked_pieces(x) for x in done]
                left = jnp.concatenate([x[0] for x in both[: size // LANES - own]], axis=1)
                right = jnp.concatenate([x[1] for x in both], axis=1)
                update = dot_tn(left, right)
            else:
                tall = jnp.concatenate([x.T for x in done[: size // LANES - own]], axis=0)
                update = turned_product(tall, jnp.concatenate(done, axis=1))
            for g in range(now + 2, len(rows)):
                top = g * PANEL - own * LANES
                for b in range(g * PANEL // LANES, blocks):
                    across = (b - own) * LANES
                    rows[g][b] = (
                        rows[g][b] - update[top : top + PANEL, across : across + LANES]
                    )


def triangle_ids():
    return (
        lax.broadcasted_iota(jnp.int32, (LANES, LANES), 0),
        lax.broadcasted_iota(jnp.int32, (LANES, LANES), 1),
    )


def store_blocks(tall_ref, outs):
    me = lax.rem(lax.axis_index(PLANE), len(outs))
    size = outs[0].shape[0]
    for d, out in enumerate(outs):
        out[...] = tall_ref[pl.ds(pl.multiple_of((me ^ d) * size, 8), size), :]


def load_blocks(blocks, tall_ref):
    me = lax.rem(lax.axis_index(PLANE), len(blocks))
    size = blocks[0].shape[0]
    for d, block in enumerate(blocks):
        tall_ref[pl.ds(pl.multiple_of((me ^ d) * size, 8), size), :] = block[...]


def chunk_copies(source, held, sems):
    steps, chunk = held.shape[:2]

    def copy(i):
        return pltpu.make_async_copy(
            source.at[pl.ds(i * chunk, chunk), :], held.at[i], sems.at[i]
        )

    for i in range(steps):
        copy(i).start()
    return copy


def gram_kernel(a_hbm, *refs):
    outs = refs[:SPREAD_ONE]
    a_ref, total_ref, tall_ref, sems = refs[SPREAD_ONE:]
    copy = chunk_copies(a_hbm, a_ref, sems)
    for i in range(a_ref.shape[0]):
        copy(i).wait()
        hi, lo = split(a_ref[i])
        part = dot_tn(hi, jnp.concatenate([hi, lo], axis=1))
        total_ref[...] = part if i == 0 else total_ref[...] + part
    width = a_ref.shape[2]
    cross = total_ref[:, width : width + RK]
    first = total_ref[:RK, :RK] + total_ref[:RK, width : width + RK] + cross[:RK, :].T
    row, col = triangle_ids()
    half = RK // 2
    lower = jnp.concatenate([first[half:, half:], first[half:, :half]], axis=1)
    tall_ref[:half, :] = jnp.where((row >= col)[:half, :], lower, first[:half, :])
    tall_ref[half : half + RK, :] = (
        total_ref[:RK, RK:width] + total_ref[:RK, width + RK :] + cross[RK:, :].T
    )
    diagonal = jnp.sum(jnp.where(row == col, first, 0.0), axis=0, keepdims=True)
    tail = tall_ref.shape[0] - half - RK
    tall_ref[half + RK :, :] = jnp.broadcast_to(diagonal, (tail, LANES))
    store_blocks(tall_ref, outs)


def relay_kernel(points, r_hbm, _, hi_ref, lo_ref, token_ref, r_ref, sems):
    token_ref[...] = jnp.zeros_like(token_ref)
    halves, steps, chunk, _ = r_ref.shape
    ranks = chunk // points

    def copy(c, i):
        return pltpu.make_async_copy(
            r_hbm.at[pl.ds(i * chunk, chunk), pl.ds(c * LANES, LANES)],
            r_ref.at[c, i],
            sems.at[c, i],
        )

    for i in range(steps):
        for c in range(halves):
            copy(c, i).start()

    def body(i, carry):
        for c in range(halves):
            copy(c, i).wait()
            for p in range(points):
                hi, lo = split(r_ref[c, i, pl.ds(p, ranks, stride=points), :])
                place = pl.ds(pl.multiple_of(i * ranks, ranks), ranks)
                hi_ref[p, place, c * LANES : (c + 1) * LANES] = hi
                lo_ref[p, place, c * LANES : (c + 1) * LANES] = lo
        return carry

    lax.fori_loop(0, steps, body, 0)


def absorb_kernel(scale, *refs):
    blocks, refs = refs[:SPREAD_ONE], refs[SPREAD_ONE:]
    hi_ref, lo_ref, absorbed_ref, linv_ref = refs[:4]
    outs = refs[4 : 4 + SPREAD_TWO]
    tall_ref, pack_ref, w_ref, total_ref = refs[4 + SPREAD_TWO :]
    row, col = triangle_ids()
    load_blocks(blocks, tall_ref)
    half = RK // 2
    top = tall_ref[:half, :]
    mixed = jnp.concatenate(
        [top, jnp.concatenate([top[:, half:], top[:, :half]], axis=1)], axis=0
    )
    sent = ((row < half) & (col > row)) | ((col >= half) & (row > col))
    diagonal = jnp.broadcast_to(tall_ref[half + RK : half + RK + 1, :], (LANES, LANES))
    w_ref[:, :LANES] = jnp.where(sent, mixed, jnp.where(row == col, diagonal, mixed.T))
    w_ref[:, LANES : 2 * LANES] = tall_ref[half : half + RK, :]
    w_ref[:, 2 * LANES :] = jnp.where(row == col, 1.0, 0.0).astype(F32)
    factor_rows(w_ref, 3, True)
    linv_ref[...] = w_ref[:, 2 * LANES :] * scale
    upper = jnp.concatenate(
        [jnp.where(col >= row, w_ref[:, :LANES], 0.0), w_ref[:, LANES : 2 * LANES]], axis=1
    )
    upper_hi, upper_lo = split(upper)
    upper_both = jnp.concatenate([upper_hi, upper_lo], axis=0)
    points = absorbed_ref.shape[0]
    group = 4
    for step in range(points // group):
        pieces = []
        for i in range(group):
            p = step * group + i
            first = dot_nn(upper_both, hi_ref[p])
            b = first[:RK, :] + first[RK:, :] + dot_nn(upper_hi, lo_ref[p])
            absorbed_ref[p] = b
            pieces.append(split(b))
        b_hi = jnp.concatenate([x[0] for x in pieces], axis=0)
        b_lo = jnp.concatenate([x[1] for x in pieces], axis=0)
        part = dot_tn(b_hi, jnp.concatenate([b_hi, b_lo], axis=1))
        total_ref[...] = part if step == 0 else total_ref[...] + part
    cross = total_ref[:, 256:]
    gram = total_ref[:, :256] + cross + cross.T
    lower_right = gram[LANES:, LANES:]
    pack_ref[:LANES, :] = jnp.where(col >= row, gram[:LANES, :LANES], lower_right)
    pack_ref[LANES : 2 * LANES, :] = gram[:LANES, LANES:]
    diagonal = jnp.sum(jnp.where(row == col, lower_right, 0.0), axis=0, keepdims=True)
    tail = pack_ref.shape[0] - 2 * LANES
    pack_ref[2 * LANES :, :] = jnp.broadcast_to(diagonal, (tail, LANES))
    store_blocks(pack_ref, outs)


def left_kernel(a_ref, linv_ref, _, left_ref, token_ref):
    l_hi, l_lo = split(linv_ref[...])
    hi, lo = split(a_ref[...])
    left_ref[...] = dot_nt(hi, l_hi) + dot_nt(hi, l_lo) + dot_nt(lo, l_hi)
    token_ref[...] = jnp.zeros_like(token_ref)


def right_kernel(points, absorbed_ref, _, right_ref, token_ref):
    count = absorbed_ref.shape[1]
    for p in range(points):
        right_ref[pl.ds(p, count, stride=points), :] = absorbed_ref[p]
    token_ref[...] = jnp.zeros_like(token_ref)


def factor_kernel(scale, *refs):
    blocks, (out_ref, pack_ref, w_ref) = refs[:SPREAD_TWO], refs[SPREAD_TWO:]
    load_blocks(blocks, pack_ref)
    row, col = triangle_ids()
    packed = pack_ref[:LANES, :] * scale
    turned = packed.T
    diagonal = jnp.broadcast_to(pack_ref[2 * LANES : 2 * LANES + 1, :], (LANES, LANES)) * scale
    w_ref[:LANES, :LANES] = jnp.where(col >= row, packed, turned)
    w_ref[:LANES, LANES:] = pack_ref[LANES : 2 * LANES, :] * scale
    w_ref[LANES:, :LANES] = jnp.zeros((LANES, LANES), F32)
    w_ref[LANES:, LANES:] = jnp.where(row > col, packed, jnp.where(row == col, diagonal, turned))
    factor_rows(w_ref, 2, False)
    out_ref[:LANES, :LANES] = jnp.where(col >= row, w_ref[:LANES, :LANES], 0.0)
    out_ref[:LANES, LANES:] = w_ref[:LANES, LANES:]
    out_ref[LANES:, :LANES] = jnp.zeros((LANES, LANES), F32)
    out_ref[LANES:, LANES:] = jnp.where(col >= row, w_ref[LANES:, LANES:], 0.0)


def shape(*dims, dtype=F32):
    return jax.ShapeDtypeStruct(dims, dtype)


TOKEN = shape(8, LANES)


def params(steps=0, limit=VMEM_LIMIT):
    return pltpu.CompilerParams(
        dimension_semantics=("arbitrary",) * steps or None, vmem_limit_bytes=limit
    )


def cost(mebibytes):
    return pl.CostEstimate(flops=0, bytes_accessed=mebibytes * 2**20, transcendentals=0)


def swap(value, axes, mask):
    axes = axes if isinstance(axes, tuple) else (axes,)
    size = math.prod(lax.axis_size(a) for a in axes)
    return lax.ppermute(value, axes, [(i, i ^ mask) for i in range(size)])


def four_sum(total, axes, one, two, work):
    first = swap(total, axes, one)
    second = swap(total, axes, two)
    third = swap(total, axes, one ^ two)
    result = None
    if work is not None:
        result, token = work(total)
        third = third + token[:1, :]
    return (total + first) + (second + third), result


def rest_sum(total, pairs):
    for axes, mask in pairs:
        total = total + swap(total, axes, mask)
    return total


def bits(axis, first):
    return [1 << i for i in range(first, lax.axis_size(axis).bit_length() - 1)]


def sum_over_devices(blocks, works):
    n = len(blocks)
    total = blocks[0]
    for d in range(1, n):
        total = total + swap(blocks[d], PLANE, d)
    far = [("gx", m) for m in bits("gx", 1)] + [("gz", m) for m in bits("gz", 2)]
    total, first = four_sum(total, PLANE, 2, 4, works[0])
    total, second = four_sum(total, "gz", 1, 2, works[1])
    total = rest_sum(total, far)
    return [total] + [swap(total, PLANE, d) for d in range(1, n)], (first, second)


def relay_part(rows_right, points, token):
    steps = 4
    rows, width = rows_right.shape
    chunk = rows // steps
    vmem = pl.BlockSpec(memory_space=pltpu.VMEM)
    high, low, token = pl.pallas_call(
        functools.partial(relay_kernel, points),
        in_specs=[pl.BlockSpec(memory_space=pl.ANY), vmem],
        out_specs=[vmem] * 3,
        out_shape=[shape(points, rows // points, width, dtype=BF16)] * 2 + [TOKEN],
        scratch_shapes=[
            pltpu.VMEM((width // LANES, steps, chunk, LANES), F32),
            pltpu.SemaphoreType.DMA((width // LANES, steps)),
        ],
        compiler_params=params(limit=47 * 1024 * 1024),
        cost_estimate=cost(8),
        name="relay_right",
    )(rows_right, token)
    return (high, low), token


def left_part(unfold, linv, token):
    steps = 4
    chunk = unfold.shape[0] // steps
    return pl.pallas_call(
        left_kernel,
        grid=(steps,),
        in_specs=[
            pl.BlockSpec((chunk, RK), lambda i: (i, 0)),
            pl.BlockSpec((RK, RK), lambda i: (0, 0)),
            pl.BlockSpec((8, LANES), lambda i: (0, 0)),
        ],
        out_specs=[
            pl.BlockSpec((chunk, RK), lambda i: (i, 0)),
            pl.BlockSpec((8, LANES), lambda i: (0, 0)),
        ],
        out_shape=[shape(unfold.shape[0], RK), TOKEN],
        compiler_params=params(1, 16 * 1024 * 1024),
        cost_estimate=cost(8),
        name="left_out",
    )(unfold, linv, token)


def right_part(absorbed, token):
    points, ranks, width = absorbed.shape
    steps = 2
    return pl.pallas_call(
        functools.partial(right_kernel, points),
        grid=(steps, 2),
        in_specs=[
            pl.BlockSpec((points, ranks // steps, LANES), lambda i, c: (0, i, c)),
            pl.BlockSpec((8, LANES), lambda i, c: (0, 0)),
        ],
        out_specs=[
            pl.BlockSpec((ranks // steps * points, LANES), lambda i, c: (i, c)),
            pl.BlockSpec((8, LANES), lambda i, c: (0, 0)),
        ],
        out_shape=[shape(ranks * points, width), TOKEN],
        compiler_params=params(2, 16 * 1024 * 1024),
        cost_estimate=cost(8),
        name="right_out",
    )(absorbed, token)


def per_device(left_core, right_core):
    rank_left, points, rank_mid = left_core.shape
    rank_right = right_core.shape[2]
    total_points = points * lax.axis_size("gx") * lax.axis_size("gy") * lax.axis_size("gz")
    unfold = left_core.reshape(rank_left * points, rank_mid)
    rows_right = right_core.reshape(rank_mid * points, rank_right)
    vmem = pl.BlockSpec(memory_space=pltpu.VMEM)

    steps = 8
    block_rows = (RK // 2 + RK + 16) // SPREAD_ONE
    blocks = pl.pallas_call(
        gram_kernel,
        in_specs=[pl.BlockSpec(memory_space=pl.ANY)],
        out_specs=[vmem] * SPREAD_ONE,
        out_shape=[shape(block_rows, LANES)] * SPREAD_ONE,
        scratch_shapes=[
            pltpu.VMEM((steps, unfold.shape[0] // steps, rank_mid), F32),
            pltpu.VMEM((rank_mid, 2 * rank_mid), F32),
            pltpu.VMEM((SPREAD_ONE * block_rows, LANES), F32),
            pltpu.SemaphoreType.DMA((steps,)),
        ],
        compiler_params=params(limit=53 * 1024 * 1024),
        name="gram_top",
    )(unfold)
    summed, (_, relayed) = sum_over_devices(
        blocks,
        [None, functools.partial(relay_part, rows_right, points)],
    )

    tall_rows = SPREAD_ONE * block_rows
    block_rows = LANES + 8
    packed_rows = SPREAD_TWO * block_rows
    absorbed, linv, *blocks = pl.pallas_call(
        functools.partial(absorb_kernel, math.sqrt(rank_left * total_points)),
        in_specs=[vmem] * (SPREAD_ONE + 2),
        out_specs=[vmem] * (2 + SPREAD_TWO),
        out_shape=[shape(points, RK, rank_right), shape(RK, RK)] + [shape(block_rows, LANES)] * SPREAD_TWO,
        scratch_shapes=[
            pltpu.VMEM((tall_rows, LANES), F32),
            pltpu.VMEM((packed_rows, LANES), F32),
            pltpu.VMEM((LANES, 3 * LANES), F32),
            pltpu.VMEM((rank_right, 2 * rank_right), F32),
        ],
        compiler_params=params(limit=24 * 1024 * 1024),
        name="factor_absorb",
    )(*summed, *relayed)
    summed, (right_out, left_out) = sum_over_devices(
        blocks,
        [
            functools.partial(right_part, absorbed),
            functools.partial(left_part, unfold, linv),
        ],
    )

    factor = pl.pallas_call(
        functools.partial(factor_kernel, 1.0 / (RK * total_points)),
        in_specs=[vmem] * SPREAD_TWO,
        out_specs=vmem,
        out_shape=shape(rank_right, rank_right),
        scratch_shapes=[
            pltpu.VMEM((packed_rows, LANES), F32),
            pltpu.VMEM((2 * LANES, 2 * LANES), F32),
        ],
        compiler_params=params(limit=16 * 1024 * 1024),
        name="factor_next",
    )(*summed)
    return (
        left_out.reshape(rank_left, points, RK),
        right_out.reshape(RK, points, rank_right),
        factor,
    )


def solution(mesh):
    in_specs = (P(None, AXES, None), P(None, AXES, None))
    out_specs = (P(None, AXES, None), P(None, AXES, None), P())
    return jax.shard_map(
        per_device, mesh=mesh, in_specs=in_specs, out_specs=out_specs, check_vma=False
    )
```

```python
import functools
import math

import jax
import jax.numpy as jnp
from jax import lax
from jax.experimental import pallas as pl
from jax.experimental.pallas import tpu as pltpu
from jax.sharding import PartitionSpec as P

RK = 128
AXES = ("gx", "gy", "gz")
LANES = 128
PANEL = 16
PLANE = ("gx", "gy")
SPREAD_ONE = 2
SPREAD_TWO = 2
F32 = jnp.float32
BF16 = jnp.bfloat16
VMEM_LIMIT = 48 * 1024 * 1024


def split(x):
    hi = x.astype(BF16)
    return hi, (x - hi.astype(F32)).astype(BF16)


def dot_tn(a, b):
    return lax.dot_general(a, b, (((0,), (0,)), ((), ())), preferred_element_type=F32)


def dot_nt(a, b):
    return lax.dot_general(a, b, (((1,), (1,)), ((), ())), preferred_element_type=F32)


def dot_nn(a, b):
    return lax.dot_general(a, b, (((1,), (0,)), ((), ())), preferred_element_type=F32)


def stacked_pieces(x):
    one = x.astype(BF16).astype(F32)
    rest = x - one
    two = rest.astype(BF16).astype(F32)
    three = rest - two
    left = jnp.concatenate([one, one, two, two, one, three], axis=0).astype(BF16)
    right = jnp.concatenate([one, two, one, two, three, one], axis=0).astype(BF16)
    return left, right


def spread_row(x, k):
    return jnp.broadcast_to(x[k : k + 1, :], x.shape)


def factor_rows(w_ref, blocks):
    size = w_ref.shape[0]
    row_id = lax.broadcasted_iota(jnp.int32, (PANEL, LANES), 0)
    rows = [
        [w_ref[g : g + PANEL, b * LANES : (b + 1) * LANES] for b in range(blocks)]
        for g in range(0, size, PANEL)
    ]
    for now in range(len(rows)):
        own, lane = divmod(now * PANEL, LANES)
        panel = rows[now]
        columns = [
            jnp.broadcast_to(panel[own][:, lane + k : lane + k + 1], (PANEL, LANES))
            for k in range(PANEL)
        ]
        follows = now + 1 < len(rows)
        if follows:
            block, down = divmod((now + 1) * PANEL, LANES)
            turned = panel[block].T[down : down + PANEL, :]
            ahead = [jnp.broadcast_to(turned[:, k : k + 1], (PANEL, LANES)) for k in range(PANEL)]
        scale = jnp.zeros((PANEL, LANES), F32)
        pivot = spread_row(columns[0], 0)
        partial_pivot = spread_row(columns[1], 1)
        beneath = spread_row(columns[0], 1)
        for k in range(PANEL):
            inverse = pl.reciprocal(pivot, approx=True)
            scale = jnp.where(row_id == k, lax.rsqrt(pivot), scale)
            multiples = columns[k] * inverse
            if follows:
                ahead_multiples = ahead[k] * inverse
            entries = {m: spread_row(columns[k], m) for m in range(k + 1, PANEL)}
            pivot = partial_pivot - (beneath * inverse) * beneath
            if k + 2 < PANEL:
                second = entries[k + 2] * inverse
                beneath = spread_row(columns[k + 1], k + 2) - second * entries[k + 1]
                partial_pivot = spread_row(columns[k + 2], k + 2) - second * entries[k + 2]
            for m, entry in entries.items():
                columns[m] = columns[m] - multiples * entry
                if follows:
                    ahead[m] = ahead[m] - ahead_multiples * entry
            below = jnp.where(row_id > k, multiples, 0.0)
            for b in range(own, blocks):
                source = spread_row(panel[b], k)
                panel[b] = panel[b] - below * source
                if follows:
                    rows[now + 1][b] = rows[now + 1][b] - ahead_multiples * source
        done = [panel[b] * scale for b in range(own, blocks)]
        for b in range(own, blocks):
            w_ref[now * PANEL : (now + 1) * PANEL, b * LANES : (b + 1) * LANES] = done[b - own]
        if now + 2 < len(rows):
            both = [stacked_pieces(x) for x in done]
            left = jnp.concatenate([x[0] for x in both[: size // LANES - own]], axis=1)
            right = jnp.concatenate([x[1] for x in both], axis=1)
            update = dot_tn(left, right)
            for g in range(now + 2, len(rows)):
                top = g * PANEL - own * LANES
                for b in range(g * PANEL // LANES, blocks):
                    across = (b - own) * LANES
                    rows[g][b] = (
                        rows[g][b] - update[top : top + PANEL, across : across + LANES]
                    )


def triangle_ids():
    return (
        lax.broadcasted_iota(jnp.int32, (LANES, LANES), 0),
        lax.broadcasted_iota(jnp.int32, (LANES, LANES), 1),
    )


def store_blocks(tall_ref, outs):
    me = lax.rem(lax.axis_index(PLANE), len(outs))
    size = outs[0].shape[0]
    for d, out in enumerate(outs):
        out[...] = tall_ref[pl.ds(pl.multiple_of((me ^ d) * size, 8), size), :]


def load_blocks(blocks, tall_ref):
    me = lax.rem(lax.axis_index(PLANE), len(blocks))
    size = blocks[0].shape[0]
    for d, block in enumerate(blocks):
        tall_ref[pl.ds(pl.multiple_of((me ^ d) * size, 8), size), :] = block[...]


def chunk_copies(source, held, sems):
    steps, chunk = held.shape[:2]

    def copy(i):
        return pltpu.make_async_copy(
            source.at[pl.ds(i * chunk, chunk), :], held.at[i], sems.at[i]
        )

    for i in range(steps):
        copy(i).start(priority=i % 2)
    return copy


def gram_kernel(a_hbm, *refs):
    outs = refs[:SPREAD_ONE]
    a_ref, total_ref, tall_ref, sems = refs[SPREAD_ONE:]
    copy = chunk_copies(a_hbm, a_ref, sems)
    for i in range(a_ref.shape[0]):
        copy(i).wait()
        hi, lo = split(a_ref[i])
        part = dot_tn(hi, jnp.concatenate([hi, lo], axis=1))
        total_ref[...] = part if i == 0 else total_ref[...] + part
    width = a_ref.shape[2]
    cross = total_ref[:, width : width + RK]
    first = total_ref[:RK, :RK] + total_ref[:RK, width : width + RK] + cross[:RK, :].T
    row, col = triangle_ids()
    half = RK // 2
    lower = jnp.concatenate([first[half:, half:], first[half:, :half]], axis=1)
    tall_ref[:half, :] = jnp.where((row >= col)[:half, :], lower, first[:half, :])
    tall_ref[half : half + RK, :] = (
        total_ref[:RK, RK:width] + total_ref[:RK, width + RK :] + cross[RK:, :].T
    )
    diagonal = jnp.sum(jnp.where(row == col, first, 0.0), axis=0, keepdims=True)
    tail = tall_ref.shape[0] - half - RK
    tall_ref[half + RK :, :] = jnp.broadcast_to(diagonal, (tail, LANES))
    store_blocks(tall_ref, outs)


def relay_kernel(points, r_hbm, _, hi_ref, lo_ref, token_ref, r_ref, sems):
    token_ref[...] = jnp.zeros_like(token_ref)
    halves, steps, chunk, _ = r_ref.shape
    ranks = chunk // points

    def copy(c, i):
        return pltpu.make_async_copy(
            r_hbm.at[pl.ds(i * chunk, chunk), pl.ds(c * LANES, LANES)],
            r_ref.at[c, i],
            sems.at[c, i],
        )

    for i in range(steps):
        for c in range(halves):
            copy(c, i).start()

    def body(i, carry):
        for c in range(halves):
            copy(c, i).wait()
            for p in range(points):
                hi, lo = split(r_ref[c, i, pl.ds(p, ranks, stride=points), :])
                place = pl.ds(pl.multiple_of(i * ranks, ranks), ranks)
                hi_ref[p, place, c * LANES : (c + 1) * LANES] = hi
                lo_ref[p, place, c * LANES : (c + 1) * LANES] = lo
        return carry

    lax.fori_loop(0, steps, body, 0)


def absorb_kernel(scale, *refs):
    blocks, refs = refs[:SPREAD_ONE], refs[SPREAD_ONE:]
    hi_ref, lo_ref, absorbed_ref, linv_ref = refs[:4]
    outs = refs[4 : 4 + SPREAD_TWO]
    tall_ref, pack_ref, w_ref, total_ref = refs[4 + SPREAD_TWO :]
    row, col = triangle_ids()
    load_blocks(blocks, tall_ref)
    half = RK // 2
    top = tall_ref[:half, :]
    mixed = jnp.concatenate(
        [top, jnp.concatenate([top[:, half:], top[:, :half]], axis=1)], axis=0
    )
    sent = ((row < half) & (col > row)) | ((col >= half) & (row > col))
    diagonal = jnp.broadcast_to(tall_ref[half + RK : half + RK + 1, :], (LANES, LANES))
    w_ref[:, :LANES] = jnp.where(sent, mixed, jnp.where(row == col, diagonal, mixed.T))
    w_ref[:, LANES : 2 * LANES] = tall_ref[half : half + RK, :]
    w_ref[:, 2 * LANES :] = jnp.where(row == col, 1.0, 0.0).astype(F32)
    factor_rows(w_ref, 3)
    linv_ref[...] = w_ref[:, 2 * LANES :] * scale
    upper = jnp.concatenate(
        [jnp.where(col >= row, w_ref[:, :LANES], 0.0), w_ref[:, LANES : 2 * LANES]], axis=1
    )
    upper_hi, upper_lo = split(upper)
    upper_both = jnp.concatenate([upper_hi, upper_lo], axis=0)
    points = absorbed_ref.shape[0]
    group = 4
    for step in range(points // group):
        pieces = []
        for i in range(group):
            p = step * group + i
            first = dot_nn(upper_both, hi_ref[p])
            b = first[:RK, :] + first[RK:, :] + dot_nn(upper_hi, lo_ref[p])
            absorbed_ref[p] = b
            pieces.append(split(b))
        b_hi = jnp.concatenate([x[0] for x in pieces], axis=0)
        b_lo = jnp.concatenate([x[1] for x in pieces], axis=0)
        part = dot_tn(b_hi, jnp.concatenate([b_hi, b_lo], axis=1))
        total_ref[...] = part if step == 0 else total_ref[...] + part
    cross = total_ref[:, 256:]
    gram = total_ref[:, :256] + cross + cross.T
    lower_right = gram[LANES:, LANES:]
    pack_ref[:LANES, :] = jnp.where(col >= row, gram[:LANES, :LANES], lower_right)
    pack_ref[LANES : 2 * LANES, :] = gram[:LANES, LANES:]
    diagonal = jnp.sum(jnp.where(row == col, lower_right, 0.0), axis=0, keepdims=True)
    tail = pack_ref.shape[0] - 2 * LANES
    pack_ref[2 * LANES :, :] = jnp.broadcast_to(diagonal, (tail, LANES))
    store_blocks(pack_ref, outs)


def left_kernel(a_ref, linv_ref, _, left_ref, token_ref):
    l_hi, l_lo = split(linv_ref[...])
    hi, lo = split(a_ref[...])
    left_ref[...] = dot_nt(hi, l_hi) + dot_nt(hi, l_lo) + dot_nt(lo, l_hi)
    token_ref[...] = jnp.zeros_like(token_ref)


def right_kernel(points, absorbed_ref, _, right_ref, token_ref):
    count = absorbed_ref.shape[1]
    for p in range(points):
        right_ref[pl.ds(p, count, stride=points), :] = absorbed_ref[p]
    token_ref[...] = jnp.zeros_like(token_ref)


def factor_kernel(scale, *refs):
    blocks, (out_ref, pack_ref, w_ref) = refs[:SPREAD_TWO], refs[SPREAD_TWO:]
    load_blocks(blocks, pack_ref)
    row, col = triangle_ids()
    packed = pack_ref[:LANES, :] * scale
    turned = packed.T
    diagonal = jnp.broadcast_to(pack_ref[2 * LANES : 2 * LANES + 1, :], (LANES, LANES)) * scale
    w_ref[:LANES, :LANES] = jnp.where(col >= row, packed, turned)
    w_ref[:LANES, LANES:] = pack_ref[LANES : 2 * LANES, :] * scale
    w_ref[LANES:, :LANES] = jnp.zeros((LANES, LANES), F32)
    w_ref[LANES:, LANES:] = jnp.where(row > col, packed, jnp.where(row == col, diagonal, turned))
    factor_rows(w_ref, 2)
    out_ref[:LANES, :LANES] = jnp.where(col >= row, w_ref[:LANES, :LANES], 0.0)
    out_ref[:LANES, LANES:] = w_ref[:LANES, LANES:]
    out_ref[LANES:, :LANES] = jnp.zeros((LANES, LANES), F32)
    out_ref[LANES:, LANES:] = jnp.where(col >= row, w_ref[LANES:, LANES:], 0.0)


def shape(*dims, dtype=F32):
    return jax.ShapeDtypeStruct(dims, dtype)


TOKEN = shape(8, LANES)


def params(steps=0, limit=VMEM_LIMIT):
    return pltpu.CompilerParams(
        dimension_semantics=("arbitrary",) * steps or None, vmem_limit_bytes=limit
    )


def cost(mebibytes):
    return pl.CostEstimate(flops=0, bytes_accessed=mebibytes * 2**20, transcendentals=0)


def swap(value, axes, mask):
    axes = axes if isinstance(axes, tuple) else (axes,)
    size = math.prod(lax.axis_size(a) for a in axes)
    return lax.ppermute(value, axes, [(i, i ^ mask) for i in range(size)])


def four_sum(total, axes, one, two, work):
    first = swap(total, axes, one)
    second = swap(total, axes, two)
    third = swap(total, axes, one ^ two)
    result = None
    if work is not None:
        result, token = work(total)
        third = third + token[:1, :]
    return (total + first) + (second + third), result


def rest_sum(total, pairs):
    for axes, mask in pairs:
        total = total + swap(total, axes, mask)
    return total


def bits(axis, first):
    return [1 << i for i in range(first, lax.axis_size(axis).bit_length() - 1)]


def sum_over_devices(blocks, works):
    n = len(blocks)
    total = blocks[0]
    for d in range(1, n):
        total = total + swap(blocks[d], PLANE, d)
    far = [("gx", m) for m in bits("gx", 1)] + [("gz", m) for m in bits("gz", 2)]
    total, first = four_sum(total, PLANE, 2, 4, works[0])
    total, second = four_sum(total, "gz", 1, 2, works[1])
    total = rest_sum(total, far)
    return [total] + [swap(total, PLANE, d) for d in range(1, n)], (first, second)


def relay_part(rows_right, points, token):
    steps = 4
    rows, width = rows_right.shape
    chunk = rows // steps
    vmem = pl.BlockSpec(memory_space=pltpu.VMEM)
    high, low, token = pl.pallas_call(
        functools.partial(relay_kernel, points),
        in_specs=[pl.BlockSpec(memory_space=pl.ANY), vmem],
        out_specs=[vmem] * 3,
        out_shape=[shape(points, rows // points, width, dtype=BF16)] * 2 + [TOKEN],
        scratch_shapes=[
            pltpu.VMEM((width // LANES, steps, chunk, LANES), F32),
            pltpu.SemaphoreType.DMA((width // LANES, steps)),
        ],
        compiler_params=params(limit=47 * 1024 * 1024),
        cost_estimate=cost(8),
        name="relay_right",
    )(rows_right, token)
    return (high, low), token


def left_part(unfold, linv, token):
    steps = 4
    chunk = unfold.shape[0] // steps
    return pl.pallas_call(
        left_kernel,
        grid=(steps,),
        in_specs=[
            pl.BlockSpec((chunk, RK), lambda i: (i, 0)),
            pl.BlockSpec((RK, RK), lambda i: (0, 0)),
            pl.BlockSpec((8, LANES), lambda i: (0, 0)),
        ],
        out_specs=[
            pl.BlockSpec((chunk, RK), lambda i: (i, 0)),
            pl.BlockSpec((8, LANES), lambda i: (0, 0)),
        ],
        out_shape=[shape(unfold.shape[0], RK), TOKEN],
        compiler_params=params(1, 16 * 1024 * 1024),
        cost_estimate=cost(8),
        name="left_out",
    )(unfold, linv, token)


def right_part(absorbed, token):
    points, ranks, width = absorbed.shape
    steps = 2
    return pl.pallas_call(
        functools.partial(right_kernel, points),
        grid=(steps, 2),
        in_specs=[
            pl.BlockSpec((points, ranks // steps, LANES), lambda i, c: (0, i, c)),
            pl.BlockSpec((8, LANES), lambda i, c: (0, 0)),
        ],
        out_specs=[
            pl.BlockSpec((ranks // steps * points, LANES), lambda i, c: (i, c)),
            pl.BlockSpec((8, LANES), lambda i, c: (0, 0)),
        ],
        out_shape=[shape(ranks * points, width), TOKEN],
        compiler_params=params(2, 16 * 1024 * 1024),
        cost_estimate=cost(8),
        name="right_out",
    )(absorbed, token)


def per_device(left_core, right_core):
    rank_left, points, rank_mid = left_core.shape
    rank_right = right_core.shape[2]
    total_points = points * lax.axis_size("gx") * lax.axis_size("gy") * lax.axis_size("gz")
    unfold = left_core.reshape(rank_left * points, rank_mid)
    rows_right = right_core.reshape(rank_mid * points, rank_right)
    vmem = pl.BlockSpec(memory_space=pltpu.VMEM)

    steps = 8
    block_rows = (RK // 2 + RK + 16) // SPREAD_ONE
    blocks = pl.pallas_call(
        gram_kernel,
        in_specs=[pl.BlockSpec(memory_space=pl.ANY)],
        out_specs=[vmem] * SPREAD_ONE,
        out_shape=[shape(block_rows, LANES)] * SPREAD_ONE,
        scratch_shapes=[
            pltpu.VMEM((steps, unfold.shape[0] // steps, rank_mid), F32),
            pltpu.VMEM((rank_mid, 2 * rank_mid), F32),
            pltpu.VMEM((SPREAD_ONE * block_rows, LANES), F32),
            pltpu.SemaphoreType.DMA((steps,)),
        ],
        compiler_params=params(limit=53 * 1024 * 1024),
        name="gram_top",
    )(unfold)
    summed, (_, relayed) = sum_over_devices(
        blocks,
        [None, functools.partial(relay_part, rows_right, points)],
    )

    tall_rows = SPREAD_ONE * block_rows
    block_rows = LANES + 8
    packed_rows = SPREAD_TWO * block_rows
    absorbed, linv, *blocks = pl.pallas_call(
        functools.partial(absorb_kernel, math.sqrt(rank_left * total_points)),
        in_specs=[vmem] * (SPREAD_ONE + 2),
        out_specs=[vmem] * (2 + SPREAD_TWO),
        out_shape=[shape(points, RK, rank_right), shape(RK, RK)] + [shape(block_rows, LANES)] * SPREAD_TWO,
        scratch_shapes=[
            pltpu.VMEM((tall_rows, LANES), F32),
            pltpu.VMEM((packed_rows, LANES), F32),
            pltpu.VMEM((LANES, 3 * LANES), F32),
            pltpu.VMEM((rank_right, 2 * rank_right), F32),
        ],
        compiler_params=params(limit=24 * 1024 * 1024),
        name="factor_absorb",
    )(*summed, *relayed)
    summed, (right_out, left_out) = sum_over_devices(
        blocks,
        [
            functools.partial(right_part, absorbed),
            functools.partial(left_part, unfold, linv),
        ],
    )

    factor = pl.pallas_call(
        functools.partial(factor_kernel, 1.0 / (RK * total_points)),
        in_specs=[vmem] * SPREAD_TWO,
        out_specs=vmem,
        out_shape=shape(rank_right, rank_right),
        scratch_shapes=[
            pltpu.VMEM((packed_rows, LANES), F32),
            pltpu.VMEM((2 * LANES, 2 * LANES), F32),
        ],
        compiler_params=params(limit=16 * 1024 * 1024),
        name="factor_next",
    )(*summed)
    return (
        left_out.reshape(rank_left, points, RK),
        right_out.reshape(RK, points, rank_right),
        factor,
    )


def solution(mesh):
    in_specs = (P(None, AXES, None), P(None, AXES, None))
    out_specs = (P(None, AXES, None), P(None, AXES, None), P())
    return jax.shard_map(
        per_device, mesh=mesh, in_specs=in_specs, out_specs=out_specs, check_vma=False
    )
```

```python
import functools
import math

import jax
import jax.numpy as jnp
from jax import lax
from jax.experimental import pallas as pl
from jax.experimental.pallas import tpu as pltpu
from jax.sharding import PartitionSpec as P

RK = 128
AXES = ("gx", "gy", "gz")
LANES = 128
PANEL = 16
PLANE = ("gx", "gy")
QUARTERS = 4
SENT = 3
F32 = jnp.float32
BF16 = jnp.bfloat16
VMEM_LIMIT = 48 * 1024 * 1024


def split(x):
    hi = x.astype(BF16)
    return hi, (x - hi.astype(F32)).astype(BF16)


def dot_tn(a, b):
    return lax.dot_general(a, b, (((0,), (0,)), ((), ())), preferred_element_type=F32)


def dot_nt(a, b):
    return lax.dot_general(a, b, (((1,), (1,)), ((), ())), preferred_element_type=F32)


def dot_nn(a, b):
    return lax.dot_general(a, b, (((1,), (0,)), ((), ())), preferred_element_type=F32)


def stacked_pieces(x):
    one = x.astype(BF16).astype(F32)
    rest = x - one
    two = rest.astype(BF16).astype(F32)
    three = rest - two
    left = jnp.concatenate([one, one, two, two, one, three], axis=0).astype(BF16)
    right = jnp.concatenate([one, two, one, two, three, one], axis=0).astype(BF16)
    return left, right


def spread_row(x, k):
    return jnp.broadcast_to(x[k : k + 1, :], x.shape)


def factor_rows(w_ref, blocks):
    size = w_ref.shape[0]
    row_id = lax.broadcasted_iota(jnp.int32, (PANEL, LANES), 0)
    rows = [
        [w_ref[g : g + PANEL, b * LANES : (b + 1) * LANES] for b in range(blocks)]
        for g in range(0, size, PANEL)
    ]
    for now in range(len(rows)):
        own, lane = divmod(now * PANEL, LANES)
        panel = rows[now]
        columns = [
            jnp.broadcast_to(panel[own][:, lane + k : lane + k + 1], (PANEL, LANES))
            for k in range(PANEL)
        ]
        follows = now + 1 < len(rows)
        if follows:
            block, down = divmod((now + 1) * PANEL, LANES)
            turned = panel[block].T[down : down + PANEL, :]
            ahead = [jnp.broadcast_to(turned[:, k : k + 1], (PANEL, LANES)) for k in range(PANEL)]
        scale = jnp.zeros((PANEL, LANES), F32)
        pivot = spread_row(columns[0], 0)
        partial_pivot = spread_row(columns[1], 1)
        beneath = spread_row(columns[0], 1)
        for k in range(PANEL):
            inverse = pl.reciprocal(pivot, approx=True)
            scale = jnp.where(row_id == k, lax.rsqrt(pivot), scale)
            multiples = columns[k] * inverse
            if follows:
                ahead_multiples = ahead[k] * inverse
            entries = {m: spread_row(columns[k], m) for m in range(k + 1, PANEL)}
            pivot = partial_pivot - (beneath * inverse) * beneath
            if k + 2 < PANEL:
                second = entries[k + 2] * inverse
                beneath = spread_row(columns[k + 1], k + 2) - second * entries[k + 1]
                partial_pivot = spread_row(columns[k + 2], k + 2) - second * entries[k + 2]
            for m, entry in entries.items():
                columns[m] = columns[m] - multiples * entry
                if follows:
                    ahead[m] = ahead[m] - ahead_multiples * entry
            below = jnp.where(row_id > k, multiples, 0.0)
            for b in range(own, blocks):
                source = spread_row(panel[b], k)
                panel[b] = panel[b] - below * source
                if follows:
                    rows[now + 1][b] = rows[now + 1][b] - ahead_multiples * source
        done = [panel[b] * scale for b in range(own, blocks)]
        for b in range(own, blocks):
            w_ref[now * PANEL : (now + 1) * PANEL, b * LANES : (b + 1) * LANES] = done[b - own]
        if now + 2 < len(rows):
            both = [stacked_pieces(x) for x in done]
            left = jnp.concatenate([x[0] for x in both[: size // LANES - own]], axis=1)
            right = jnp.concatenate([x[1] for x in both], axis=1)
            update = dot_tn(left, right)
            for g in range(now + 2, len(rows)):
                top = g * PANEL - own * LANES
                for b in range(g * PANEL // LANES, blocks):
                    across = (b - own) * LANES
                    rows[g][b] = (
                        rows[g][b] - update[top : top + PANEL, across : across + LANES]
                    )


def triangle_ids():
    return (
        lax.broadcasted_iota(jnp.int32, (LANES, LANES), 0),
        lax.broadcasted_iota(jnp.int32, (LANES, LANES), 1),
    )


def store_blocks(tall_ref, own, across, pair):
    me = lax.rem(lax.axis_index(PLANE), QUARTERS)
    size = own.shape[0]
    for d, out, at in ((0, own, 0), (2, across, 0), (1, pair, 0), (3, pair, size)):
        out[at : at + size, :] = tall_ref[pl.ds(pl.multiple_of((me ^ d) * size, 8), size), :]


def load_blocks(blocks, tall_ref):
    me = lax.rem(lax.axis_index(PLANE), len(blocks))
    size = blocks[0].shape[0]
    for d, block in enumerate(blocks):
        tall_ref[pl.ds(pl.multiple_of((me ^ d) * size, 8), size), :] = block[...]


def chunk_copies(source, held, sems):
    steps, chunk = held.shape[:2]

    def copy(i):
        return pltpu.make_async_copy(
            source.at[pl.ds(i * chunk, chunk), :], held.at[i], sems.at[i]
        )

    for i in range(steps):
        copy(i).start()
    return copy


def gram_kernel(a_hbm, *refs):
    outs = refs[:SENT]
    a_ref, total_ref, tall_ref, sems = refs[SENT:]
    copy = chunk_copies(a_hbm, a_ref, sems)
    for i in range(a_ref.shape[0]):
        copy(i).wait()
        hi, lo = split(a_ref[i])
        part = dot_tn(hi, jnp.concatenate([hi, lo], axis=1))
        total_ref[...] = part if i == 0 else total_ref[...] + part
    width = a_ref.shape[2]
    cross = total_ref[:, width : width + RK]
    first = total_ref[:RK, :RK] + total_ref[:RK, width : width + RK] + cross[:RK, :].T
    row, col = triangle_ids()
    half = RK // 2
    lower = jnp.concatenate([first[half:, half:], first[half:, :half]], axis=1)
    tall_ref[:half, :] = jnp.where((row >= col)[:half, :], lower, first[:half, :])
    tall_ref[half : half + RK, :] = (
        total_ref[:RK, RK:width] + total_ref[:RK, width + RK :] + cross[RK:, :].T
    )
    diagonal = jnp.sum(jnp.where(row == col, first, 0.0), axis=0, keepdims=True)
    tail = tall_ref.shape[0] - half - RK
    tall_ref[half + RK :, :] = jnp.broadcast_to(diagonal, (tail, LANES))
    store_blocks(tall_ref, *outs)


def relay_kernel(points, r_hbm, _, hi_ref, lo_ref, token_ref, r_ref, sems):
    token_ref[...] = jnp.zeros_like(token_ref)
    halves, steps, chunk, _ = r_ref.shape
    ranks = chunk // points

    def copy(c, i):
        return pltpu.make_async_copy(
            r_hbm.at[pl.ds(i * chunk, chunk), pl.ds(c * LANES, LANES)],
            r_ref.at[c, i],
            sems.at[c, i],
        )

    for i in range(steps):
        for c in range(halves):
            copy(c, i).start()

    def body(i, carry):
        for c in range(halves):
            copy(c, i).wait()
            for p in range(points):
                hi, lo = split(r_ref[c, i, pl.ds(p, ranks, stride=points), :])
                place = pl.ds(pl.multiple_of(i * ranks, ranks), ranks)
                hi_ref[p, place, c * LANES : (c + 1) * LANES] = hi
                lo_ref[p, place, c * LANES : (c + 1) * LANES] = lo
        return carry

    lax.fori_loop(0, steps, body, 0)


def absorb_kernel(scale, *refs):
    blocks, refs = refs[:QUARTERS], refs[QUARTERS:]
    hi_ref, lo_ref, absorbed_ref, linv_ref = refs[:4]
    outs = refs[4 : 4 + SENT]
    tall_ref, pack_ref, w_ref, total_ref = refs[4 + SENT :]
    row, col = triangle_ids()
    load_blocks(blocks, tall_ref)
    half = RK // 2
    top = tall_ref[:half, :]
    mixed = jnp.concatenate(
        [top, jnp.concatenate([top[:, half:], top[:, :half]], axis=1)], axis=0
    )
    sent = ((row < half) & (col > row)) | ((col >= half) & (row > col))
    diagonal = jnp.broadcast_to(tall_ref[half + RK : half + RK + 1, :], (LANES, LANES))
    w_ref[:, :LANES] = jnp.where(sent, mixed, jnp.where(row == col, diagonal, mixed.T))
    w_ref[:, LANES : 2 * LANES] = tall_ref[half : half + RK, :]
    w_ref[:, 2 * LANES :] = jnp.where(row == col, 1.0, 0.0).astype(F32)
    factor_rows(w_ref, 3)
    linv_ref[...] = w_ref[:, 2 * LANES :] * scale
    upper = jnp.concatenate(
        [jnp.where(col >= row, w_ref[:, :LANES], 0.0), w_ref[:, LANES : 2 * LANES]], axis=1
    )
    upper_hi, upper_lo = split(upper)
    upper_both = jnp.concatenate([upper_hi, upper_lo], axis=0)
    points = absorbed_ref.shape[0]
    group = 4
    for step in range(points // group):
        pieces = []
        for i in range(group):
            p = step * group + i
            first = dot_nn(upper_both, hi_ref[p])
            b = first[:RK, :] + first[RK:, :] + dot_nn(upper_hi, lo_ref[p])
            absorbed_ref[p] = b
            pieces.append(split(b))
        b_hi = jnp.concatenate([x[0] for x in pieces], axis=0)
        b_lo = jnp.concatenate([x[1] for x in pieces], axis=0)
        part = dot_tn(b_hi, jnp.concatenate([b_hi, b_lo], axis=1))
        total_ref[...] = part if step == 0 else total_ref[...] + part
    cross = total_ref[:, 256:]
    gram = total_ref[:, :256] + cross + cross.T
    lower_right = gram[LANES:, LANES:]
    pack_ref[:LANES, :] = jnp.where(col >= row, gram[:LANES, :LANES], lower_right)
    pack_ref[LANES : 2 * LANES, :] = gram[:LANES, LANES:]
    diagonal = jnp.sum(jnp.where(row == col, lower_right, 0.0), axis=0, keepdims=True)
    tail = pack_ref.shape[0] - 2 * LANES
    pack_ref[2 * LANES :, :] = jnp.broadcast_to(diagonal, (tail, LANES))
    store_blocks(pack_ref, *outs)


def left_kernel(a_ref, linv_ref, _, left_ref, token_ref):
    l_hi, l_lo = split(linv_ref[...])
    hi, lo = split(a_ref[...])
    left_ref[...] = dot_nt(hi, l_hi) + dot_nt(hi, l_lo) + dot_nt(lo, l_hi)
    token_ref[...] = jnp.zeros_like(token_ref)


def right_kernel(points, absorbed_ref, _, right_ref, token_ref):
    count = absorbed_ref.shape[1]
    for p in range(points):
        right_ref[pl.ds(p, count, stride=points), :] = absorbed_ref[p]
    token_ref[...] = jnp.zeros_like(token_ref)


def factor_kernel(scale, *refs):
    blocks, (out_ref, pack_ref, w_ref) = refs[:QUARTERS], refs[QUARTERS:]
    load_blocks(blocks, pack_ref)
    row, col = triangle_ids()
    packed = pack_ref[:LANES, :] * scale
    turned = packed.T
    diagonal = jnp.broadcast_to(pack_ref[2 * LANES : 2 * LANES + 1, :], (LANES, LANES)) * scale
    w_ref[:LANES, :LANES] = jnp.where(col >= row, packed, turned)
    w_ref[:LANES, LANES:] = pack_ref[LANES : 2 * LANES, :] * scale
    w_ref[LANES:, :LANES] = jnp.zeros((LANES, LANES), F32)
    w_ref[LANES:, LANES:] = jnp.where(row > col, packed, jnp.where(row == col, diagonal, turned))
    factor_rows(w_ref, 2)
    out_ref[:LANES, :LANES] = jnp.where(col >= row, w_ref[:LANES, :LANES], 0.0)
    out_ref[:LANES, LANES:] = w_ref[:LANES, LANES:]
    out_ref[LANES:, :LANES] = jnp.zeros((LANES, LANES), F32)
    out_ref[LANES:, LANES:] = jnp.where(col >= row, w_ref[LANES:, LANES:], 0.0)


def shape(*dims, dtype=F32):
    return jax.ShapeDtypeStruct(dims, dtype)


def quarter_shapes(rows):
    return [shape(rows, LANES), shape(rows, LANES), shape(2 * rows, LANES)]


TOKEN = shape(8, LANES)


def params(steps=0, limit=VMEM_LIMIT):
    return pltpu.CompilerParams(
        dimension_semantics=("arbitrary",) * steps or None, vmem_limit_bytes=limit
    )


def cost(mebibytes):
    return pl.CostEstimate(flops=0, bytes_accessed=mebibytes * 2**20, transcendentals=0)


def swap(value, axes, mask):
    axes = axes if isinstance(axes, tuple) else (axes,)
    size = math.prod(lax.axis_size(a) for a in axes)
    return lax.ppermute(value, axes, [(i, i ^ mask) for i in range(size)])


def four_sum(total, moves, work):
    first, second, third = [swap(*move) for move in moves]
    result = None
    if work is not None:
        result, token = work(total)
        third = third + token[:1, :]
    return (total + first) + (second + third), result


def rest_sum(total, pairs):
    for axes, mask in pairs:
        total = total + swap(total, axes, mask)
    return total


def bits(axis, first):
    return [1 << i for i in range(first, lax.axis_size(axis).bit_length() - 1)]


def sum_over_devices(parts, works):
    own, across, pair = parts
    size = own.shape[0]
    received = swap(pair, PLANE, 1)
    own, across = own + received[:size], across + received[size:]
    moves = [(across, PLANE, 2), (own, PLANE, 4), (across, PLANE, 6)]
    total, first = four_sum(own, moves, works[0])
    total, second = four_sum(total, [(total, "gz", m) for m in (1, 2, 3)], works[1])
    total = rest_sum(
        total, [("gx", m) for m in bits("gx", 1)] + [("gz", m) for m in bits("gz", 2)]
    )
    return [total] + [swap(total, PLANE, d) for d in range(1, QUARTERS)], (first, second)


def relay_part(rows_right, points, token):
    steps = 4
    rows, width = rows_right.shape
    chunk = rows // steps
    vmem = pl.BlockSpec(memory_space=pltpu.VMEM)
    high, low, token = pl.pallas_call(
        functools.partial(relay_kernel, points),
        in_specs=[pl.BlockSpec(memory_space=pl.ANY), vmem],
        out_specs=[vmem] * 3,
        out_shape=[shape(points, rows // points, width, dtype=BF16)] * 2 + [TOKEN],
        scratch_shapes=[
            pltpu.VMEM((width // LANES, steps, chunk, LANES), F32),
            pltpu.SemaphoreType.DMA((width // LANES, steps)),
        ],
        compiler_params=params(limit=47 * 1024 * 1024),
        cost_estimate=cost(8),
        name="relay_right",
    )(rows_right, token)
    return (high, low), token


def left_part(unfold, linv, token):
    steps = 4
    chunk = unfold.shape[0] // steps
    return pl.pallas_call(
        left_kernel,
        grid=(steps,),
        in_specs=[
            pl.BlockSpec((chunk, RK), lambda i: (i, 0)),
            pl.BlockSpec((RK, RK), lambda i: (0, 0)),
            pl.BlockSpec((8, LANES), lambda i: (0, 0)),
        ],
        out_specs=[
            pl.BlockSpec((chunk, RK), lambda i: (i, 0)),
            pl.BlockSpec((8, LANES), lambda i: (0, 0)),
        ],
        out_shape=[shape(unfold.shape[0], RK), TOKEN],
        compiler_params=params(1, 16 * 1024 * 1024),
        cost_estimate=cost(8),
        name="left_out",
    )(unfold, linv, token)


def right_part(absorbed, token):
    points, ranks, width = absorbed.shape
    steps = 2
    return pl.pallas_call(
        functools.partial(right_kernel, points),
        grid=(steps, 2),
        in_specs=[
            pl.BlockSpec((points, ranks // steps, LANES), lambda i, c: (0, i, c)),
            pl.BlockSpec((8, LANES), lambda i, c: (0, 0)),
        ],
        out_specs=[
            pl.BlockSpec((ranks // steps * points, LANES), lambda i, c: (i, c)),
            pl.BlockSpec((8, LANES), lambda i, c: (0, 0)),
        ],
        out_shape=[shape(ranks * points, width), TOKEN],
        compiler_params=params(2, 16 * 1024 * 1024),
        cost_estimate=cost(8),
        name="right_out",
    )(absorbed, token)


def per_device(left_core, right_core):
    rank_left, points, rank_mid = left_core.shape
    rank_right = right_core.shape[2]
    total_points = points * lax.axis_size("gx") * lax.axis_size("gy") * lax.axis_size("gz")
    unfold = left_core.reshape(rank_left * points, rank_mid)
    rows_right = right_core.reshape(rank_mid * points, rank_right)
    vmem = pl.BlockSpec(memory_space=pltpu.VMEM)

    steps = 8
    block_rows = (RK // 2 + RK + 32) // QUARTERS
    blocks = pl.pallas_call(
        gram_kernel,
        in_specs=[pl.BlockSpec(memory_space=pl.ANY)],
        out_specs=[vmem] * SENT,
        out_shape=quarter_shapes(block_rows),
        scratch_shapes=[
            pltpu.VMEM((steps, unfold.shape[0] // steps, rank_mid), F32),
            pltpu.VMEM((rank_mid, 2 * rank_mid), F32),
            pltpu.VMEM((QUARTERS * block_rows, LANES), F32),
            pltpu.SemaphoreType.DMA((steps,)),
        ],
        compiler_params=params(limit=53 * 1024 * 1024),
        name="gram_top",
    )(unfold)
    summed, (_, relayed) = sum_over_devices(
        blocks,
        [None, functools.partial(relay_part, rows_right, points)],
    )

    tall_rows = QUARTERS * block_rows
    block_rows = (2 * LANES + 32) // QUARTERS
    packed_rows = QUARTERS * block_rows
    absorbed, linv, *blocks = pl.pallas_call(
        functools.partial(absorb_kernel, math.sqrt(rank_left * total_points)),
        in_specs=[vmem] * (QUARTERS + 2),
        out_specs=[vmem] * (2 + SENT),
        out_shape=[shape(points, RK, rank_right), shape(RK, RK)] + quarter_shapes(block_rows),
        scratch_shapes=[
            pltpu.VMEM((tall_rows, LANES), F32),
            pltpu.VMEM((packed_rows, LANES), F32),
            pltpu.VMEM((LANES, 3 * LANES), F32),
            pltpu.VMEM((rank_right, 2 * rank_right), F32),
        ],
        compiler_params=params(limit=24 * 1024 * 1024),
        name="factor_absorb",
    )(*summed, *relayed)
    summed, (right_out, left_out) = sum_over_devices(
        blocks,
        [
            functools.partial(right_part, absorbed),
            functools.partial(left_part, unfold, linv),
        ],
    )

    factor = pl.pallas_call(
        functools.partial(factor_kernel, 1.0 / (RK * total_points)),
        in_specs=[vmem] * QUARTERS,
        out_specs=vmem,
        out_shape=shape(rank_right, rank_right),
        scratch_shapes=[
            pltpu.VMEM((packed_rows, LANES), F32),
            pltpu.VMEM((2 * LANES, 2 * LANES), F32),
        ],
        compiler_params=params(limit=16 * 1024 * 1024),
        name="factor_next",
    )(*summed)
    return (
        left_out.reshape(rank_left, points, RK),
        right_out.reshape(RK, points, rank_right),
        factor,
    )


def solution(mesh):
    in_specs = (P(None, AXES, None), P(None, AXES, None))
    out_specs = (P(None, AXES, None), P(None, AXES, None), P())
    return jax.shard_map(
        per_device, mesh=mesh, in_specs=in_specs, out_specs=out_specs, check_vma=False
    )
```

```python
import functools
import math

import jax
import jax.numpy as jnp
from jax import lax
from jax.experimental import pallas as pl
from jax.experimental.pallas import tpu as pltpu
from jax.sharding import PartitionSpec as P

RK = 128
AXES = ("gx", "gy", "gz")
LANES = 128
PANEL = 16
PLANE = ("gx", "gy")
SPREAD_ONE = 2
SPREAD_TWO = 2
F32 = jnp.float32
BF16 = jnp.bfloat16
VMEM_LIMIT = 48 * 1024 * 1024


def split(x):
    hi = x.astype(BF16)
    return hi, (x - hi.astype(F32)).astype(BF16)


def dot_tn(a, b):
    return lax.dot_general(a, b, (((0,), (0,)), ((), ())), preferred_element_type=F32)


def dot_nt(a, b):
    return lax.dot_general(a, b, (((1,), (1,)), ((), ())), preferred_element_type=F32)


def dot_nn(a, b):
    return lax.dot_general(a, b, (((1,), (0,)), ((), ())), preferred_element_type=F32)


def stacked_pieces(x):
    one = x.astype(BF16).astype(F32)
    rest = x - one
    two = rest.astype(BF16).astype(F32)
    three = rest - two
    left = jnp.concatenate([one, one, two, two, one, three], axis=0).astype(BF16)
    right = jnp.concatenate([one, two, one, two, three, one], axis=0).astype(BF16)
    return left, right


def spread_row(x, k):
    return jnp.broadcast_to(x[k : k + 1, :], x.shape)


def factor_rows(w_ref, blocks):
    size = w_ref.shape[0]
    row_id = lax.broadcasted_iota(jnp.int32, (PANEL, LANES), 0)
    rows = [
        [w_ref[g : g + PANEL, b * LANES : (b + 1) * LANES] for b in range(blocks)]
        for g in range(0, size, PANEL)
    ]
    for now in range(len(rows)):
        own, lane = divmod(now * PANEL, LANES)
        panel = rows[now]
        columns = [
            jnp.broadcast_to(panel[own][:, lane + k : lane + k + 1], (PANEL, LANES))
            for k in range(PANEL)
        ]
        follows = now + 1 < len(rows)
        if follows:
            block, down = divmod((now + 1) * PANEL, LANES)
            turned = panel[block].T[down : down + PANEL, :]
            ahead = [jnp.broadcast_to(turned[:, k : k + 1], (PANEL, LANES)) for k in range(PANEL)]
        scale = jnp.zeros((PANEL, LANES), F32)
        pivot = spread_row(columns[0], 0)
        partial_pivot = spread_row(columns[1], 1)
        beneath = spread_row(columns[0], 1)
        for k in range(PANEL):
            inverse = pl.reciprocal(pivot, approx=True)
            scale = jnp.where(row_id == k, lax.rsqrt(pivot), scale)
            multiples = columns[k] * inverse
            if follows:
                ahead_multiples = ahead[k] * inverse
            entries = {m: spread_row(columns[k], m) for m in range(k + 1, PANEL)}
            pivot = partial_pivot - (beneath * inverse) * beneath
            if k + 2 < PANEL:
                second = entries[k + 2] * inverse
                beneath = spread_row(columns[k + 1], k + 2) - second * entries[k + 1]
                partial_pivot = spread_row(columns[k + 2], k + 2) - second * entries[k + 2]
            for m, entry in entries.items():
                columns[m] = columns[m] - multiples * entry
                if follows:
                    ahead[m] = ahead[m] - ahead_multiples * entry
            below = jnp.where(row_id > k, multiples, 0.0)
            for b in range(own, blocks):
                source = spread_row(panel[b], k)
                panel[b] = panel[b] - below * source
                if follows:
                    rows[now + 1][b] = rows[now + 1][b] - ahead_multiples * source
        done = [panel[b] * scale for b in range(own, blocks)]
        for b in range(own, blocks):
            w_ref[now * PANEL : (now + 1) * PANEL, b * LANES : (b + 1) * LANES] = done[b - own]
        if now + 2 < len(rows):
            both = [stacked_pieces(x) for x in done]
            left = jnp.concatenate([x[0] for x in both[: size // LANES - own]], axis=1)
            right = jnp.concatenate([x[1] for x in both], axis=1)
            update = dot_tn(left, right)
            for g in range(now + 2, len(rows)):
                top = g * PANEL - own * LANES
                for b in range(g * PANEL // LANES, blocks):
                    across = (b - own) * LANES
                    rows[g][b] = (
                        rows[g][b] - update[top : top + PANEL, across : across + LANES]
                    )


def triangle_ids():
    return (
        lax.broadcasted_iota(jnp.int32, (LANES, LANES), 0),
        lax.broadcasted_iota(jnp.int32, (LANES, LANES), 1),
    )


def store_blocks(tall_ref, outs):
    me = lax.rem(lax.axis_index(PLANE), len(outs))
    size = outs[0].shape[0]
    for d, out in enumerate(outs):
        out[...] = tall_ref[pl.ds(pl.multiple_of((me ^ d) * size, 8), size), :]


def load_blocks(blocks, tall_ref):
    me = lax.rem(lax.axis_index(PLANE), len(blocks))
    size = blocks[0].shape[0]
    for d, block in enumerate(blocks):
        tall_ref[pl.ds(pl.multiple_of((me ^ d) * size, 8), size), :] = block[...]


def chunk_copies(source, held, sems):
    steps, chunk = held.shape[:2]

    def copy(i):
        return pltpu.make_async_copy(
            source.at[pl.ds(i * chunk, chunk), :], held.at[i], sems.at[i]
        )

    for i in range(steps):
        copy(i).start()
    return copy


def gram_kernel(a_hbm, *refs):
    outs = refs[:SPREAD_ONE]
    a_ref, total_ref, tall_ref, sems = refs[SPREAD_ONE:]
    copy = chunk_copies(a_hbm, a_ref, sems)
    for i in range(a_ref.shape[0]):
        copy(i).wait()
        hi, lo = split(a_ref[i])
        part = dot_tn(hi, jnp.concatenate([hi, lo], axis=1))
        total_ref[...] = part if i == 0 else total_ref[...] + part
    width = a_ref.shape[2]
    cross = total_ref[:, width : width + RK]
    first = total_ref[:RK, :RK] + total_ref[:RK, width : width + RK] + cross[:RK, :].T
    row, col = triangle_ids()
    half = RK // 2
    lower = jnp.concatenate([first[half:, half:], first[half:, :half]], axis=1)
    tall_ref[:half, :] = jnp.where((row >= col)[:half, :], lower, first[:half, :])
    tall_ref[half : half + RK, :] = (
        total_ref[:RK, RK:width] + total_ref[:RK, width + RK :] + cross[RK:, :].T
    )
    diagonal = jnp.sum(jnp.where(row == col, first, 0.0), axis=0, keepdims=True)
    tail = tall_ref.shape[0] - half - RK
    tall_ref[half + RK :, :] = jnp.broadcast_to(diagonal, (tail, LANES))
    store_blocks(tall_ref, outs)


def relay_kernel(points, r_hbm, _, hi_ref, lo_ref, token_ref, r_ref, sems):
    token_ref[...] = jnp.zeros_like(token_ref)
    halves, steps, chunk, _ = r_ref.shape
    ranks = chunk // points

    def copy(c, i):
        return pltpu.make_async_copy(
            r_hbm.at[pl.ds(i * chunk, chunk), pl.ds(c * LANES, LANES)],
            r_ref.at[c, i],
            sems.at[c, i],
        )

    for i in range(steps):
        for c in range(halves):
            copy(c, i).start()

    def body(i, carry):
        for c in range(halves):
            copy(c, i).wait()
            for p in range(points):
                hi, lo = split(r_ref[c, i, pl.ds(p, ranks, stride=points), :])
                place = pl.ds(pl.multiple_of(i * ranks, ranks), ranks)
                hi_ref[p, place, c * LANES : (c + 1) * LANES] = hi
                lo_ref[p, place, c * LANES : (c + 1) * LANES] = lo
        return carry

    lax.fori_loop(0, steps, body, 0)


def absorb_kernel(scale, *refs):
    blocks, refs = refs[:SPREAD_ONE], refs[SPREAD_ONE:]
    hi_ref, lo_ref, absorbed_ref, linv_ref = refs[:4]
    outs = refs[4 : 4 + SPREAD_TWO]
    tall_ref, pack_ref, w_ref, total_ref = refs[4 + SPREAD_TWO :]
    row, col = triangle_ids()
    load_blocks(blocks, tall_ref)
    half = RK // 2
    top = tall_ref[:half, :]
    mixed = jnp.concatenate(
        [top, jnp.concatenate([top[:, half:], top[:, :half]], axis=1)], axis=0
    )
    sent = ((row < half) & (col > row)) | ((col >= half) & (row > col))
    diagonal = jnp.broadcast_to(tall_ref[half + RK : half + RK + 1, :], (LANES, LANES))
    w_ref[:, :LANES] = jnp.where(sent, mixed, jnp.where(row == col, diagonal, mixed.T))
    w_ref[:, LANES : 2 * LANES] = tall_ref[half : half + RK, :]
    w_ref[:, 2 * LANES :] = jnp.where(row == col, 1.0, 0.0).astype(F32)
    factor_rows(w_ref, 3)
    linv_ref[...] = w_ref[:, 2 * LANES :] * scale
    upper = jnp.concatenate(
        [jnp.where(col >= row, w_ref[:, :LANES], 0.0), w_ref[:, LANES : 2 * LANES]], axis=1
    )
    upper_hi, upper_lo = split(upper)
    upper_both = jnp.concatenate([upper_hi, upper_lo], axis=0)
    points = absorbed_ref.shape[0]
    group = 4
    for step in range(points // group):
        pieces = []
        for i in range(group):
            p = step * group + i
            first = dot_nn(upper_both, hi_ref[p])
            b = first[:RK, :] + first[RK:, :] + dot_nn(upper_hi, lo_ref[p])
            absorbed_ref[p] = b
            pieces.append(split(b))
        b_hi = jnp.concatenate([x[0] for x in pieces], axis=0)
        b_lo = jnp.concatenate([x[1] for x in pieces], axis=0)
        part = dot_tn(b_hi, jnp.concatenate([b_hi, b_lo], axis=1))
        total_ref[...] = part if step == 0 else total_ref[...] + part
    cross = total_ref[:, 256:]
    gram = total_ref[:, :256] + cross + cross.T
    lower_right = gram[LANES:, LANES:]
    pack_ref[:LANES, :] = jnp.where(col >= row, gram[:LANES, :LANES], lower_right)
    pack_ref[LANES : 2 * LANES, :] = gram[:LANES, LANES:]
    diagonal = jnp.sum(jnp.where(row == col, lower_right, 0.0), axis=0, keepdims=True)
    tail = pack_ref.shape[0] - 2 * LANES
    pack_ref[2 * LANES :, :] = jnp.broadcast_to(diagonal, (tail, LANES))
    store_blocks(pack_ref, outs)


def left_kernel(a_ref, linv_ref, _, left_ref, token_ref):
    l_hi, l_lo = split(linv_ref[...])
    hi, lo = split(a_ref[...])
    left_ref[...] = dot_nt(hi, l_hi) + dot_nt(hi, l_lo) + dot_nt(lo, l_hi)
    token_ref[...] = jnp.zeros_like(token_ref)


def right_kernel(points, absorbed_ref, _, right_ref, token_ref):
    count = absorbed_ref.shape[1]
    for p in range(points):
        right_ref[pl.ds(p, count, stride=points), :] = absorbed_ref[p]
    token_ref[...] = jnp.zeros_like(token_ref)


def factor_kernel(scale, *refs):
    blocks, (out_ref, pack_ref, w_ref) = refs[:SPREAD_TWO], refs[SPREAD_TWO:]
    load_blocks(blocks, pack_ref)
    row, col = triangle_ids()
    packed = pack_ref[:LANES, :] * scale
    turned = packed.T
    diagonal = jnp.broadcast_to(pack_ref[2 * LANES : 2 * LANES + 1, :], (LANES, LANES)) * scale
    w_ref[:LANES, :LANES] = jnp.where(col >= row, packed, turned)
    w_ref[:LANES, LANES:] = pack_ref[LANES : 2 * LANES, :] * scale
    w_ref[LANES:, :LANES] = jnp.zeros((LANES, LANES), F32)
    w_ref[LANES:, LANES:] = jnp.where(row > col, packed, jnp.where(row == col, diagonal, turned))
    factor_rows(w_ref, 2)
    out_ref[:LANES, :LANES] = jnp.where(col >= row, w_ref[:LANES, :LANES], 0.0)
    out_ref[:LANES, LANES:] = w_ref[:LANES, LANES:]
    out_ref[LANES:, :LANES] = jnp.zeros((LANES, LANES), F32)
    out_ref[LANES:, LANES:] = jnp.where(col >= row, w_ref[LANES:, LANES:], 0.0)


def shape(*dims, dtype=F32):
    return jax.ShapeDtypeStruct(dims, dtype)


TOKEN = shape(8, LANES)


def params(steps=0, limit=VMEM_LIMIT):
    return pltpu.CompilerParams(
        dimension_semantics=("arbitrary",) * steps or None, vmem_limit_bytes=limit
    )


def cost(mebibytes):
    return pl.CostEstimate(flops=0, bytes_accessed=mebibytes * 2**20, transcendentals=0)


def swap(value, axes, mask):
    axes = axes if isinstance(axes, tuple) else (axes,)
    size = math.prod(lax.axis_size(a) for a in axes)
    return lax.ppermute(value, axes, [(i, i ^ mask) for i in range(size)])


def four_sum(total, axes, one, two, work):
    first = swap(total, axes, one)
    second = swap(total, axes, two)
    third = swap(total, axes, one ^ two)
    result = None
    if work is not None:
        result, token = work(total)
        third = third + token[:1, :]
    return (total + first) + (second + third), result


def rest_sum(total, pairs):
    for axes, mask in pairs:
        total = total + swap(total, axes, mask)
    return total


def bits(axis, first):
    return [1 << i for i in range(first, lax.axis_size(axis).bit_length() - 1)]


def sum_over_devices(blocks, works):
    n = len(blocks)
    total = blocks[0]
    for d in range(1, n):
        total = total + swap(blocks[d], PLANE, d)
    far = [("gx", m) for m in bits("gx", 1)] + [("gz", m) for m in bits("gz", 2)]
    total, first = four_sum(total, PLANE, 2, 4, works[0])
    total, second = four_sum(total, "gz", 1, 2, works[1])
    total = rest_sum(total, far)
    return [total] + [swap(total, PLANE, d) for d in range(1, n)], (first, second)


def relay_part(rows_right, points, token):
    steps = 4
    rows, width = rows_right.shape
    chunk = rows // steps
    vmem = pl.BlockSpec(memory_space=pltpu.VMEM)
    high, low, token = pl.pallas_call(
        functools.partial(relay_kernel, points),
        in_specs=[pl.BlockSpec(memory_space=pl.ANY), vmem],
        out_specs=[vmem] * 3,
        out_shape=[shape(points, rows // points, width, dtype=BF16)] * 2 + [TOKEN],
        scratch_shapes=[
            pltpu.VMEM((width // LANES, steps, chunk, LANES), F32),
            pltpu.SemaphoreType.DMA((width // LANES, steps)),
        ],
        compiler_params=params(limit=47 * 1024 * 1024),
        cost_estimate=cost(8),
        name="relay_right",
    )(rows_right, token)
    return (high, low), token


def left_part(unfold, linv, token):
    steps = 4
    chunk = unfold.shape[0] // steps
    return pl.pallas_call(
        left_kernel,
        grid=(steps,),
        in_specs=[
            pl.BlockSpec((chunk, RK), lambda i: (i, 0)),
            pl.BlockSpec((RK, RK), lambda i: (0, 0)),
            pl.BlockSpec((8, LANES), lambda i: (0, 0)),
        ],
        out_specs=[
            pl.BlockSpec((chunk, RK), lambda i: (i, 0)),
            pl.BlockSpec((8, LANES), lambda i: (0, 0)),
        ],
        out_shape=[shape(unfold.shape[0], RK), TOKEN],
        compiler_params=params(1, 16 * 1024 * 1024),
        cost_estimate=cost(8),
        name="left_out",
    )(unfold, linv, token)


def right_part(absorbed, token):
    points, ranks, width = absorbed.shape
    steps = 2
    return pl.pallas_call(
        functools.partial(right_kernel, points),
        grid=(steps, 2),
        in_specs=[
            pl.BlockSpec((points, ranks // steps, LANES), lambda i, c: (0, i, c)),
            pl.BlockSpec((8, LANES), lambda i, c: (0, 0)),
        ],
        out_specs=[
            pl.BlockSpec((ranks // steps * points, LANES), lambda i, c: (i, c)),
            pl.BlockSpec((8, LANES), lambda i, c: (0, 0)),
        ],
        out_shape=[shape(ranks * points, width), TOKEN],
        compiler_params=params(2, 16 * 1024 * 1024),
        cost_estimate=cost(8),
        name="right_out",
    )(absorbed, token)


def per_device(left_core, right_core):
    rank_left, points, rank_mid = left_core.shape
    rank_right = right_core.shape[2]
    total_points = points * lax.axis_size("gx") * lax.axis_size("gy") * lax.axis_size("gz")
    unfold = left_core.reshape(rank_left * points, rank_mid)
    rows_right = right_core.reshape(rank_mid * points, rank_right)
    vmem = pl.BlockSpec(memory_space=pltpu.VMEM)

    steps = 8
    block_rows = (RK // 2 + RK + 16) // SPREAD_ONE
    blocks = pl.pallas_call(
        gram_kernel,
        in_specs=[pl.BlockSpec(memory_space=pl.ANY)],
        out_specs=[vmem] * SPREAD_ONE,
        out_shape=[shape(block_rows, LANES)] * SPREAD_ONE,
        scratch_shapes=[
            pltpu.VMEM((steps, unfold.shape[0] // steps, rank_mid), F32),
            pltpu.VMEM((rank_mid, 2 * rank_mid), F32),
            pltpu.VMEM((SPREAD_ONE * block_rows, LANES), F32),
            pltpu.SemaphoreType.DMA((steps,)),
        ],
        compiler_params=params(limit=53 * 1024 * 1024),
        name="gram_top",
    )(unfold)
    summed, (_, relayed) = sum_over_devices(
        blocks,
        [None, functools.partial(relay_part, rows_right, points)],
    )

    tall_rows = SPREAD_ONE * block_rows
    block_rows = LANES + 8
    packed_rows = SPREAD_TWO * block_rows
    absorbed, linv, *blocks = pl.pallas_call(
        functools.partial(absorb_kernel, math.sqrt(rank_left * total_points)),
        in_specs=[vmem] * (SPREAD_ONE + 2),
        out_specs=[vmem] * (2 + SPREAD_TWO),
        out_shape=[shape(points, RK, rank_right), shape(RK, RK)] + [shape(block_rows, LANES)] * SPREAD_TWO,
        scratch_shapes=[
            pltpu.VMEM((tall_rows, LANES), F32),
            pltpu.VMEM((packed_rows, LANES), F32),
            pltpu.VMEM((LANES, 3 * LANES), F32),
            pltpu.VMEM((rank_right, 2 * rank_right), F32),
        ],
        compiler_params=params(limit=24 * 1024 * 1024),
        name="factor_absorb",
    )(*summed, *relayed)
    summed, (right_out, left_out) = sum_over_devices(
        blocks,
        [
            functools.partial(right_part, absorbed),
            functools.partial(left_part, unfold, linv),
        ],
    )

    factor = pl.pallas_call(
        functools.partial(factor_kernel, 1.0 / (RK * total_points)),
        in_specs=[vmem] * SPREAD_TWO,
        out_specs=vmem,
        out_shape=shape(rank_right, rank_right),
        scratch_shapes=[
            pltpu.VMEM((packed_rows, LANES), F32),
            pltpu.VMEM((2 * LANES, 2 * LANES), F32),
        ],
        compiler_params=params(limit=16 * 1024 * 1024),
        name="factor_next",
    )(*summed)
    return (
        left_out.reshape(rank_left, points, RK),
        right_out.reshape(RK, points, rank_right),
        factor,
    )


def solution(mesh):
    in_specs = (P(None, AXES, None), P(None, AXES, None))
    out_specs = (P(None, AXES, None), P(None, AXES, None), P())
    return jax.shard_map(
        per_device, mesh=mesh, in_specs=in_specs, out_specs=out_specs, check_vma=False
    )
```

```python
import functools
import math

import jax
import jax.numpy as jnp
from jax import lax
from jax.experimental import pallas as pl
from jax.experimental.pallas import tpu as pltpu
from jax.sharding import PartitionSpec as P

RK = 128
AXES = ("gx", "gy", "gz")
LANES = 128
PANEL = 16
PLANE = ("gx", "gy")
SPREAD_ONE = 2
SPREAD_TWO = 2
F32 = jnp.float32
BF16 = jnp.bfloat16
VMEM_LIMIT = 48 * 1024 * 1024


def split(x):
    hi = x.astype(BF16)
    return hi, (x - hi.astype(F32)).astype(BF16)


def dot_tn(a, b):
    return lax.dot_general(a, b, (((0,), (0,)), ((), ())), preferred_element_type=F32)


def dot_nt(a, b):
    return lax.dot_general(a, b, (((1,), (1,)), ((), ())), preferred_element_type=F32)


def dot_nn(a, b):
    return lax.dot_general(a, b, (((1,), (0,)), ((), ())), preferred_element_type=F32)


def stacked_pieces(x):
    one = x.astype(BF16).astype(F32)
    rest = x - one
    two = rest.astype(BF16).astype(F32)
    three = rest - two
    left = jnp.concatenate([one, one, two, two, one, three], axis=0).astype(BF16)
    right = jnp.concatenate([one, two, one, two, three, one], axis=0).astype(BF16)
    return left, right


def spread_row(x, k):
    return jnp.broadcast_to(x[k : k + 1, :], x.shape)


def factor_rows(w_ref, blocks):
    size = w_ref.shape[0]
    row_id = lax.broadcasted_iota(jnp.int32, (PANEL, LANES), 0)
    rows = [
        [w_ref[g : g + PANEL, b * LANES : (b + 1) * LANES] for b in range(blocks)]
        for g in range(0, size, PANEL)
    ]
    for now in range(len(rows)):
        own, lane = divmod(now * PANEL, LANES)
        panel = rows[now]
        columns = [
            jnp.broadcast_to(panel[own][:, lane + k : lane + k + 1], (PANEL, LANES))
            for k in range(PANEL)
        ]
        follows = now + 1 < len(rows)
        if follows:
            block, down = divmod((now + 1) * PANEL, LANES)
            turned = panel[block].T[down : down + PANEL, :]
            ahead = [jnp.broadcast_to(turned[:, k : k + 1], (PANEL, LANES)) for k in range(PANEL)]
        scale = jnp.zeros((PANEL, LANES), F32)
        pivot = spread_row(columns[0], 0)
        partial_pivot = spread_row(columns[1], 1)
        beneath = spread_row(columns[0], 1)
        for k in range(PANEL):
            inverse = pl.reciprocal(pivot, approx=True)
            scale = jnp.where(row_id == k, lax.rsqrt(pivot), scale)
            multiples = columns[k] * inverse
            if follows:
                ahead_multiples = ahead[k] * inverse
            entries = {m: spread_row(columns[k], m) for m in range(k + 1, PANEL)}
            pivot = partial_pivot - (beneath * inverse) * beneath
            if k + 2 < PANEL:
                second = entries[k + 2] * inverse
                beneath = spread_row(columns[k + 1], k + 2) - second * entries[k + 1]
                partial_pivot = spread_row(columns[k + 2], k + 2) - second * entries[k + 2]
            for m, entry in entries.items():
                columns[m] = columns[m] - multiples * entry
                if follows:
                    ahead[m] = ahead[m] - ahead_multiples * entry
            below = jnp.where(row_id > k, multiples, 0.0)
            for b in range(own, blocks):
                source = spread_row(panel[b], k)
                panel[b] = panel[b] - below * source
                if follows:
                    rows[now + 1][b] = rows[now + 1][b] - ahead_multiples * source
        done = [panel[b] * scale for b in range(own, blocks)]
        for b in range(own, blocks):
            w_ref[now * PANEL : (now + 1) * PANEL, b * LANES : (b + 1) * LANES] = done[b - own]
        if now + 2 < len(rows):
            both = [stacked_pieces(x) for x in done]
            left = jnp.concatenate([x[0] for x in both[: size // LANES - own]], axis=1)
            right = jnp.concatenate([x[1] for x in both], axis=1)
            update = dot_tn(left, right)
            for g in range(now + 2, len(rows)):
                top = g * PANEL - own * LANES
                for b in range(g * PANEL // LANES, blocks):
                    across = (b - own) * LANES
                    rows[g][b] = (
                        rows[g][b] - update[top : top + PANEL, across : across + LANES]
                    )


def triangle_ids():
    return (
        lax.broadcasted_iota(jnp.int32, (LANES, LANES), 0),
        lax.broadcasted_iota(jnp.int32, (LANES, LANES), 1),
    )


def store_blocks(tall_ref, outs):
    me = lax.rem(lax.axis_index(PLANE), len(outs))
    size = outs[0].shape[0]
    for d, out in enumerate(outs):
        out[...] = tall_ref[pl.ds(pl.multiple_of((me ^ d) * size, 8), size), :]


def load_blocks(blocks, tall_ref):
    me = lax.rem(lax.axis_index(PLANE), len(blocks))
    size = blocks[0].shape[0]
    for d, block in enumerate(blocks):
        tall_ref[pl.ds(pl.multiple_of((me ^ d) * size, 8), size), :] = block[...]


def chunk_copies(source, held, sems):
    steps, chunk = held.shape[:2]

    def copy(i):
        return pltpu.make_async_copy(
            source.at[pl.ds(i * chunk, chunk), :], held.at[i], sems.at[i]
        )

    for i in range(steps):
        copy(i).start()
    return copy


def gram_kernel(a_hbm, *refs):
    outs = refs[:SPREAD_ONE]
    a_ref, total_ref, tall_ref, sems = refs[SPREAD_ONE:]
    copy = chunk_copies(a_hbm, a_ref, sems)
    for i in range(a_ref.shape[0]):
        copy(i).wait()
        hi, lo = split(a_ref[i])
        part = dot_tn(hi, jnp.concatenate([hi, lo], axis=1))
        total_ref[...] = part if i == 0 else total_ref[...] + part
    width = a_ref.shape[2]
    cross = total_ref[:, width : width + RK]
    first = total_ref[:RK, :RK] + total_ref[:RK, width : width + RK] + cross[:RK, :].T
    row, col = triangle_ids()
    half = RK // 2
    lower = jnp.concatenate([first[half:, half:], first[half:, :half]], axis=1)
    tall_ref[:half, :] = jnp.where((row >= col)[:half, :], lower, first[:half, :])
    tall_ref[half : half + RK, :] = (
        total_ref[:RK, RK:width] + total_ref[:RK, width + RK :] + cross[RK:, :].T
    )
    diagonal = jnp.sum(jnp.where(row == col, first, 0.0), axis=0, keepdims=True)
    tail = tall_ref.shape[0] - half - RK
    tall_ref[half + RK :, :] = jnp.broadcast_to(diagonal, (tail, LANES))
    store_blocks(tall_ref, outs)


def relay_kernel(points, r_hbm, _, hi_ref, lo_ref, token_ref, r_ref, sems):
    token_ref[...] = jnp.zeros_like(token_ref)
    halves, steps, chunk, _ = r_ref.shape
    ranks = chunk // points

    def copy(c, i):
        return pltpu.make_async_copy(
            r_hbm.at[pl.ds(i * chunk, chunk), pl.ds(c * LANES, LANES)],
            r_ref.at[c, i],
            sems.at[c, i],
        )

    for i in range(steps):
        for c in range(halves):
            copy(c, i).start()

    def body(i, carry):
        for c in range(halves):
            copy(c, i).wait()
            for p in range(points):
                hi, lo = split(r_ref[c, i, pl.ds(p, ranks, stride=points), :])
                place = pl.ds(pl.multiple_of(i * ranks, ranks), ranks)
                hi_ref[p, place, c * LANES : (c + 1) * LANES] = hi
                lo_ref[p, place, c * LANES : (c + 1) * LANES] = lo
        return carry

    lax.fori_loop(0, steps, body, 0)


def absorb_kernel(scale, *refs):
    blocks, refs = refs[:SPREAD_ONE], refs[SPREAD_ONE:]
    hi_ref, lo_ref, absorbed_ref, linv_ref = refs[:4]
    outs = refs[4 : 4 + SPREAD_TWO]
    tall_ref, pack_ref, w_ref, total_ref = refs[4 + SPREAD_TWO :]
    row, col = triangle_ids()
    load_blocks(blocks, tall_ref)
    half = RK // 2
    top = tall_ref[:half, :]
    mixed = jnp.concatenate(
        [top, jnp.concatenate([top[:, half:], top[:, :half]], axis=1)], axis=0
    )
    sent = ((row < half) & (col > row)) | ((col >= half) & (row > col))
    diagonal = jnp.broadcast_to(tall_ref[half + RK : half + RK + 1, :], (LANES, LANES))
    w_ref[:, :LANES] = jnp.where(sent, mixed, jnp.where(row == col, diagonal, mixed.T))
    w_ref[:, LANES : 2 * LANES] = tall_ref[half : half + RK, :]
    w_ref[:, 2 * LANES :] = jnp.where(row == col, 1.0, 0.0).astype(F32)
    factor_rows(w_ref, 3)
    linv_ref[...] = w_ref[:, 2 * LANES :] * scale
    upper = jnp.concatenate(
        [jnp.where(col >= row, w_ref[:, :LANES], 0.0), w_ref[:, LANES : 2 * LANES]], axis=1
    )
    upper_hi, upper_lo = split(upper)
    upper_both = jnp.concatenate([upper_hi, upper_lo], axis=0)
    points = absorbed_ref.shape[0]
    group = 4
    for step in range(points // group):
        pieces = []
        for i in range(group):
            p = step * group + i
            first = dot_nn(upper_both, hi_ref[p])
            b = first[:RK, :] + first[RK:, :] + dot_nn(upper_hi, lo_ref[p])
            absorbed_ref[p] = b
            pieces.append(split(b))
        b_hi = jnp.concatenate([x[0] for x in pieces], axis=0)
        b_lo = jnp.concatenate([x[1] for x in pieces], axis=0)
        part = dot_tn(b_hi, jnp.concatenate([b_hi, b_lo], axis=1))
        total_ref[...] = part if step == 0 else total_ref[...] + part
    cross = total_ref[:, 256:]
    gram = total_ref[:, :256] + cross + cross.T
    lower_right = gram[LANES:, LANES:]
    pack_ref[:LANES, :] = jnp.where(col >= row, gram[:LANES, :LANES], lower_right)
    pack_ref[LANES : 2 * LANES, :] = gram[:LANES, LANES:]
    diagonal = jnp.sum(jnp.where(row == col, lower_right, 0.0), axis=0, keepdims=True)
    tail = pack_ref.shape[0] - 2 * LANES
    pack_ref[2 * LANES :, :] = jnp.broadcast_to(diagonal, (tail, LANES))
    store_blocks(pack_ref, outs)


def left_kernel(a_ref, linv_ref, _, left_ref, token_ref):
    l_hi, l_lo = split(linv_ref[...])
    hi, lo = split(a_ref[...])
    left_ref[...] = dot_nt(hi, l_hi) + dot_nt(hi, l_lo) + dot_nt(lo, l_hi)
    token_ref[...] = jnp.zeros_like(token_ref)


def right_kernel(points, absorbed_ref, _, right_ref, token_ref):
    count = absorbed_ref.shape[1]
    for p in range(points):
        right_ref[pl.ds(p, count, stride=points), :] = absorbed_ref[p]
    token_ref[...] = jnp.zeros_like(token_ref)


def factor_kernel(scale, *refs):
    blocks, (out_ref, pack_ref, w_ref) = refs[:SPREAD_TWO], refs[SPREAD_TWO:]
    load_blocks(blocks, pack_ref)
    row, col = triangle_ids()
    packed = pack_ref[:LANES, :] * scale
    turned = packed.T
    diagonal = jnp.broadcast_to(pack_ref[2 * LANES : 2 * LANES + 1, :], (LANES, LANES)) * scale
    w_ref[:LANES, :LANES] = jnp.where(col >= row, packed, turned)
    w_ref[:LANES, LANES:] = pack_ref[LANES : 2 * LANES, :] * scale
    w_ref[LANES:, :LANES] = jnp.zeros((LANES, LANES), F32)
    w_ref[LANES:, LANES:] = jnp.where(row > col, packed, jnp.where(row == col, diagonal, turned))
    factor_rows(w_ref, 2)
    out_ref[:LANES, :LANES] = jnp.where(col >= row, w_ref[:LANES, :LANES], 0.0)
    out_ref[:LANES, LANES:] = w_ref[:LANES, LANES:]
    out_ref[LANES:, :LANES] = jnp.zeros((LANES, LANES), F32)
    out_ref[LANES:, LANES:] = jnp.where(col >= row, w_ref[LANES:, LANES:], 0.0)


def shape(*dims, dtype=F32):
    return jax.ShapeDtypeStruct(dims, dtype)


TOKEN = shape(8, LANES)


def params(steps=0, limit=VMEM_LIMIT):
    return pltpu.CompilerParams(
        dimension_semantics=("arbitrary",) * steps or None, vmem_limit_bytes=limit
    )


def cost(mebibytes):
    return pl.CostEstimate(flops=0, bytes_accessed=mebibytes * 2**20, transcendentals=0)


def swap(value, axes, mask):
    axes = axes if isinstance(axes, tuple) else (axes,)
    size = math.prod(lax.axis_size(a) for a in axes)
    return lax.ppermute(value, axes, [(i, i ^ mask) for i in range(size)])


def four_sum(total, axes, one, two, work):
    first = swap(total, axes, one)
    second = swap(total, axes, two)
    third = swap(total, axes, one ^ two)
    result = None
    if work is not None:
        result, token = work(total)
        third = third + token[:1, :]
    return (total + first) + (second + third), result


def rest_sum(total, pairs):
    for axes, mask in pairs:
        total = total + swap(total, axes, mask)
    return total


def bits(axis, first):
    return [1 << i for i in range(first, lax.axis_size(axis).bit_length() - 1)]


def sum_over_devices(blocks, works):
    n = len(blocks)
    total = blocks[0]
    for d in range(1, n):
        total = total + swap(blocks[d], PLANE, d)
    far = [("gx", m) for m in bits("gx", 1)] + [("gz", m) for m in bits("gz", 2)]
    total, first = four_sum(total, PLANE, 2, 4, works[0])
    total, second = four_sum(total, "gz", 1, 2, works[1])
    total = rest_sum(total, far)
    return [total] + [swap(total, PLANE, d) for d in range(1, n)], (first, second)


def relay_part(rows_right, points, token):
    steps = 4
    rows, width = rows_right.shape
    chunk = rows // steps
    vmem = pl.BlockSpec(memory_space=pltpu.VMEM)
    high, low, token = pl.pallas_call(
        functools.partial(relay_kernel, points),
        in_specs=[pl.BlockSpec(memory_space=pl.ANY), vmem],
        out_specs=[vmem] * 3,
        out_shape=[shape(points, rows // points, width, dtype=BF16)] * 2 + [TOKEN],
        scratch_shapes=[
            pltpu.VMEM((width // LANES, steps, chunk, LANES), F32),
            pltpu.SemaphoreType.DMA((width // LANES, steps)),
        ],
        compiler_params=params(limit=47 * 1024 * 1024),
        cost_estimate=cost(8),
        name="relay_right",
    )(rows_right, token)
    return (high, low), token


def left_part(unfold, linv, token):
    steps = 4
    chunk = unfold.shape[0] // steps
    return pl.pallas_call(
        left_kernel,
        grid=(steps,),
        in_specs=[
            pl.BlockSpec((chunk, RK), lambda i: (i, 0)),
            pl.BlockSpec((RK, RK), lambda i: (0, 0)),
            pl.BlockSpec((8, LANES), lambda i: (0, 0)),
        ],
        out_specs=[
            pl.BlockSpec((chunk, RK), lambda i: (i, 0)),
            pl.BlockSpec((8, LANES), lambda i: (0, 0)),
        ],
        out_shape=[shape(unfold.shape[0], RK), TOKEN],
        compiler_params=params(1, 16 * 1024 * 1024),
        cost_estimate=cost(8),
        name="left_out",
    )(unfold, linv, token)


def right_part(absorbed, token):
    points, ranks, width = absorbed.shape
    steps = 2
    return pl.pallas_call(
        functools.partial(right_kernel, points),
        grid=(steps, 2),
        in_specs=[
            pl.BlockSpec((points, ranks // steps, LANES), lambda i, c: (0, i, c)),
            pl.BlockSpec((8, LANES), lambda i, c: (0, 0)),
        ],
        out_specs=[
            pl.BlockSpec((ranks // steps * points, LANES), lambda i, c: (i, c)),
            pl.BlockSpec((8, LANES), lambda i, c: (0, 0)),
        ],
        out_shape=[shape(ranks * points, width), TOKEN],
        compiler_params=params(2, 16 * 1024 * 1024),
        cost_estimate=cost(8),
        name="right_out",
    )(absorbed, token)


def per_device(left_core, right_core):
    rank_left, points, rank_mid = left_core.shape
    rank_right = right_core.shape[2]
    total_points = points * lax.axis_size("gx") * lax.axis_size("gy") * lax.axis_size("gz")
    unfold = left_core.reshape(rank_left * points, rank_mid)
    rows_right = right_core.reshape(rank_mid * points, rank_right)
    vmem = pl.BlockSpec(memory_space=pltpu.VMEM)

    steps = 16
    block_rows = (RK // 2 + RK + 16) // SPREAD_ONE
    blocks = pl.pallas_call(
        gram_kernel,
        in_specs=[pl.BlockSpec(memory_space=pl.ANY)],
        out_specs=[vmem] * SPREAD_ONE,
        out_shape=[shape(block_rows, LANES)] * SPREAD_ONE,
        scratch_shapes=[
            pltpu.VMEM((steps, unfold.shape[0] // steps, rank_mid), F32),
            pltpu.VMEM((rank_mid, 2 * rank_mid), F32),
            pltpu.VMEM((SPREAD_ONE * block_rows, LANES), F32),
            pltpu.SemaphoreType.DMA((steps,)),
        ],
        compiler_params=params(limit=53 * 1024 * 1024),
        name="gram_top",
    )(unfold)
    summed, (_, relayed) = sum_over_devices(
        blocks,
        [None, functools.partial(relay_part, rows_right, points)],
    )

    tall_rows = SPREAD_ONE * block_rows
    block_rows = LANES + 8
    packed_rows = SPREAD_TWO * block_rows
    absorbed, linv, *blocks = pl.pallas_call(
        functools.partial(absorb_kernel, math.sqrt(rank_left * total_points)),
        in_specs=[vmem] * (SPREAD_ONE + 2),
        out_specs=[vmem] * (2 + SPREAD_TWO),
        out_shape=[shape(points, RK, rank_right), shape(RK, RK)] + [shape(block_rows, LANES)] * SPREAD_TWO,
        scratch_shapes=[
            pltpu.VMEM((tall_rows, LANES), F32),
            pltpu.VMEM((packed_rows, LANES), F32),
            pltpu.VMEM((LANES, 3 * LANES), F32),
            pltpu.VMEM((rank_right, 2 * rank_right), F32),
        ],
        compiler_params=params(limit=24 * 1024 * 1024),
        name="factor_absorb",
    )(*summed, *relayed)
    summed, (right_out, left_out) = sum_over_devices(
        blocks,
        [
            functools.partial(right_part, absorbed),
            functools.partial(left_part, unfold, linv),
        ],
    )

    factor = pl.pallas_call(
        functools.partial(factor_kernel, 1.0 / (RK * total_points)),
        in_specs=[vmem] * SPREAD_TWO,
        out_specs=vmem,
        out_shape=shape(rank_right, rank_right),
        scratch_shapes=[
            pltpu.VMEM((packed_rows, LANES), F32),
            pltpu.VMEM((2 * LANES, 2 * LANES), F32),
        ],
        compiler_params=params(limit=16 * 1024 * 1024),
        name="factor_next",
    )(*summed)
    return (
        left_out.reshape(rank_left, points, RK),
        right_out.reshape(RK, points, rank_right),
        factor,
    )


def solution(mesh):
    in_specs = (P(None, AXES, None), P(None, AXES, None))
    out_specs = (P(None, AXES, None), P(None, AXES, None), P())
    return jax.shard_map(
        per_device, mesh=mesh, in_specs=in_specs, out_specs=out_specs, check_vma=False
    )
```
